32 devices in a mesh: oct: 4 (over y, x), cube: 8 (over z, core).
Axes of the slice: x: 2, y: 2, z: 4, core: 2. Of those that a mesh axis runs over, the one named last changes fastest.
Arguments:
- charges: bfloat16 [8192, 128], P(('oct', 'cube')), may hold values from -6 to 6
- panel_counts: int32 [8192], P(('oct', 'cube')), may hold values from 32 to 128
- positions: float32 [3, 8192, 128], P(None, ('oct', 'cube')), may hold values from 0 to 2
- moment_map: bfloat16 [128, 128], replicated, may hold values from -0.5 to 0.5
- translations: bfloat16 [16, 128, 128], replicated, may hold values from -0.15625 to 0.15625
- evaluation: bfloat16 [128, 128], replicated, may hold values from -0.5 to 0.5
- near_boxes: int32 [8192, 4], P(('oct', 'cube')), may hold values from 0 to 255
- group_sources: int32 [8192, 8], P(('oct', 'cube')), may hold values from 0 to 2047
- group_patterns: int32 [8192, 8], P(('oct', 'cube')), may hold values from 0 to 15
- remote_sources: int32 [4, 8, 4, 64, 4], P('oct', 'cube'), may hold values from 0 to 255
- remote_patterns: int32 [4, 8, 4, 64, 4], P('oct', 'cube'), may hold values from 0 to 15
- remote_targets: int32 [4, 8, 4, 64], P('oct', 'cube'), may hold values from 0 to 255
Outputs:
- potential: float32 [8192, 128], P(('oct', 'cube'))
The draws below stay inside these ranges and needn't reach their ends.
All inputs are finite; a program needn't handle non-finite values.
Results may differ from the reference program's by a relative error of at most 0.0024.
Values may be sent and summed in bfloat16 or wider, within the bound.
No kernel may reach another device: no remote copies, remote signals or barrier semaphores. Data moves between devices by JAX's collectives and lax.ppermute only.
A program may use at most 64 MiB of HBM per device.

```python
import math
import jax
import jax.numpy as jnp
from jax import lax

BOX_DEV = 256
NPAN = 128
COEFF = 128
NPAT = 16
KNEAR = 4
KLIST = 8
SLOTS = 64
KREMOTE = 4
NBOX = 8192
GROUP = 2048
N_OCT = 4
N_CUBE = 8


def touch_ends(array, stream_key, smallest, largest):
    shape = array.shape
    place = [jax.random.randint(jax.random.fold_in(stream_key, axis), (), 0, shape[axis]) for axis in range(len(shape))]
    array = array.at[tuple(place)].set(smallest)
    longest = shape.index(max(shape))
    place[longest] = (place[longest] + 1) % shape[longest]
    return array.at[tuple(place)].set(largest)


def block_levels(own_key, dims, pieces, low, top_value):
    loudness, own = 1.0, jax.random.fold_in(own_key, 6)
    for dim, parts in pieces:
        draws = jnp.exp(jax.random.uniform(jax.random.fold_in(own, dim), (parts,), jnp.float32, low / len(pieces), top_value / len(pieces)))
        loudness = loudness * jnp.repeat(draws, dims[dim] // parts).reshape([-1 if axis == dim else 1 for axis in range(len(dims))])
    return loudness


def centred(stream_key, extent, scale, most, pieces=(), kind=jnp.bfloat16):
    drawn = jax.random.normal(stream_key, extent, jnp.float32) * scale
    if len(pieces) > 0:
        drawn = block_levels(stream_key, extent, pieces, -0.22, 0.18) * drawn
    return jnp.clip(drawn, min=-most, max=most).astype(kind)


def setup_inputs(seed: int = 0) -> dict:
    arg_keys = jax.random.split(jax.random.key(seed), 13)
    charges = centred(arg_keys[0], (NBOX, NPAN), 1.0, 6.0, ((0, 32),))
    panel_counts = touch_ends(jax.random.randint(arg_keys[1], (NBOX,), NPAN // 4, NPAN + 1), jax.random.fold_in(arg_keys[1], 1), NPAN // 4, NPAN).astype(jnp.int32)
    positions = jnp.clip(2.0 * jax.random.uniform(arg_keys[2], (3, NBOX, NPAN), jnp.float32) ** block_levels(arg_keys[2], (3, NBOX, NPAN), ((1, 32),), -0.2, 0.2), 0.0, 2.0)
    moment_map = centred(arg_keys[3], (NPAN, COEFF), NPAN ** -0.5, 0.5)
    translations = centred(arg_keys[4], (NPAT, COEFF, COEFF), (COEFF * (KLIST + KREMOTE)) ** -0.5, 0.15625)
    evaluation = centred(arg_keys[5], (COEFF, NPAN), COEFF ** -0.5, 0.5)
    near_boxes = touch_ends(jax.random.randint(arg_keys[6], (NBOX, KNEAR), 0, BOX_DEV), jax.random.fold_in(arg_keys[6], 1), 0, BOX_DEV - 1).astype(jnp.int32)
    group_sources = touch_ends(jax.random.randint(arg_keys[7], (NBOX, KLIST), 0, GROUP), jax.random.fold_in(arg_keys[7], 1), 0, GROUP - 1).astype(jnp.int32)
    group_patterns = touch_ends(jax.random.randint(arg_keys[8], (NBOX, KLIST), 0, NPAT), jax.random.fold_in(arg_keys[8], 1), 0, NPAT - 1).astype(jnp.int32)
    remote_sources = touch_ends(jax.random.randint(arg_keys[9], (N_OCT, N_CUBE, N_OCT, SLOTS, KREMOTE), 0, BOX_DEV), jax.random.fold_in(arg_keys[9], 1), 0, BOX_DEV - 1).astype(jnp.int32)
    remote_patterns = touch_ends(jax.random.randint(arg_keys[10], (N_OCT, N_CUBE, N_OCT, SLOTS, KREMOTE), 0, NPAT), jax.random.fold_in(arg_keys[10], 1), 0, NPAT - 1).astype(jnp.int32)
    remote_targets = touch_ends(jax.random.randint(arg_keys[11], (N_OCT, N_CUBE, N_OCT, SLOTS), 0, BOX_DEV), jax.random.fold_in(arg_keys[11], 1), 0, BOX_DEV - 1).astype(jnp.int32)
    return {"charges": charges, "panel_counts": panel_counts, "positions": positions, "moment_map": moment_map, "translations": translations, "evaluation": evaluation, "near_boxes": near_boxes, "group_sources": group_sources, "group_patterns": group_patterns, "remote_sources": remote_sources, "remote_patterns": remote_patterns, "remote_targets": remote_targets}


def pattern_sums(rows, patterns):
    onehot = (patterns[..., None] == jnp.arange(NPAT, dtype=jnp.int32)).astype(jnp.float32)
    summed = jnp.einsum('nkp,nkc->npc', onehot, rows.astype(jnp.float32))
    return summed.astype(jnp.bfloat16).reshape(rows.shape[0], NPAT * COEFF)

def near_block(args):
    target_pos, source_pos, source_q = args
    diffs = target_pos[:, :, None, :, None] - source_pos[:, :, :, None, :]
    dist_sq = lax.optimization_barrier(jnp.sum(diffs * diffs, axis=0)) + 0.0025
    kernel = source_q[:, :, None, :] * lax.rsqrt(dist_sq)
    return lax.optimization_barrier(jnp.sum(kernel, axis=(1, 3)))

def reference(charges, panel_counts, positions, moment_map, translations, evaluation, near_boxes, group_sources, group_patterns, remote_sources, remote_patterns, remote_targets):
    slot_index = jnp.arange(NPAN, dtype=jnp.int32)
    live = slot_index[None, :] < panel_counts[:, None]
    strength = jnp.where(live, charges, jnp.zeros_like(charges))
    multipole = jnp.dot(strength, moment_map, preferred_element_type=jnp.float32).astype(jnp.bfloat16)
    operators = translations.reshape(NPAT * COEFF, COEFF)
    box_ids = jnp.arange(NBOX, dtype=jnp.int32)
    group_base = box_ids // GROUP * GROUP
    group_rows = multipole[(group_base[:, None] + group_sources).astype(jnp.int32)]
    group_sum = pattern_sums(group_rows, group_patterns)
    near_local = jnp.dot(group_sum, operators, preferred_element_type=jnp.float32)

    def per_sender(args):
        octant, sources, patterns = args
        cube_ids = jnp.arange(N_CUBE, dtype=jnp.int32)
        base = (octant * N_CUBE + cube_ids) * BOX_DEV
        index = (base[:, None, None, None] + sources).astype(jnp.int32)
        rows = multipole[index].reshape(-1, KREMOTE, COEFF)
        slot_sum = pattern_sums(rows, patterns.reshape(-1, KREMOTE))
        return jnp.dot(slot_sum, operators, preferred_element_type=jnp.float32)
    octants = jnp.arange(N_OCT, dtype=jnp.int32)
    slot_local = lax.map(per_sender, (octants, remote_sources, remote_patterns))
    slot_local = slot_local.reshape(-1, COEFF)
    dest = jnp.arange(N_OCT, dtype=jnp.int32)[None, None, :, None]
    cube = jnp.arange(N_CUBE, dtype=jnp.int32)[None, :, None, None]
    target = ((dest * N_CUBE + cube) * BOX_DEV + remote_targets).reshape(-1).astype(jnp.int32)
    remote_local = jnp.zeros((NBOX, COEFF), jnp.float32).at[target].add(slot_local)
    local = (near_local + remote_local).astype(jnp.bfloat16)
    far = jnp.dot(local, evaluation, preferred_element_type=jnp.float32)
    device_base = box_ids // BOX_DEV * BOX_DEV
    near_index = (device_base[:, None] + near_boxes).astype(jnp.int32)
    strength_f = strength.astype(jnp.float32)
    block = 64
    count = NBOX // block if NBOX % block == 0 else NBOX
    size = NBOX // count
    target_pos = positions.reshape(3, count, size, NPAN).transpose(1, 0, 2, 3)
    source_pos = positions[:, near_index].reshape(3, count, size, KNEAR, NPAN).transpose(1, 0, 2, 3, 4)
    source_q = strength_f[near_index].reshape(count, size, KNEAR, NPAN)
    near = lax.map(near_block, (target_pos, source_pos, source_q)).reshape(NBOX, NPAN)
    total = near * (1.0 / (4.0 * math.pi)) + far
    return jnp.where(live, total, jnp.zeros_like(total))
```

```python
import functools
import math

import jax
import jax.numpy as jnp
from jax import lax
from jax.experimental import pallas as pl
from jax.experimental.pallas import tpu as pltpu
from jax.sharding import PartitionSpec as P

F32 = jnp.float32
BF16 = jnp.bfloat16
LANES = 128
EPS = 0.0025


def iota(shape, dim):
    return lax.broadcasted_iota(jnp.int32, shape, dim)


def count_columns(cnt_ref, boxes):
    eye = iota((LANES, LANES), 0) == iota((LANES, LANES), 1)
    cols = [
        jnp.sum(jnp.where(eye, cnt_ref[i : i + 1, :], 0), axis=1, keepdims=True)
        for i in range(boxes // LANES)
    ]
    return jnp.concatenate(cols, axis=0)


def code_columns(codes):
    rows = codes.shape[0]
    padded = jnp.concatenate([codes, jnp.zeros((LANES - rows, LANES), codes.dtype)], axis=0)
    return padded.T


def onehot(local, width):
    lane = iota((LANES, LANES), 1)
    parts = [
        jnp.where(local == lane + LANES * i, 1.0, 0.0).astype(BF16) for i in range(width // LANES)
    ]
    return jnp.concatenate(parts, axis=1)


def pattern_matrix(pattern_row, targets, fanin, patterns):
    eye = iota((targets, LANES), 0) == iota((targets, LANES), 1) // fanin
    own = jnp.where(eye, jnp.broadcast_to(pattern_row, (targets, LANES)), -1)
    parts = [jnp.where(own == p, 1.0, 0.0).astype(BF16) for p in range(patterns)]
    return jnp.concatenate(parts, axis=0)


def dot(a, b):
    return jnp.dot(a, b, preferred_element_type=F32)


def slot_kernel(m_ref, code_ref, targets_ref, ops_ref, out_ref, sums):
    boxes = m_ref.shape[0]
    width = m_ref.shape[1]
    patterns = ops_ref.shape[0] // width
    groups, rows, _ = out_ref.shape
    slots = targets_ref.shape[1] // 2
    tiles = code_ref.shape[0]
    fanin = tiles * LANES // (groups * slots)
    per = LANES // fanin
    m = m_ref[...]
    for base in range(0, tiles, LANES):
        codes = code_ref[base : min(base + LANES, tiles), :]
        here = codes.shape[0]
        cols = code_columns(codes)
        for i in range(here):
            col = jnp.broadcast_to(cols[:, i : i + 1], (LANES, LANES))
            got = dot(onehot(lax.rem(col, boxes), boxes), m).astype(BF16)
            pat = pattern_matrix(codes[i : i + 1, :] // boxes, per, fanin, patterns)
            s = dot(pat, got).astype(BF16)
            for p in range(patterns):
                sums[(base + i) * per : (base + i + 1) * per, p * width : (p + 1) * width] = s[
                    p * per : (p + 1) * per
                ]
    result = dot(sums[...], ops_ref[...])
    hi = result.astype(BF16)
    lo = (result - hi.astype(F32)).astype(BF16)
    for d in range(groups):
        out_ref[d, 0:slots, :] = hi[d * slots : (d + 1) * slots]
        out_ref[d, slots : 2 * slots, :] = lo[d * slots : (d + 1) * slots]
        out_ref[d, 2 * slots : rows, :] = jnp.broadcast_to(
            targets_ref[d : d + 1, :].astype(F32), (rows - 2 * slots, 2 * slots)
        ).astype(BF16)


def near_kernel(nb_ref, cnt_ref, chg_ref, pos_ref, out_ref, feat, left, qcol):
    boxes = chg_ref.shape[0]
    knear = nb_ref.shape[0]
    live = iota((boxes, LANES), 1) < count_columns(cnt_ref, boxes)
    feat[7] = jnp.where(live, chg_ref[...].astype(F32), 0.0)
    norm = jnp.zeros((boxes, LANES), F32)
    for c in range(3):
        u = pos_ref[c] - 1.0
        h = u.astype(BF16).astype(F32)
        m = (u - h).astype(BF16).astype(F32)
        feat[2 * c] = h
        feat[2 * c + 1] = m
        v = h + m
        norm = norm + v * v
    feat[6] = norm

    masks = [
        jnp.where(iota((LANES, LANES), 1) % 8 == j, 1.0, 0.0).astype(BF16) for j in range(8)
    ]

    def build(g, carry):
        rows = pl.ds(pl.multiple_of(g * 8, 8), 8)
        parts = []
        for c in range(3):
            h = -2.0 * feat[2 * c, rows, :]
            m = -2.0 * feat[2 * c + 1, rows, :]
            parts += [h, h, m, m]
        n = feat[6, rows, :]
        n1 = n.astype(BF16).astype(F32)
        n2 = (n - n1).astype(BF16).astype(F32)
        parts += [n1, n2, n - n1 - n2, feat[7, rows, :]]
        turned = jnp.concatenate(parts, axis=0).T
        packed = turned.astype(BF16)
        for j in range(8):
            left[g * 8 + j] = packed * masks[j]
            qcol[g * 8 + j] = jnp.broadcast_to(
                turned[:, 120 + j : 121 + j], (LANES, LANES)
            )
        return carry

    lax.fori_loop(0, boxes // 8, build, 0)

    zero = jnp.zeros((LANES, LANES), BF16)
    one8 = jnp.ones((24, LANES), F32)
    zero8 = jnp.zeros((8, LANES), F32)

    def weights(tile, r):
        parts = []
        for c in range(3):
            h = jnp.broadcast_to(tile[2 * c][r : r + 1], (8, LANES))
            m = jnp.broadcast_to(tile[2 * c + 1][r : r + 1], (8, LANES))
            parts += [h, m, h, m]
        return jnp.concatenate(parts + [one8, zero8], axis=0).astype(BF16)

    def group(g, carry):
        rows = pl.ds(pl.multiple_of(g * 8, 8), 8)
        tile = [feat[f, rows, :] for f in range(7)]
        shift = tile[6] + EPS
        outs = []
        for pair in range(4):
            pick = [2 * pair, 2 * pair + 1]
            w1, w2 = [weights(tile, r) for r in pick]
            right = jnp.concatenate(
                [jnp.concatenate([w1, zero], axis=1), jnp.concatenate([zero, w2], axis=1)], axis=0
            )
            near = [[nb_ref[k, g * 8 + r] for k in range(knear)] for r in pick]
            lhs = jnp.concatenate(
                [
                    jnp.concatenate([left[near[0][k]], left[near[1][k]]], axis=1)
                    for k in range(knear)
                ],
                axis=0,
            )
            dist = dot(lhs, right)
            for side in range(2):
                row = shift[pick[side] : pick[side] + 1]
                inv = lax.rsqrt(dist[:, side * LANES : (side + 1) * LANES] + row)
                acc = inv[0:LANES] * qcol[near[side][0]]
                for k in range(1, knear):
                    acc = acc + inv[k * LANES : (k + 1) * LANES] * qcol[near[side][k]]
                outs.append(jnp.sum(acc, axis=0, keepdims=True))
        out_ref[rows, :] = jnp.concatenate(outs, axis=0)
        return carry

    lax.fori_loop(0, boxes // 8, group, 0)


def far_kernel(*refs, blocks, groups, fanin):
    code_ref, cnt_ref, near_ref, ops_ref, eval_ref = refs[:5]
    m_refs = refs[5 : 5 + blocks]
    pay_refs = refs[5 + blocks : 5 + blocks + groups]
    out_ref, sums = refs[5 + blocks + groups :]
    boxes, width = m_refs[0].shape
    patterns = ops_ref.shape[0] // width
    per = LANES // fanin
    tiles = code_ref.shape[0]
    span = 2 * boxes
    pages = blocks // 2
    table = jnp.concatenate(
        [
            jnp.concatenate([m_refs[2 * j][...], m_refs[2 * j + 1][...]], axis=0)
            for j in range(pages)
        ],
        axis=1,
    )
    codes = code_ref[...]
    cols = code_columns(codes)
    for i in range(tiles):
        col = jnp.broadcast_to(cols[:, i : i + 1], (LANES, LANES))
        wide = dot(onehot(col & (span - 1), span), table)
        page = (col // span) & (pages - 1)
        got = wide[:, 0:width]
        for j in range(1, pages):
            got = jnp.where(page == j, wide[:, j * width : (j + 1) * width], got)
        pat = pattern_matrix(codes[i : i + 1, :] // (blocks * boxes), per, fanin, patterns)
        s = dot(pat, got.astype(BF16)).astype(BF16)
        for p in range(patterns):
            sums[i * per : (i + 1) * per, p * width : (p + 1) * width] = s[
                p * per : (p + 1) * per
            ]
    local = dot(sums[...], ops_ref[...])
    hits = []
    values = []
    for pay in pay_refs:
        depth = pay.shape[0] - 16
        target = pay[depth : depth + 16, :].astype(F32)[0:1]
        box = iota((boxes, depth), 0).astype(F32)
        hits.append(jnp.where(box == target, 1.0, 0.0).astype(BF16))
        values.append(pay[0:depth, :])
    local = local + dot(jnp.concatenate(hits, axis=1), jnp.concatenate(values, axis=0))
    far = dot(local.astype(BF16), eval_ref[...])
    total = near_ref[...] * (1.0 / (4.0 * math.pi)) + far
    live = iota((boxes, LANES), 1) < count_columns(cnt_ref, boxes)
    out_ref[...] = jnp.where(live, total, 0.0)


VMEM = pl.BlockSpec(memory_space=pltpu.VMEM)
SMEM = pl.BlockSpec(memory_space=pltpu.SMEM)
MIB = 1024 * 1024


def body(
    n_oct,
    n_cube,
    charges,
    panel_counts,
    positions,
    moment_map,
    translations,
    evaluation,
    near_boxes,
    group_sources,
    group_patterns,
    remote_sources,
    remote_patterns,
    remote_targets,
):
    boxes, panels = charges.shape
    width = moment_map.shape[1]
    patterns = translations.shape[0]
    operators = translations.reshape(patterns * width, width)
    counts = panel_counts.reshape(boxes // LANES, LANES)
    slot_index = jnp.arange(panels, dtype=jnp.int32)
    live = slot_index[None, :] < panel_counts[:, None]
    strength = jnp.where(live, charges, jnp.zeros_like(charges))
    multipole = jnp.dot(strength, moment_map, preferred_element_type=F32).astype(BF16)

    me = lax.axis_index("cube")
    blocks = [multipole] + [
        lax.ppermute(multipole, "cube", [(i, i ^ k) for i in range(n_cube)])
        for k in range(1, n_cube)
    ]

    slots, fanin = remote_sources.shape[3:]
    slot_code = (remote_sources[0, 0] + boxes * remote_patterns[0, 0]).reshape(-1, LANES)
    targets = jnp.concatenate([remote_targets[0, 0]] * 2, axis=1)
    sent = pl.pallas_call(
        slot_kernel,
        out_shape=jax.ShapeDtypeStruct((n_oct, 2 * slots + 16, width), BF16),
        in_specs=[VMEM] * 4,
        out_specs=VMEM,
        scratch_shapes=[pltpu.VMEM((n_oct * slots, patterns * width), BF16)],
        compiler_params=pltpu.CompilerParams(vmem_limit_bytes=16 * MIB),
        cost_estimate=pl.CostEstimate(
            flops=1_000_000_000, bytes_accessed=1_000_000, transcendentals=0
        ),
        name="slots",
    )(multipole, slot_code, targets, operators)
    mine = lax.axis_index("oct")
    payloads = []
    for k in range(n_oct):
        part = lax.dynamic_index_in_dim(sent, mine ^ k, 0, keepdims=False)
        if k > 0:
            part = lax.ppermute(part, "oct", [(i, i ^ k) for i in range(n_oct)])
        payloads.append(part)

    near = pl.pallas_call(
        near_kernel,
        out_shape=jax.ShapeDtypeStruct((boxes, panels), F32),
        in_specs=[SMEM, VMEM, VMEM, VMEM],
        out_specs=VMEM,
        scratch_shapes=[
            pltpu.VMEM((8, boxes, panels), F32),
            pltpu.VMEM((boxes, panels, LANES), BF16),
            pltpu.VMEM((boxes, panels, LANES), F32),
        ],
        compiler_params=pltpu.CompilerParams(vmem_limit_bytes=48 * MIB),
        cost_estimate=pl.CostEstimate(
            flops=15_000_000_000, bytes_accessed=1_000_000, transcendentals=16_000_000
        ),
        name="near",
    )(near_boxes.T, counts, charges, positions)

    klist = group_sources.shape[1]
    group = n_cube * boxes
    code = (group_sources ^ (me * boxes)) + group * group_patterns
    return pl.pallas_call(
        functools.partial(far_kernel, blocks=n_cube, groups=n_oct, fanin=klist),
        out_shape=jax.ShapeDtypeStruct((boxes, panels), F32),
        in_specs=[VMEM] * (5 + n_cube + n_oct),
        out_specs=VMEM,
        scratch_shapes=[pltpu.VMEM((boxes, patterns * width), BF16)],
        compiler_params=pltpu.CompilerParams(vmem_limit_bytes=24 * MIB),
        cost_estimate=pl.CostEstimate(
            flops=3_000_000_000, bytes_accessed=2_000_000, transcendentals=0
        ),
        name="far",
    )(code.reshape(-1, LANES), counts, near, operators, evaluation, *blocks, *payloads)


def solution(mesh):
    n_oct = mesh.shape["oct"]
    n_cube = mesh.shape["cube"]

    def run(*arrays):
        return body(n_oct, n_cube, *arrays)

    return jax.shard_map(
        run,
        mesh=mesh,
        in_specs=(
            P(("oct", "cube"), None),
            P(("oct", "cube")),
            P(None, ("oct", "cube"), None),
            P(),
            P(),
            P(),
            P(("oct", "cube"), None),
            P(("oct", "cube"), None),
            P(("oct", "cube"), None),
            P("oct", "cube", None, None, None),
            P("oct", "cube", None, None, None),
            P("oct", "cube", None, None),
        ),
        out_specs=P(("oct", "cube"), None),
        check_vma=False,
    )
```

```python
import functools
import math

import jax
import jax.numpy as jnp
from jax import lax
from jax.experimental import pallas as pl
from jax.experimental.pallas import tpu as pltpu
from jax.sharding import PartitionSpec as P

F32 = jnp.float32
BF16 = jnp.bfloat16
LANES = 128
EPS = 0.0025


def iota(shape, dim):
    return lax.broadcasted_iota(jnp.int32, shape, dim)


def count_columns(cnt_ref, boxes):
    eye = iota((LANES, LANES), 0) == iota((LANES, LANES), 1)
    cols = [
        jnp.sum(jnp.where(eye, cnt_ref[i : i + 1, :], 0), axis=1, keepdims=True)
        for i in range(boxes // LANES)
    ]
    return jnp.concatenate(cols, axis=0)


def log2(value):
    return value.bit_length() - 1


def code_columns(codes):
    rows = codes.shape[0]
    padded = jnp.concatenate([codes, jnp.zeros((LANES - rows, LANES), codes.dtype)], axis=0)
    return padded.T


def onehot(local, width):
    lane = iota((LANES, LANES), 1)
    parts = [
        jnp.where(local == lane + LANES * i, 1.0, 0.0).astype(BF16) for i in range(width // LANES)
    ]
    return jnp.concatenate(parts, axis=1)


def pattern_matrix(pattern_row, eye, patterns):
    own = jnp.where(eye, jnp.broadcast_to(pattern_row, eye.shape), -1)
    parts = [jnp.where(own == p, 1.0, 0.0).astype(BF16) for p in range(patterns)]
    return jnp.concatenate(parts, axis=0)


def dot(a, b):
    return jnp.dot(a, b, preferred_element_type=F32)


def slot_kernel(m_ref, src_ref, pat_ref, tgt_ref, ops_ref, out_ref, sums):
    boxes, width = m_ref.shape
    patterns = ops_ref.shape[0] // width
    groups, fanin, slots = src_ref.shape
    rows = out_ref.shape[1]
    pack = LANES // slots
    tiles = fanin // pack
    m = m_ref[...]

    def packed(ref, d, h):
        return jnp.concatenate([ref[d, h * pack + i : h * pack + i + 1, :] for i in range(pack)], axis=1)

    sources = [packed(src_ref, d, h) for d in range(groups) for h in range(tiles)]
    cols = code_columns(jnp.concatenate(sources, axis=0))
    eye = iota((slots, LANES), 0) == (iota((slots, LANES), 1) & (slots - 1))
    for d in range(groups):
        ones = []
        pats = []
        for h in range(tiles):
            i = d * tiles + h
            ones.append(onehot(jnp.broadcast_to(cols[:, i : i + 1], (LANES, LANES)), boxes))
            pats.append(pattern_matrix(packed(pat_ref, d, h), eye, patterns))
        got = dot(jnp.concatenate(ones, axis=0), m).astype(BF16)
        s = dot(jnp.concatenate(pats, axis=1), got).astype(BF16)
        for p in range(patterns):
            sums[d * slots : (d + 1) * slots, p * width : (p + 1) * width] = s[
                p * slots : (p + 1) * slots
            ]
    result = dot(sums[...], ops_ref[...])
    hi = result.astype(BF16)
    lo = (result - hi.astype(F32)).astype(BF16)
    for d in range(groups):
        target = tgt_ref[d : d + 1, :].astype(F32)
        out_ref[d, 0:slots, :] = hi[d * slots : (d + 1) * slots]
        out_ref[d, slots : 2 * slots, :] = lo[d * slots : (d + 1) * slots]
        out_ref[d, 2 * slots : rows, :] = jnp.broadcast_to(
            jnp.concatenate([target, target], axis=1), (rows - 2 * slots, 2 * slots)
        ).astype(BF16)


def near_kernel(nb_ref, cnt_ref, chg_ref, pos_ref, out_ref, feat, right, left):
    boxes = chg_ref.shape[0]
    knear = nb_ref.shape[0]
    live = iota((boxes, LANES), 1) < count_columns(cnt_ref, boxes)
    feat[7] = jnp.where(live, chg_ref[...].astype(F32), 0.0)
    norm = jnp.zeros((boxes, LANES), F32)
    for c in range(3):
        u = pos_ref[c] - 1.0
        h = u.astype(BF16).astype(F32)
        m = (u - h).astype(BF16).astype(F32)
        feat[2 * c] = h
        feat[2 * c + 1] = m
        v = h + m
        norm = norm + v * v
    feat[6] = norm

    def build(g, carry):
        rows = pl.ds(pl.multiple_of(g * 8, 8), 8)
        tile = [feat[f, rows, :] for f in range(7)]
        parts = []
        for c in range(3):
            h = -2.0 * tile[2 * c]
            m = -2.0 * tile[2 * c + 1]
            parts += [h, h, m, m]
        n = tile[6] + EPS
        n1 = n.astype(BF16).astype(F32)
        n2 = (n - n1).astype(BF16).astype(F32)
        parts += [n1, n2, n - n1 - n2, jnp.zeros((8, LANES), F32)]
        left[g] = jnp.concatenate(parts, axis=0).T.astype(BF16)
        for r in range(8):
            for c in range(3):
                h = jnp.broadcast_to(tile[2 * c][r : r + 1], (8, LANES))
                m = jnp.broadcast_to(tile[2 * c + 1][r : r + 1], (8, LANES))
                right[g * 8 + r, 16 * c : 16 * c + 16, :] = jnp.concatenate(
                    [h, m], axis=0
                ).astype(BF16)
        return carry

    lax.fori_loop(0, boxes // 8, build, 0)

    masks = [
        jnp.where((iota((LANES, LANES), 1) & 7) == j, 1.0, 0.0).astype(BF16) for j in range(8)
    ]
    eye = iota((LANES, LANES), 0) == iota((LANES, LANES), 1)
    ones = jnp.where(iota((32, LANES), 0) < 24, 1.0, 0.0).astype(BF16)

    def operand(box):
        x, y, z = [right[box, 16 * c : 16 * c + 16, :] for c in range(3)]
        return jnp.concatenate([x, x, y, y, z, z, ones], axis=0)

    def group(g, carry):
        turned = left[g]
        outs = []
        for r in range(8):
            lhs = turned * masks[r]
            acc = None
            for k in range(0, knear, 2):
                pair = [nb_ref[k + i, g * 8 + r] for i in range(2)]
                dist = dot(lhs, jnp.concatenate([operand(b) for b in pair], axis=1))
                for i in range(2):
                    shift = feat[6, pl.ds(pair[i], 1), :]
                    q = feat[7, pl.ds(pair[i], 1), :]
                    term = lax.rsqrt(dist[:, i * LANES : (i + 1) * LANES] + shift) * q
                    acc = term if acc is None else acc + term
            total = jnp.sum(acc, axis=1, keepdims=True)
            outs.append(jnp.sum(jnp.where(eye, total, 0.0), axis=0, keepdims=True))
        out_ref[pl.ds(pl.multiple_of(g * 8, 8), 8), :] = jnp.concatenate(outs, axis=0)
        return carry

    lax.fori_loop(0, boxes // 8, group, 0, unroll=2)


def group_kernel(*refs, blocks, fanin):
    code_ref, ops_ref, mine_ref, other_ref, out_ref, sums = refs
    width = mine_ref.shape[1]
    boxes = mine_ref.shape[0] // (blocks // 2)
    patterns = ops_ref.shape[0] // width
    per = LANES // fanin
    tiles = code_ref.shape[0]
    span = 2 * boxes
    pages = blocks // 2
    table = jnp.concatenate(
        [
            jnp.concatenate(
                [mine_ref[j * boxes : (j + 1) * boxes], other_ref[j * boxes : (j + 1) * boxes]], axis=0
            )
            for j in range(pages)
        ],
        axis=1,
    )
    codes = code_ref[...]
    cols = code_columns(codes)
    eye = iota((per, LANES), 0) == (iota((per, LANES), 1) >> log2(fanin))
    batch = 4
    for base in range(0, tiles, batch):
        picks = [
            jnp.broadcast_to(cols[:, i : i + 1], (LANES, LANES)) for i in range(base, base + batch)
        ]
        wide = dot(jnp.concatenate([onehot(c & (span - 1), span) for c in picks], axis=0), table)
        for n in range(batch):
            i = base + n
            page = (picks[n] >> log2(span)) & (pages - 1)
            part = wide[n * LANES : (n + 1) * LANES]
            got = part[:, 0:width]
            for j in range(1, pages):
                got = jnp.where(page == j, part[:, j * width : (j + 1) * width], got)
            pat = pattern_matrix(codes[i : i + 1, :] >> log2(blocks * boxes), eye, patterns)
            s = dot(pat, got.astype(BF16)).astype(BF16)
            for p in range(patterns):
                sums[i * per : (i + 1) * per, p * width : (p + 1) * width] = s[
                    p * per : (p + 1) * per
                ]
    out_ref[...] = dot(sums[...], ops_ref[...])


def final_kernel(*refs):
    cnt_ref, near_ref, local_ref, eval_ref = refs[:4]
    pay_refs = refs[4:-1]
    out_ref = refs[-1]
    boxes = local_ref.shape[0]
    hits = []
    values = []
    for pay in pay_refs:
        depth = pay.shape[0] - 16
        target = pay[depth : depth + 16, :].astype(F32)[0:1]
        box = iota((boxes, depth), 0).astype(F32)
        hits.append(jnp.where(box == target, 1.0, 0.0).astype(BF16))
        values.append(pay[0:depth, :])
    local = local_ref[...] + dot(jnp.concatenate(hits, axis=1), jnp.concatenate(values, axis=0))
    far = dot(local.astype(BF16), eval_ref[...])
    total = near_ref[...] * (1.0 / (4.0 * math.pi)) + far
    live = iota((boxes, LANES), 1) < count_columns(cnt_ref, boxes)
    out_ref[...] = jnp.where(live, total, 0.0)


VMEM = pl.BlockSpec(memory_space=pltpu.VMEM)
SMEM = pl.BlockSpec(memory_space=pltpu.SMEM)
MIB = 1024 * 1024


def body(
    n_oct,
    n_cube,
    charges,
    panel_counts,
    positions,
    moment_map,
    translations,
    evaluation,
    near_boxes,
    group_sources,
    group_patterns,
    remote_sources,
    remote_patterns,
    remote_targets,
):
    boxes, panels = charges.shape
    width = moment_map.shape[1]
    patterns = translations.shape[0]
    operators = translations.reshape(patterns * width, width)
    counts = panel_counts.reshape(boxes // LANES, LANES)
    slot_index = jnp.arange(panels, dtype=jnp.int32)
    live = slot_index[None, :] < panel_counts[:, None]
    strength = jnp.where(live, charges, jnp.zeros_like(charges))
    multipole = jnp.dot(strength, moment_map, preferred_element_type=F32).astype(BF16)

    me = lax.axis_index("cube")
    along = [multipole] + [
        lax.ppermute(multipole, "cube", [(i, i ^ k) for i in range(n_cube)])
        for k in range(2, n_cube, 2)
    ]

    near = pl.pallas_call(
        near_kernel,
        out_shape=jax.ShapeDtypeStruct((boxes, panels), F32),
        in_specs=[SMEM, VMEM, VMEM, VMEM],
        out_specs=VMEM,
        scratch_shapes=[
            pltpu.VMEM((8, boxes, panels), F32),
            pltpu.VMEM((boxes, 48, panels), BF16),
            pltpu.VMEM((boxes // 8, panels, LANES), BF16),
        ],
        compiler_params=pltpu.CompilerParams(vmem_limit_bytes=24 * MIB),
        cost_estimate=pl.CostEstimate(
            flops=15_000_000_000, bytes_accessed=1_000_000, transcendentals=16_000_000
        ),
        name="near",
    )(near_boxes.T, counts, charges, positions)

    near, base, *along = lax.optimization_barrier((near, multipole, *along))
    mine = jnp.concatenate(along, axis=0)
    other = lax.ppermute(mine, "cube", [(i, i ^ 1) for i in range(n_cube)])

    slots, fanin = remote_sources.shape[3:]
    sent = pl.pallas_call(
        slot_kernel,
        out_shape=jax.ShapeDtypeStruct((n_oct, 2 * slots + 16, width), BF16),
        in_specs=[VMEM] * 5,
        out_specs=VMEM,
        scratch_shapes=[pltpu.VMEM((n_oct * slots, patterns * width), BF16)],
        compiler_params=pltpu.CompilerParams(vmem_limit_bytes=16 * MIB),
        cost_estimate=pl.CostEstimate(
            flops=1_000_000_000, bytes_accessed=1_000_000, transcendentals=0
        ),
        name="slots",
    )(
        base,
        remote_sources[0, 0].transpose(0, 2, 1),
        remote_patterns[0, 0].transpose(0, 2, 1),
        remote_targets[0, 0],
        operators,
    )
    octant = lax.axis_index("oct")
    payloads = []
    for k in range(n_oct):
        part = lax.dynamic_index_in_dim(sent, octant ^ k, 0, keepdims=False)
        if k > 0:
            part = lax.ppermute(part, "oct", [(i, i ^ k) for i in range(n_oct)])
        payloads.append(part)

    klist = group_sources.shape[1]
    group = n_cube * boxes
    code = (group_sources ^ (me * boxes)) + group * group_patterns
    near_local = pl.pallas_call(
        functools.partial(group_kernel, blocks=n_cube, fanin=klist),
        out_shape=jax.ShapeDtypeStruct((boxes, width), F32),
        in_specs=[VMEM] * 4,
        out_specs=VMEM,
        scratch_shapes=[pltpu.VMEM((boxes, patterns * width), BF16)],
        compiler_params=pltpu.CompilerParams(vmem_limit_bytes=24 * MIB),
        cost_estimate=pl.CostEstimate(
            flops=3_000_000_000, bytes_accessed=2_000_000, transcendentals=0
        ),
        name="group",
    )(code.reshape(-1, LANES), operators, mine, other)

    return pl.pallas_call(
        final_kernel,
        out_shape=jax.ShapeDtypeStruct((boxes, panels), F32),
        in_specs=[VMEM] * (4 + n_oct),
        out_specs=VMEM,
        compiler_params=pltpu.CompilerParams(vmem_limit_bytes=16 * MIB),
        cost_estimate=pl.CostEstimate(
            flops=200_000_000, bytes_accessed=600_000, transcendentals=0
        ),
        name="final",
    )(counts, near, near_local, evaluation, *payloads)


def solution(mesh):
    n_oct = mesh.shape["oct"]
    n_cube = mesh.shape["cube"]

    def run(*arrays):
        return body(n_oct, n_cube, *arrays)

    return jax.shard_map(
        run,
        mesh=mesh,
        in_specs=(
            P(("oct", "cube"), None),
            P(("oct", "cube")),
            P(None, ("oct", "cube"), None),
            P(),
            P(),
            P(),
            P(("oct", "cube"), None),
            P(("oct", "cube"), None),
            P(("oct", "cube"), None),
            P("oct", "cube", None, None, None),
            P("oct", "cube", None, None, None),
            P("oct", "cube", None, None),
        ),
        out_specs=P(("oct", "cube"), None),
        check_vma=False,
    )
```

```python
import functools
import math

import jax
import jax.numpy as jnp
from jax import lax
from jax.experimental import pallas as pl
from jax.experimental.pallas import tpu as pltpu
from jax.sharding import PartitionSpec as P

F32 = jnp.float32
BF16 = jnp.bfloat16
LANES = 128
EPS = 0.0025


def iota(shape, dim):
    return lax.broadcasted_iota(jnp.int32, shape, dim)


def count_columns(cnt_ref, boxes):
    eye = iota((LANES, LANES), 0) == iota((LANES, LANES), 1)
    cols = [
        jnp.sum(jnp.where(eye, cnt_ref[i : i + 1, :], 0), axis=1, keepdims=True)
        for i in range(boxes // LANES)
    ]
    return jnp.concatenate(cols, axis=0)


def log2(value):
    return value.bit_length() - 1


def code_columns(codes):
    rows = codes.shape[0]
    padded = jnp.concatenate([codes, jnp.zeros((LANES - rows, LANES), codes.dtype)], axis=0)
    return padded.T


def onehot(local, width):
    lane = iota((LANES, LANES), 1)
    parts = [
        jnp.where(local == lane + LANES * i, 1.0, 0.0).astype(BF16) for i in range(width // LANES)
    ]
    return jnp.concatenate(parts, axis=1)


def pattern_matrix(pattern_row, eye, patterns):
    own = jnp.where(eye, jnp.broadcast_to(pattern_row, eye.shape), -1)
    parts = [jnp.where(own == p, 1.0, 0.0).astype(BF16) for p in range(patterns)]
    return jnp.concatenate(parts, axis=0)


def dot(a, b):
    return jnp.dot(a, b, preferred_element_type=F32)


def slot_kernel(m_ref, src_ref, pat_ref, tgt_ref, ops_ref, out_ref, sums):
    boxes, width = m_ref.shape
    patterns = ops_ref.shape[0] // width
    groups, fanin, slots = src_ref.shape
    rows = out_ref.shape[1]
    pack = LANES // slots
    tiles = fanin // pack
    m = m_ref[...]

    def packed(ref, d, h):
        return jnp.concatenate([ref[d, h * pack + i : h * pack + i + 1, :] for i in range(pack)], axis=1)

    sources = [packed(src_ref, d, h) for d in range(groups) for h in range(tiles)]
    cols = code_columns(jnp.concatenate(sources, axis=0))
    eye = iota((slots, LANES), 0) == (iota((slots, LANES), 1) & (slots - 1))
    for d in range(groups):
        ones = []
        pats = []
        for h in range(tiles):
            i = d * tiles + h
            ones.append(onehot(jnp.broadcast_to(cols[:, i : i + 1], (LANES, LANES)), boxes))
            pats.append(pattern_matrix(packed(pat_ref, d, h), eye, patterns))
        got = dot(jnp.concatenate(ones, axis=0), m).astype(BF16)
        s = dot(jnp.concatenate(pats, axis=1), got).astype(BF16)
        for p in range(patterns):
            sums[d * slots : (d + 1) * slots, p * width : (p + 1) * width] = s[
                p * slots : (p + 1) * slots
            ]
    result = dot(sums[...], ops_ref[...])
    hi = result.astype(BF16)
    lo = (result - hi.astype(F32)).astype(BF16)
    for d in range(groups):
        target = tgt_ref[d : d + 1, :].astype(F32)
        out_ref[d, 0:slots, :] = hi[d * slots : (d + 1) * slots]
        out_ref[d, slots : 2 * slots, :] = lo[d * slots : (d + 1) * slots]
        out_ref[d, 2 * slots : rows, :] = jnp.broadcast_to(
            jnp.concatenate([target, target], axis=1), (rows - 2 * slots, 2 * slots)
        ).astype(BF16)


def near_kernel(nb_ref, cnt_ref, chg_ref, pos_ref, out_ref, feat, right, left):
    boxes = chg_ref.shape[0]
    knear = nb_ref.shape[0]
    live = iota((boxes, LANES), 1) < count_columns(cnt_ref, boxes)
    feat[7] = jnp.where(live, chg_ref[...].astype(F32), 0.0)
    norm = jnp.zeros((boxes, LANES), F32)
    for c in range(3):
        u = pos_ref[c] - 1.0
        h = u.astype(BF16).astype(F32)
        m = (u - h).astype(BF16).astype(F32)
        feat[2 * c] = h
        feat[2 * c + 1] = m
        v = h + m
        norm = norm + v * v
    feat[6] = norm

    def split(n):
        n1 = n.astype(BF16).astype(F32)
        n2 = (n - n1).astype(BF16).astype(F32)
        return n1, n2, n - n1 - n2

    zero8 = jnp.zeros((8, LANES), F32)

    def build(g, carry):
        rows = pl.ds(pl.multiple_of(g * 8, 8), 8)
        tile = [feat[f, rows, :] for f in range(7)]
        parts = []
        for c in range(3):
            h = -2.0 * tile[2 * c]
            m = -2.0 * tile[2 * c + 1]
            parts += [h, h, m, m]
        parts += [*split(tile[6] + EPS), zero8]
        left[g] = jnp.concatenate(parts, axis=0).T.astype(BF16)
        columns = tile[:6] + list(split(tile[6]))
        for r in range(8):
            wide = [jnp.broadcast_to(v[r : r + 1], (8, LANES)) for v in columns] + [zero8]
            for i in range(5):
                right[g * 8 + r, 16 * i : 16 * i + 16, :] = jnp.concatenate(
                    wide[2 * i : 2 * i + 2], axis=0
                ).astype(BF16)
        return carry

    lax.fori_loop(0, boxes // 8, build, 0)

    lane = iota((LANES, LANES), 1)
    own = [jnp.where((lane & 7) == j, 1.0, 0.0).astype(BF16) for j in range(8)]
    unit = [jnp.where(((lane & 7) == j) & (lane < 24), 1.0, 0.0).astype(BF16) for j in range(8)]
    eye = iota((LANES, LANES), 0) == lane
    ones = jnp.where(iota((32, LANES), 0) < 24, 1.0, 0.0).astype(BF16)
    none = jnp.zeros((96, LANES), BF16)

    def operand(box):
        x, y, z, n, t = [right[box, 16 * c : 16 * c + 16, :] for c in range(5)]
        return jnp.concatenate([x, x, y, y, z, z, ones, n, t, none], axis=0)

    assert knear == 4
    last = boxes // 8 - 1

    def issue(accs, g, r, slot):
        box = g * 8 + r
        lhs = jnp.concatenate([left[g] * own[r], unit[r]], axis=1)
        for side in range(2):
            pair = [operand(nb_ref[2 * side + i, box]) for i in range(2)]
            pltpu.matmul_push_rhs(jnp.concatenate(pair, axis=1), slot, side)
            pltpu.matmul_acc_lhs(accs[2 * side + slot], lhs, load_staged_rhs=slot)

    def collect(accs, g, r, slot):
        box = g * 8 + r
        acc = None
        for side in range(2):
            dist = pltpu.matmul_pop(accs[2 * side + slot])
            for i in range(2):
                q = feat[7, pl.ds(nb_ref[2 * side + i, box], 1), :]
                term = lax.rsqrt(dist[:, i * LANES : (i + 1) * LANES]) * q
                acc = term if acc is None else acc + term
        total = jnp.sum(acc, axis=1, keepdims=True)
        return jnp.sum(jnp.where(eye, total, 0.0), axis=0, keepdims=True)

    def run(*accs):
        issue(accs, 0, 0, 0)

        def group(g, carry):
            outs = []
            for r in range(8):
                if r < 7:
                    issue(accs, g, r + 1, (r + 1) % 2)
                else:
                    issue(accs, jnp.minimum(g + 1, last), 0, 0)
                outs.append(collect(accs, g, r, r % 2))
            out_ref[pl.ds(pl.multiple_of(g * 8, 8), 8), :] = jnp.concatenate(outs, axis=0)
            return carry

        lax.fori_loop(0, boxes // 8, group, 0)
        for side in range(2):
            pltpu.matmul_pop(accs[2 * side])

    pl.run_scoped(run, *[pltpu.ACC(i // 2)((LANES, 2 * LANES), F32) for i in range(4)])


def group_kernel(*refs, blocks, fanin):
    code_ref, ops_ref, mine_ref, other_ref, out_ref, sums = refs
    width = mine_ref.shape[1]
    boxes = mine_ref.shape[0] // (blocks // 2)
    patterns = ops_ref.shape[0] // width
    per = LANES // fanin
    tiles = code_ref.shape[0]
    span = 2 * boxes
    pages = blocks // 2
    table = jnp.concatenate(
        [
            jnp.concatenate(
                [mine_ref[j * boxes : (j + 1) * boxes], other_ref[j * boxes : (j + 1) * boxes]], axis=0
            )
            for j in range(pages)
        ],
        axis=1,
    )
    codes = code_ref[...]
    cols = code_columns(codes)
    eye = iota((per, LANES), 0) == (iota((per, LANES), 1) >> log2(fanin))
    batch = 4
    for base in range(0, tiles, batch):
        picks = [
            jnp.broadcast_to(cols[:, i : i + 1], (LANES, LANES)) for i in range(base, base + batch)
        ]
        wide = dot(jnp.concatenate([onehot(c & (span - 1), span) for c in picks], axis=0), table)
        for n in range(batch):
            i = base + n
            page = (picks[n] >> log2(span)) & (pages - 1)
            part = wide[n * LANES : (n + 1) * LANES]
            got = part[:, 0:width]
            for j in range(1, pages):
                got = jnp.where(page == j, part[:, j * width : (j + 1) * width], got)
            pat = pattern_matrix(codes[i : i + 1, :] >> log2(blocks * boxes), eye, patterns)
            s = dot(pat, got.astype(BF16)).astype(BF16)
            for p in range(patterns):
                sums[i * per : (i + 1) * per, p * width : (p + 1) * width] = s[
                    p * per : (p + 1) * per
                ]
    out_ref[...] = dot(sums[...], ops_ref[...])


def final_kernel(*refs):
    cnt_ref, near_ref, local_ref, eval_ref = refs[:4]
    pay_refs = refs[4:-1]
    out_ref = refs[-1]
    boxes = local_ref.shape[0]
    hits = []
    values = []
    for pay in pay_refs:
        depth = pay.shape[0] - 16
        target = pay[depth : depth + 16, :].astype(F32)[0:1]
        box = iota((boxes, depth), 0).astype(F32)
        hits.append(jnp.where(box == target, 1.0, 0.0).astype(BF16))
        values.append(pay[0:depth, :])
    local = local_ref[...] + dot(jnp.concatenate(hits, axis=1), jnp.concatenate(values, axis=0))
    far = dot(local.astype(BF16), eval_ref[...])
    total = near_ref[...] * (1.0 / (4.0 * math.pi)) + far
    live = iota((boxes, LANES), 1) < count_columns(cnt_ref, boxes)
    out_ref[...] = jnp.where(live, total, 0.0)


VMEM = pl.BlockSpec(memory_space=pltpu.VMEM)
SMEM = pl.BlockSpec(memory_space=pltpu.SMEM)
MIB = 1024 * 1024


def body(
    n_oct,
    n_cube,
    charges,
    panel_counts,
    positions,
    moment_map,
    translations,
    evaluation,
    near_boxes,
    group_sources,
    group_patterns,
    remote_sources,
    remote_patterns,
    remote_targets,
):
    boxes, panels = charges.shape
    width = moment_map.shape[1]
    patterns = translations.shape[0]
    operators = translations.reshape(patterns * width, width)
    counts = panel_counts.reshape(boxes // LANES, LANES)
    slot_index = jnp.arange(panels, dtype=jnp.int32)
    live = slot_index[None, :] < panel_counts[:, None]
    strength = jnp.where(live, charges, jnp.zeros_like(charges))
    multipole = jnp.dot(strength, moment_map, preferred_element_type=F32).astype(BF16)

    me = lax.axis_index("cube")
    along = [multipole] + [
        lax.ppermute(multipole, "cube", [(i, i ^ k) for i in range(n_cube)])
        for k in range(2, n_cube, 2)
    ]

    near = pl.pallas_call(
        near_kernel,
        out_shape=jax.ShapeDtypeStruct((boxes, panels), F32),
        in_specs=[SMEM, VMEM, VMEM, VMEM],
        out_specs=VMEM,
        scratch_shapes=[
            pltpu.VMEM((8, boxes, panels), F32),
            pltpu.VMEM((boxes, 80, panels), BF16),
            pltpu.VMEM((boxes // 8, panels, LANES), BF16),
        ],
        compiler_params=pltpu.CompilerParams(vmem_limit_bytes=24 * MIB),
        cost_estimate=pl.CostEstimate(
            flops=15_000_000_000, bytes_accessed=1_000_000, transcendentals=16_000_000
        ),
        name="near",
    )(near_boxes.T, counts, charges, positions)

    near, base, *along = lax.optimization_barrier((near, multipole, *along))
    mine = jnp.concatenate(along, axis=0)
    other = lax.ppermute(mine, "cube", [(i, i ^ 1) for i in range(n_cube)])

    slots, fanin = remote_sources.shape[3:]
    sent = pl.pallas_call(
        slot_kernel,
        out_shape=jax.ShapeDtypeStruct((n_oct, 2 * slots + 16, width), BF16),
        in_specs=[VMEM] * 5,
        out_specs=VMEM,
        scratch_shapes=[pltpu.VMEM((n_oct * slots, patterns * width), BF16)],
        compiler_params=pltpu.CompilerParams(vmem_limit_bytes=16 * MIB),
        cost_estimate=pl.CostEstimate(
            flops=1_000_000_000, bytes_accessed=1_000_000, transcendentals=0
        ),
        name="slots",
    )(
        base,
        remote_sources[0, 0].transpose(0, 2, 1),
        remote_patterns[0, 0].transpose(0, 2, 1),
        remote_targets[0, 0],
        operators,
    )
    octant = lax.axis_index("oct")
    payloads = []
    for k in range(n_oct):
        part = lax.dynamic_index_in_dim(sent, octant ^ k, 0, keepdims=False)
        if k > 0:
            part = lax.ppermute(part, "oct", [(i, i ^ k) for i in range(n_oct)])
        payloads.append(part)

    klist = group_sources.shape[1]
    group = n_cube * boxes
    code = (group_sources ^ (me * boxes)) + group * group_patterns
    near_local = pl.pallas_call(
        functools.partial(group_kernel, blocks=n_cube, fanin=klist),
        out_shape=jax.ShapeDtypeStruct((boxes, width), F32),
        in_specs=[VMEM] * 4,
        out_specs=VMEM,
        scratch_shapes=[pltpu.VMEM((boxes, patterns * width), BF16)],
        compiler_params=pltpu.CompilerParams(vmem_limit_bytes=24 * MIB),
        cost_estimate=pl.CostEstimate(
            flops=3_000_000_000, bytes_accessed=2_000_000, transcendentals=0
        ),
        name="group",
    )(code.reshape(-1, LANES), operators, mine, other)

    return pl.pallas_call(
        final_kernel,
        out_shape=jax.ShapeDtypeStruct((boxes, panels), F32),
        in_specs=[VMEM] * (4 + n_oct),
        out_specs=VMEM,
        compiler_params=pltpu.CompilerParams(vmem_limit_bytes=16 * MIB),
        cost_estimate=pl.CostEstimate(
            flops=200_000_000, bytes_accessed=600_000, transcendentals=0
        ),
        name="final",
    )(counts, near, near_local, evaluation, *payloads)


def solution(mesh):
    n_oct = mesh.shape["oct"]
    n_cube = mesh.shape["cube"]

    def run(*arrays):
        return body(n_oct, n_cube, *arrays)

    return jax.shard_map(
        run,
        mesh=mesh,
        in_specs=(
            P(("oct", "cube"), None),
            P(("oct", "cube")),
            P(None, ("oct", "cube"), None),
            P(),
            P(),
            P(),
            P(("oct", "cube"), None),
            P(("oct", "cube"), None),
            P(("oct", "cube"), None),
            P("oct", "cube", None, None, None),
            P("oct", "cube", None, None, None),
            P("oct", "cube", None, None),
        ),
        out_specs=P(("oct", "cube"), None),
        check_vma=False,
    )
```

```python
import functools
import math

import jax
import jax.numpy as jnp
from jax import lax
from jax.experimental import pallas as pl
from jax.experimental.pallas import tpu as pltpu
from jax.sharding import PartitionSpec as P

F32 = jnp.float32
BF16 = jnp.bfloat16
LANES = 128
EPS = 0.0025


def iota(shape, dim):
    return lax.broadcasted_iota(jnp.int32, shape, dim)


def count_columns(cnt_ref, boxes):
    eye = iota((LANES, LANES), 0) == iota((LANES, LANES), 1)
    cols = [
        jnp.sum(jnp.where(eye, cnt_ref[i : i + 1, :], 0), axis=1, keepdims=True)
        for i in range(boxes // LANES)
    ]
    return jnp.concatenate(cols, axis=0)


def log2(value):
    return value.bit_length() - 1


def code_columns(codes):
    rows = codes.shape[0]
    padded = jnp.concatenate([codes, jnp.zeros((LANES - rows, LANES), codes.dtype)], axis=0)
    return padded.T


def onehot(local, width):
    lane = iota((LANES, LANES), 1)
    parts = [
        jnp.where(local == lane + LANES * i, 1.0, 0.0).astype(BF16) for i in range(width // LANES)
    ]
    return jnp.concatenate(parts, axis=1)


def pattern_matrix(pattern_row, eye, patterns):
    own = jnp.where(eye, jnp.broadcast_to(pattern_row, eye.shape), -1)
    parts = [jnp.where(own == p, 1.0, 0.0).astype(BF16) for p in range(patterns)]
    return jnp.concatenate(parts, axis=0)


def dot(a, b):
    return jnp.dot(a, b, preferred_element_type=F32)


def slot_kernel(m_ref, src_ref, pat_ref, tgt_ref, ops_ref, out_ref, sums):
    boxes, width = m_ref.shape
    patterns = ops_ref.shape[0] // width
    groups, fanin, slots = src_ref.shape
    pack = LANES // slots
    tiles = fanin // pack
    m = m_ref[...]

    def packed(ref, d, h):
        return jnp.concatenate([ref[d, h * pack + i : h * pack + i + 1, :] for i in range(pack)], axis=1)

    sources = [packed(src_ref, d, h) for d in range(groups) for h in range(tiles)]
    cols = code_columns(jnp.concatenate(sources, axis=0))
    eye = iota((slots, LANES), 0) == (iota((slots, LANES), 1) & (slots - 1))
    for d in range(groups):
        ones = []
        pats = []
        for h in range(tiles):
            i = d * tiles + h
            ones.append(onehot(jnp.broadcast_to(cols[:, i : i + 1], (LANES, LANES)), boxes))
            pats.append(pattern_matrix(packed(pat_ref, d, h), eye, patterns))
        got = dot(jnp.concatenate(ones, axis=0), m).astype(BF16)
        s = dot(jnp.concatenate(pats, axis=1), got).astype(BF16)
        for p in range(patterns):
            sums[d * slots : (d + 1) * slots, p * width : (p + 1) * width] = s[
                p * slots : (p + 1) * slots
            ]
    result = dot(sums[...], ops_ref[...])
    hi = result.astype(BF16)
    lo = (result - hi.astype(F32)).astype(BF16)
    box = iota((boxes, slots), 0)
    for d in range(groups):
        hit = jnp.where(box == tgt_ref[d : d + 1, :], 1.0, 0.0)
        hit = jnp.concatenate([hit, hit], axis=1).astype(BF16)
        part = slice(d * slots, (d + 1) * slots)
        out_ref[d * boxes : (d + 1) * boxes, :] = dot(
            hit, jnp.concatenate([hi[part], lo[part]], axis=0)
        )


def near_kernel(nb_ref, cnt_ref, chg_ref, pos_ref, out_ref, feat, right, left):
    boxes = chg_ref.shape[0]
    knear = nb_ref.shape[0]
    live = iota((boxes, LANES), 1) < count_columns(cnt_ref, boxes)
    feat[7] = jnp.where(live, chg_ref[...].astype(F32), 0.0)
    norm = jnp.zeros((boxes, LANES), F32)
    for c in range(3):
        u = pos_ref[c] - 1.0
        h = u.astype(BF16).astype(F32)
        m = (u - h).astype(BF16).astype(F32)
        feat[2 * c] = h
        feat[2 * c + 1] = m
        v = h + m
        norm = norm + v * v
    feat[6] = norm

    def build(g, carry):
        rows = pl.ds(pl.multiple_of(g * 8, 8), 8)
        tile = [feat[f, rows, :] for f in range(7)]
        parts = []
        for c in range(3):
            h = -2.0 * tile[2 * c]
            m = -2.0 * tile[2 * c + 1]
            parts += [h, h, m, m]
        n = tile[6] + EPS
        n1 = n.astype(BF16).astype(F32)
        n2 = (n - n1).astype(BF16).astype(F32)
        parts += [n1, n2, n - n1 - n2, jnp.zeros((8, LANES), F32)]
        left[g] = jnp.concatenate(parts, axis=0).T.astype(BF16)
        for r in range(8):
            for c in range(3):
                h = jnp.broadcast_to(tile[2 * c][r : r + 1], (8, LANES))
                m = jnp.broadcast_to(tile[2 * c + 1][r : r + 1], (8, LANES))
                right[g * 8 + r, 16 * c : 16 * c + 16, :] = jnp.concatenate(
                    [h, m], axis=0
                ).astype(BF16)
        return carry

    lax.fori_loop(0, boxes // 8, build, 0)

    masks = [
        jnp.where((iota((LANES, LANES), 1) & 7) == j, 1.0, 0.0).astype(BF16) for j in range(8)
    ]
    eye = iota((LANES, LANES), 0) == iota((LANES, LANES), 1)
    ones = jnp.where(iota((32, LANES), 0) < 24, 1.0, 0.0).astype(BF16)

    def operand(box):
        x, y, z = [right[box, 16 * c : 16 * c + 16, :] for c in range(3)]
        return jnp.concatenate([x, x, y, y, z, z, ones], axis=0)

    def group(g, carry):
        turned = left[g]
        outs = []
        for r in range(8):
            lhs = turned * masks[r]
            acc = None
            near = [nb_ref[k, g * 8 + r] for k in range(knear)]
            dist = dot(lhs, jnp.concatenate([operand(b) for b in near], axis=1))
            for k in range(knear):
                shift = feat[6, pl.ds(near[k], 1), :]
                q = feat[7, pl.ds(near[k], 1), :]
                term = lax.rsqrt(dist[:, k * LANES : (k + 1) * LANES] + shift) * q
                acc = term if acc is None else acc + term
            total = jnp.sum(acc, axis=1, keepdims=True)
            outs.append(jnp.sum(jnp.where(eye, total, 0.0), axis=0, keepdims=True))
        out_ref[pl.ds(pl.multiple_of(g * 8, 8), 8), :] = jnp.concatenate(outs, axis=0)
        return carry

    lax.fori_loop(0, boxes // 8, group, 0, unroll=2)


def far_kernel(
    code_ref, cnt_ref, near_ref, remote_ref, ops_ref, eval_ref, all_ref, out_ref, sums, *, fanin
):
    boxes, width = out_ref.shape
    sources = all_ref.shape[0]
    patterns = ops_ref.shape[0] // width
    per = LANES // fanin
    tiles = code_ref.shape[0]
    span = 2 * boxes
    pages = sources // span
    table = jnp.concatenate([all_ref[j * span : (j + 1) * span] for j in range(pages)], axis=1)
    codes = code_ref[...]
    cols = code_columns(codes)
    eye = iota((per, LANES), 0) == (iota((per, LANES), 1) >> log2(fanin))
    batch = 4
    for base in range(0, tiles, batch):
        picks = [
            jnp.broadcast_to(cols[:, i : i + 1], (LANES, LANES)) for i in range(base, base + batch)
        ]
        wide = dot(jnp.concatenate([onehot(c & (span - 1), span) for c in picks], axis=0), table)
        for n in range(batch):
            i = base + n
            page = (picks[n] >> log2(span)) & (pages - 1)
            part = wide[n * LANES : (n + 1) * LANES]
            got = part[:, 0:width]
            for j in range(1, pages):
                got = jnp.where(page == j, part[:, j * width : (j + 1) * width], got)
            pat = pattern_matrix(codes[i : i + 1, :] >> log2(sources), eye, patterns)
            s = dot(pat, got.astype(BF16)).astype(BF16)
            for p in range(patterns):
                sums[i * per : (i + 1) * per, p * width : (p + 1) * width] = s[
                    p * per : (p + 1) * per
                ]
    local = dot(sums[...], ops_ref[...]) + remote_ref[...]
    far = dot(local.astype(BF16), eval_ref[...])
    total = near_ref[...] * (1.0 / (4.0 * math.pi)) + far
    live = iota((boxes, LANES), 1) < count_columns(cnt_ref, boxes)
    out_ref[...] = jnp.where(live, total, 0.0)


VMEM = pl.BlockSpec(memory_space=pltpu.VMEM)
SMEM = pl.BlockSpec(memory_space=pltpu.SMEM)
MIB = 1024 * 1024


def body(
    n_oct,
    n_cube,
    charges,
    panel_counts,
    positions,
    moment_map,
    translations,
    evaluation,
    near_boxes,
    group_sources,
    group_patterns,
    remote_sources,
    remote_patterns,
    remote_targets,
):
    boxes, panels = charges.shape
    width = moment_map.shape[1]
    patterns = translations.shape[0]
    operators = translations.reshape(patterns * width, width)
    counts = panel_counts.reshape(boxes // LANES, LANES)
    slot_index = jnp.arange(panels, dtype=jnp.int32)
    live = slot_index[None, :] < panel_counts[:, None]
    strength = jnp.where(live, charges, jnp.zeros_like(charges))
    multipole = jnp.dot(strength, moment_map, preferred_element_type=F32).astype(BF16)

    gathered = lax.all_gather(multipole, "cube", axis=0, tiled=True)

    slots, fanin = remote_sources.shape[3:]
    sent = pl.pallas_call(
        slot_kernel,
        out_shape=jax.ShapeDtypeStruct((n_oct * boxes, width), F32),
        in_specs=[VMEM] * 5,
        out_specs=VMEM,
        scratch_shapes=[pltpu.VMEM((n_oct * slots, patterns * width), BF16)],
        compiler_params=pltpu.CompilerParams(vmem_limit_bytes=16 * MIB),
        cost_estimate=pl.CostEstimate(
            flops=1_000_000_000, bytes_accessed=1_000_000, transcendentals=0
        ),
        name="slots",
    )(
        multipole,
        remote_sources[0, 0].transpose(0, 2, 1),
        remote_patterns[0, 0].transpose(0, 2, 1),
        remote_targets[0, 0],
        operators,
    )
    remote_local = lax.psum_scatter(sent, "oct", scatter_dimension=0, tiled=True)

    near = pl.pallas_call(
        near_kernel,
        out_shape=jax.ShapeDtypeStruct((boxes, panels), F32),
        in_specs=[SMEM, VMEM, VMEM, VMEM],
        out_specs=VMEM,
        scratch_shapes=[
            pltpu.VMEM((8, boxes, panels), F32),
            pltpu.VMEM((boxes, 48, panels), BF16),
            pltpu.VMEM((boxes // 8, panels, LANES), BF16),
        ],
        compiler_params=pltpu.CompilerParams(vmem_limit_bytes=24 * MIB),
        cost_estimate=pl.CostEstimate(
            flops=15_000_000_000, bytes_accessed=1_000_000, transcendentals=16_000_000
        ),
        name="near",
    )(near_boxes.T, counts, charges, positions)

    klist = group_sources.shape[1]
    code = group_sources + (n_cube * boxes) * group_patterns
    near, gathered, remote_local = lax.optimization_barrier((near, gathered, remote_local))
    return pl.pallas_call(
        functools.partial(far_kernel, fanin=klist),
        out_shape=jax.ShapeDtypeStruct((boxes, panels), F32),
        in_specs=[VMEM] * 7,
        out_specs=VMEM,
        scratch_shapes=[pltpu.VMEM((boxes, patterns * width), BF16)],
        compiler_params=pltpu.CompilerParams(vmem_limit_bytes=24 * MIB),
        cost_estimate=pl.CostEstimate(
            flops=3_000_000_000, bytes_accessed=2_000_000, transcendentals=0
        ),
        name="far",
    )(code.reshape(-1, LANES), counts, near, remote_local, operators, evaluation, gathered)


def solution(mesh):
    n_oct = mesh.shape["oct"]
    n_cube = mesh.shape["cube"]

    def run(*arrays):
        return body(n_oct, n_cube, *arrays)

    return jax.shard_map(
        run,
        mesh=mesh,
        in_specs=(
            P(("oct", "cube"), None),
            P(("oct", "cube")),
            P(None, ("oct", "cube"), None),
            P(),
            P(),
            P(),
            P(("oct", "cube"), None),
            P(("oct", "cube"), None),
            P(("oct", "cube"), None),
            P("oct", "cube", None, None, None),
            P("oct", "cube", None, None, None),
            P("oct", "cube", None, None),
        ),
        out_specs=P(("oct", "cube"), None),
        check_vma=False,
    )
```

```python
import functools
import math

import jax
import jax.numpy as jnp
from jax import lax
from jax.experimental import pallas as pl
from jax.experimental.pallas import tpu as pltpu
from jax.sharding import PartitionSpec as P

F32 = jnp.float32
BF16 = jnp.bfloat16
LANES = 128
EPS = 0.0025


def iota(shape, dim):
    return lax.broadcasted_iota(jnp.int32, shape, dim)


def count_columns(cnt_ref, boxes):
    eye = iota((LANES, LANES), 0) == iota((LANES, LANES), 1)
    cols = [
        jnp.sum(jnp.where(eye, cnt_ref[i : i + 1, :], 0), axis=1, keepdims=True)
        for i in range(boxes // LANES)
    ]
    return jnp.concatenate(cols, axis=0)


def log2(value):
    return value.bit_length() - 1


def code_columns(codes):
    rows = codes.shape[0]
    padded = jnp.concatenate([codes, jnp.zeros((LANES - rows, LANES), codes.dtype)], axis=0)
    return padded.T


def onehot(local, width):
    lane = iota((LANES, LANES), 1)
    parts = [
        jnp.where(local == lane + LANES * i, 1.0, 0.0).astype(BF16) for i in range(width // LANES)
    ]
    return jnp.concatenate(parts, axis=1)


def pattern_matrix(pattern_row, eye, patterns):
    own = jnp.where(eye, jnp.broadcast_to(pattern_row, eye.shape), -1)
    parts = [jnp.where(own == p, 1.0, 0.0).astype(BF16) for p in range(patterns)]
    return jnp.concatenate(parts, axis=0)


def dot(a, b):
    return jnp.dot(a, b, preferred_element_type=F32)


def slot_kernel(m_ref, src_ref, pat_ref, tgt_ref, ops_ref, out_ref, sums):
    boxes, width = m_ref.shape
    patterns = ops_ref.shape[0] // width
    groups, fanin, slots = src_ref.shape
    rows = out_ref.shape[1]
    pack = LANES // slots
    tiles = fanin // pack
    m = m_ref[...]

    def packed(ref, d, h):
        return jnp.concatenate([ref[d, h * pack + i : h * pack + i + 1, :] for i in range(pack)], axis=1)

    sources = [packed(src_ref, d, h) for d in range(groups) for h in range(tiles)]
    cols = code_columns(jnp.concatenate(sources, axis=0))
    eye = iota((slots, LANES), 0) == (iota((slots, LANES), 1) & (slots - 1))
    for d in range(groups):
        ones = []
        pats = []
        for h in range(tiles):
            i = d * tiles + h
            ones.append(onehot(jnp.broadcast_to(cols[:, i : i + 1], (LANES, LANES)), boxes))
            pats.append(pattern_matrix(packed(pat_ref, d, h), eye, patterns))
        got = dot(jnp.concatenate(ones, axis=0), m).astype(BF16)
        s = dot(jnp.concatenate(pats, axis=1), got).astype(BF16)
        for p in range(patterns):
            sums[d * slots : (d + 1) * slots, p * width : (p + 1) * width] = s[
                p * slots : (p + 1) * slots
            ]
    result = dot(sums[...], ops_ref[...])
    hi = result.astype(BF16)
    lo = (result - hi.astype(F32)).astype(BF16)
    for d in range(groups):
        target = tgt_ref[d : d + 1, :].astype(F32)
        out_ref[d, 0:slots, :] = hi[d * slots : (d + 1) * slots]
        out_ref[d, slots : 2 * slots, :] = lo[d * slots : (d + 1) * slots]
        out_ref[d, 2 * slots : rows, :] = jnp.broadcast_to(
            jnp.concatenate([target, target], axis=1), (rows - 2 * slots, 2 * slots)
        ).astype(BF16)


def near_kernel(nb_ref, cnt_ref, chg_ref, pos_ref, out_ref, feat, right, left):
    boxes = chg_ref.shape[0]
    knear = nb_ref.shape[0]
    live = iota((boxes, LANES), 1) < count_columns(cnt_ref, boxes)
    feat[7] = jnp.where(live, chg_ref[...].astype(F32), 0.0)
    norm = jnp.zeros((boxes, LANES), F32)
    for c in range(3):
        u = pos_ref[c] - 1.0
        h = u.astype(BF16).astype(F32)
        m = (u - h).astype(BF16).astype(F32)
        feat[2 * c] = h
        feat[2 * c + 1] = m
        v = h + m
        norm = norm + v * v
    feat[6] = norm

    def build(g, carry):
        rows = pl.ds(pl.multiple_of(g * 8, 8), 8)
        tile = [feat[f, rows, :] for f in range(7)]
        parts = []
        for c in range(3):
            h = -2.0 * tile[2 * c]
            m = -2.0 * tile[2 * c + 1]
            parts += [h, h, m, m]
        n = tile[6] + EPS
        n1 = n.astype(BF16).astype(F32)
        n2 = (n - n1).astype(BF16).astype(F32)
        parts += [n1, n2, n - n1 - n2, jnp.zeros((8, LANES), F32)]
        left[g] = jnp.concatenate(parts, axis=0).T.astype(BF16)
        for r in range(8):
            for c in range(3):
                h = jnp.broadcast_to(tile[2 * c][r : r + 1], (8, LANES))
                m = jnp.broadcast_to(tile[2 * c + 1][r : r + 1], (8, LANES))
                right[g * 8 + r, 16 * c : 16 * c + 16, :] = jnp.concatenate(
                    [h, m], axis=0
                ).astype(BF16)
        return carry

    lax.fori_loop(0, boxes // 8, build, 0, unroll=4)

    masks = [
        jnp.where((iota((LANES, LANES), 1) & 7) == j, 1.0, 0.0).astype(BF16) for j in range(8)
    ]
    select = [
        jnp.where(iota((16, 2 * LANES), 0) == j, 1.0, 0.0).astype(BF16) for j in range(8)
    ]
    ones = jnp.where(iota((32, LANES), 0) < 24, 1.0, 0.0).astype(BF16)

    def operand(box):
        x, y, z = [right[box, 16 * c : 16 * c + 16, :] for c in range(3)]
        return jnp.concatenate([x, x, y, y, z, z, ones], axis=0)

    def group(g, carry):
        turned = left[g]
        out = jnp.zeros((16, LANES), F32)
        for r in range(8):
            lhs = turned * masks[r]
            acc = None
            for k in range(0, knear, 2):
                pair = [nb_ref[k + i, g * 8 + r] for i in range(2)]
                dist = dot(lhs, jnp.concatenate([operand(b) for b in pair], axis=1))
                for i in range(2):
                    shift = feat[6, pl.ds(pair[i], 1), :]
                    q = feat[7, pl.ds(pair[i], 1), :]
                    term = lax.rsqrt(dist[:, i * LANES : (i + 1) * LANES] + shift) * q
                    acc = term if acc is None else acc + term
            hi = acc.astype(BF16)
            lo = (acc - hi.astype(F32)).astype(BF16)
            out = out + lax.dot_general(
                select[r],
                jnp.concatenate([hi, lo], axis=1),
                (((1,), (1,)), ((), ())),
                preferred_element_type=F32,
            )
        out_ref[pl.ds(pl.multiple_of(g * 8, 8), 8), :] = out[0:8]
        return carry

    lax.fori_loop(0, boxes // 8, group, 0, unroll=2)


def group_kernel(*refs, blocks, fanin):
    code_ref, ops_ref, mine_ref, other_ref, out_ref, sums = refs
    width = mine_ref.shape[1]
    boxes = mine_ref.shape[0] // (blocks // 2)
    patterns = ops_ref.shape[0] // width
    per = LANES // fanin
    tiles = code_ref.shape[0]
    span = 2 * boxes
    pages = blocks // 2
    table = jnp.concatenate(
        [
            jnp.concatenate(
                [mine_ref[j * boxes : (j + 1) * boxes], other_ref[j * boxes : (j + 1) * boxes]], axis=0
            )
            for j in range(pages)
        ],
        axis=1,
    )
    codes = code_ref[...]
    cols = code_columns(codes)
    eye = iota((per, LANES), 0) == (iota((per, LANES), 1) >> log2(fanin))
    batch = 4
    for base in range(0, tiles, batch):
        picks = [
            jnp.broadcast_to(cols[:, i : i + 1], (LANES, LANES)) for i in range(base, base + batch)
        ]
        wide = dot(jnp.concatenate([onehot(c & (span - 1), span) for c in picks], axis=0), table)
        for n in range(batch):
            i = base + n
            page = (picks[n] >> log2(span)) & (pages - 1)
            part = wide[n * LANES : (n + 1) * LANES]
            got = part[:, 0:width]
            for j in range(1, pages):
                got = jnp.where(page == j, part[:, j * width : (j + 1) * width], got)
            pat = pattern_matrix(codes[i : i + 1, :] >> log2(blocks * boxes), eye, patterns)
            s = dot(pat, got.astype(BF16)).astype(BF16)
            for p in range(patterns):
                sums[i * per : (i + 1) * per, p * width : (p + 1) * width] = s[
                    p * per : (p + 1) * per
                ]
    out_ref[...] = dot(sums[...], ops_ref[...])


def final_kernel(*refs):
    cnt_ref, near_ref, local_ref, eval_ref = refs[:4]
    pay_refs = refs[4:-1]
    out_ref = refs[-1]
    boxes = local_ref.shape[0]
    hits = []
    values = []
    for pay in pay_refs:
        depth = pay.shape[0] - 16
        target = pay[depth : depth + 16, :].astype(F32)[0:1]
        box = iota((boxes, depth), 0).astype(F32)
        hits.append(jnp.where(box == target, 1.0, 0.0).astype(BF16))
        values.append(pay[0:depth, :])
    local = local_ref[...] + dot(jnp.concatenate(hits, axis=1), jnp.concatenate(values, axis=0))
    far = dot(local.astype(BF16), eval_ref[...])
    total = near_ref[...] * (1.0 / (4.0 * math.pi)) + far
    live = iota((boxes, LANES), 1) < count_columns(cnt_ref, boxes)
    out_ref[...] = jnp.where(live, total, 0.0)


VMEM = pl.BlockSpec(memory_space=pltpu.VMEM)
SMEM = pl.BlockSpec(memory_space=pltpu.SMEM)
MIB = 1024 * 1024


def body(
    n_oct,
    n_cube,
    charges,
    panel_counts,
    positions,
    moment_map,
    translations,
    evaluation,
    near_boxes,
    group_sources,
    group_patterns,
    remote_sources,
    remote_patterns,
    remote_targets,
):
    boxes, panels = charges.shape
    width = moment_map.shape[1]
    patterns = translations.shape[0]
    operators = translations.reshape(patterns * width, width)
    counts = panel_counts.reshape(boxes // LANES, LANES)
    slot_index = jnp.arange(panels, dtype=jnp.int32)
    live = slot_index[None, :] < panel_counts[:, None]
    strength = jnp.where(live, charges, jnp.zeros_like(charges))
    multipole = jnp.dot(strength, moment_map, preferred_element_type=F32).astype(BF16)

    me = lax.axis_index("cube")
    along = [multipole] + [
        lax.ppermute(multipole, "cube", [(i, i ^ k) for i in range(n_cube)])
        for k in range(2, n_cube, 2)
    ]

    near = pl.pallas_call(
        near_kernel,
        out_shape=jax.ShapeDtypeStruct((boxes, panels), F32),
        in_specs=[SMEM, VMEM, VMEM, VMEM],
        out_specs=VMEM,
        scratch_shapes=[
            pltpu.VMEM((8, boxes, panels), F32),
            pltpu.VMEM((boxes, 48, panels), BF16),
            pltpu.VMEM((boxes // 8, panels, LANES), BF16),
        ],
        compiler_params=pltpu.CompilerParams(vmem_limit_bytes=24 * MIB),
        cost_estimate=pl.CostEstimate(
            flops=15_000_000_000, bytes_accessed=1_000_000, transcendentals=16_000_000
        ),
        name="near",
    )(near_boxes.T, counts, charges, positions)

    near, base, *along = lax.optimization_barrier((near, multipole, *along))
    mine = jnp.concatenate(along, axis=0)
    other = lax.ppermute(mine, "cube", [(i, i ^ 1) for i in range(n_cube)])

    slots, fanin = remote_sources.shape[3:]
    sent = pl.pallas_call(
        slot_kernel,
        out_shape=jax.ShapeDtypeStruct((n_oct, 2 * slots + 16, width), BF16),
        in_specs=[VMEM] * 5,
        out_specs=VMEM,
        scratch_shapes=[pltpu.VMEM((n_oct * slots, patterns * width), BF16)],
        compiler_params=pltpu.CompilerParams(vmem_limit_bytes=16 * MIB),
        cost_estimate=pl.CostEstimate(
            flops=1_000_000_000, bytes_accessed=1_000_000, transcendentals=0
        ),
        name="slots",
    )(
        base,
        remote_sources[0, 0].transpose(0, 2, 1),
        remote_patterns[0, 0].transpose(0, 2, 1),
        remote_targets[0, 0],
        operators,
    )
    octant = lax.axis_index("oct")
    payloads = []
    for k in range(n_oct):
        part = lax.dynamic_index_in_dim(sent, octant ^ k, 0, keepdims=False)
        if k > 0:
            part = lax.ppermute(part, "oct", [(i, i ^ k) for i in range(n_oct)])
        payloads.append(part)

    klist = group_sources.shape[1]
    group = n_cube * boxes
    code = (group_sources ^ (me * boxes)) + group * group_patterns
    near_local = pl.pallas_call(
        functools.partial(group_kernel, blocks=n_cube, fanin=klist),
        out_shape=jax.ShapeDtypeStruct((boxes, width), F32),
        in_specs=[VMEM] * 4,
        out_specs=VMEM,
        scratch_shapes=[pltpu.VMEM((boxes, patterns * width), BF16)],
        compiler_params=pltpu.CompilerParams(vmem_limit_bytes=24 * MIB),
        cost_estimate=pl.CostEstimate(
            flops=3_000_000_000, bytes_accessed=2_000_000, transcendentals=0
        ),
        name="group",
    )(code.reshape(-1, LANES), operators, mine, other)

    return pl.pallas_call(
        final_kernel,
        out_shape=jax.ShapeDtypeStruct((boxes, panels), F32),
        in_specs=[VMEM] * (4 + n_oct),
        out_specs=VMEM,
        compiler_params=pltpu.CompilerParams(vmem_limit_bytes=16 * MIB),
        cost_estimate=pl.CostEstimate(
            flops=200_000_000, bytes_accessed=600_000, transcendentals=0
        ),
        name="final",
    )(counts, near, near_local, evaluation, *payloads)


def solution(mesh):
    n_oct = mesh.shape["oct"]
    n_cube = mesh.shape["cube"]

    def run(*arrays):
        return body(n_oct, n_cube, *arrays)

    return jax.shard_map(
        run,
        mesh=mesh,
        in_specs=(
            P(("oct", "cube"), None),
            P(("oct", "cube")),
            P(None, ("oct", "cube"), None),
            P(),
            P(),
            P(),
            P(("oct", "cube"), None),
            P(("oct", "cube"), None),
            P(("oct", "cube"), None),
            P("oct", "cube", None, None, None),
            P("oct", "cube", None, None, None),
            P("oct", "cube", None, None),
        ),
        out_specs=P(("oct", "cube"), None),
        check_vma=False,
    )
```

```python
import functools
import math

import jax
import jax.numpy as jnp
from jax import lax
from jax.experimental import pallas as pl
from jax.experimental.pallas import tpu as pltpu
from jax.sharding import PartitionSpec as P

F32 = jnp.float32
BF16 = jnp.bfloat16
LANES = 128
EPS = 0.0025


def iota(shape, dim):
    return lax.broadcasted_iota(jnp.int32, shape, dim)


def count_columns(cnt_ref, boxes):
    eye = iota((LANES, LANES), 0) == iota((LANES, LANES), 1)
    cols = [
        jnp.sum(jnp.where(eye, cnt_ref[i : i + 1, :], 0), axis=1, keepdims=True)
        for i in range(boxes // LANES)
    ]
    return jnp.concatenate(cols, axis=0)


def log2(value):
    return value.bit_length() - 1


def code_columns(codes):
    rows = codes.shape[0]
    padded = jnp.concatenate([codes, jnp.zeros((LANES - rows, LANES), codes.dtype)], axis=0)
    return padded.T


def onehot(local, width):
    lane = iota((LANES, LANES), 1)
    parts = [
        jnp.where(local == lane + LANES * i, 1.0, 0.0).astype(BF16) for i in range(width // LANES)
    ]
    return jnp.concatenate(parts, axis=1)


def pattern_matrix(pattern_row, eye, patterns):
    own = jnp.where(eye, jnp.broadcast_to(pattern_row, eye.shape), -1)
    parts = [jnp.where(own == p, 1.0, 0.0).astype(BF16) for p in range(patterns)]
    return jnp.concatenate(parts, axis=0)


def dot(a, b):
    return jnp.dot(a, b, preferred_element_type=F32)


def slot_kernel(m_ref, src_ref, pat_ref, tgt_ref, ops_ref, out_ref, sums):
    boxes, width = m_ref.shape
    patterns = ops_ref.shape[0] // width
    groups, fanin, slots = src_ref.shape
    rows = out_ref.shape[1]
    pack = LANES // slots
    tiles = fanin // pack
    m = m_ref[...]

    def packed(ref, d, h):
        return jnp.concatenate([ref[d, h * pack + i : h * pack + i + 1, :] for i in range(pack)], axis=1)

    sources = [packed(src_ref, d, h) for d in range(groups) for h in range(tiles)]
    cols = code_columns(jnp.concatenate(sources, axis=0))
    eye = iota((slots, LANES), 0) == (iota((slots, LANES), 1) & (slots - 1))
    for d in range(groups):
        ones = []
        pats = []
        for h in range(tiles):
            i = d * tiles + h
            ones.append(onehot(jnp.broadcast_to(cols[:, i : i + 1], (LANES, LANES)), boxes))
            pats.append(pattern_matrix(packed(pat_ref, d, h), eye, patterns))
        got = dot(jnp.concatenate(ones, axis=0), m).astype(BF16)
        s = dot(jnp.concatenate(pats, axis=1), got).astype(BF16)
        for p in range(patterns):
            sums[d * slots : (d + 1) * slots, p * width : (p + 1) * width] = s[
                p * slots : (p + 1) * slots
            ]
    result = dot(sums[...], ops_ref[...])
    hi = result.astype(BF16)
    lo = (result - hi.astype(F32)).astype(BF16)
    for d in range(groups):
        target = tgt_ref[d : d + 1, :].astype(F32)
        out_ref[d, 0:slots, :] = hi[d * slots : (d + 1) * slots]
        out_ref[d, slots : 2 * slots, :] = lo[d * slots : (d + 1) * slots]
        out_ref[d, 2 * slots : rows, :] = jnp.broadcast_to(
            jnp.concatenate([target, target], axis=1), (rows - 2 * slots, 2 * slots)
        ).astype(BF16)


def table_kernel(cnt_ref, chg_ref, pos_ref, rows_ref, right_ref, left_ref, feat):
    boxes = chg_ref.shape[0]
    live = iota((boxes, LANES), 1) < count_columns(cnt_ref, boxes)
    rows_ref[1] = jnp.where(live, chg_ref[...].astype(F32), 0.0)
    norm = jnp.zeros((boxes, LANES), F32)
    for c in range(3):
        u = pos_ref[c] - 1.0
        h = u.astype(BF16).astype(F32)
        m = (u - h).astype(BF16).astype(F32)
        feat[2 * c] = h
        feat[2 * c + 1] = m
        v = h + m
        norm = norm + v * v
    rows_ref[0] = norm

    def build(g, carry):
        rows = pl.ds(pl.multiple_of(g * 8, 8), 8)
        tile = [feat[f, rows, :] for f in range(6)]
        parts = []
        for c in range(3):
            h = -2.0 * tile[2 * c]
            m = -2.0 * tile[2 * c + 1]
            parts += [h, h, m, m]
        n = rows_ref[0, rows, :] + EPS
        n1 = n.astype(BF16).astype(F32)
        n2 = (n - n1).astype(BF16).astype(F32)
        parts += [n1, n2, n - n1 - n2, jnp.zeros((8, LANES), F32)]
        left_ref[g] = jnp.concatenate(parts, axis=0).T.astype(BF16)
        for r in range(8):
            for c in range(3):
                h = jnp.broadcast_to(tile[2 * c][r : r + 1], (8, LANES))
                m = jnp.broadcast_to(tile[2 * c + 1][r : r + 1], (8, LANES))
                right_ref[g * 8 + r, 16 * c : 16 * c + 16, :] = jnp.concatenate(
                    [h, m], axis=0
                ).astype(BF16)
        return carry

    lax.fori_loop(0, boxes // 8, build, 0, unroll=4)


def near_kernel(nb_ref, rows_ref, right_ref, left_ref, out_ref, *, start):
    knear = nb_ref.shape[0]
    masks = [
        jnp.where((iota((LANES, LANES), 1) & 7) == j, 1.0, 0.0).astype(BF16) for j in range(8)
    ]
    eye = iota((LANES, LANES), 0) == iota((LANES, LANES), 1)
    ones = jnp.where(iota((32, LANES), 0) < 24, 1.0, 0.0).astype(BF16)

    def operand(box):
        x, y, z = [right_ref[box, 16 * c : 16 * c + 16, :] for c in range(3)]
        return jnp.concatenate([x, x, y, y, z, z, ones], axis=0)

    def group(i, carry):
        g = i + start
        turned = left_ref[g]
        outs = []
        for r in range(8):
            lhs = turned * masks[r]
            acc = None
            for k in range(0, knear, 2):
                pair = [nb_ref[k + i, g * 8 + r] for i in range(2)]
                dist = dot(lhs, jnp.concatenate([operand(b) for b in pair], axis=1))
                for i in range(2):
                    shift = rows_ref[0, pl.ds(pair[i], 1), :]
                    q = rows_ref[1, pl.ds(pair[i], 1), :]
                    term = lax.rsqrt(dist[:, i * LANES : (i + 1) * LANES] + shift) * q
                    acc = term if acc is None else acc + term
            total = jnp.sum(acc, axis=1, keepdims=True)
            outs.append(jnp.sum(jnp.where(eye, total, 0.0), axis=0, keepdims=True))
        out_ref[pl.ds(pl.multiple_of((g - start) * 8, 8), 8), :] = jnp.concatenate(outs, axis=0)
        return carry

    lax.fori_loop(0, out_ref.shape[0] // 8, group, 0, unroll=2)


def far_kernel(*refs, blocks, fanin, pieces):
    code_ref, cnt_ref, ops_ref, eval_ref, mine_ref, other_ref = refs[:6]
    near_refs = refs[6 : 6 + pieces]
    pay_refs = refs[6 + pieces : -2]
    out_ref, sums = refs[-2:]
    width = mine_ref.shape[1]
    boxes = mine_ref.shape[0] // (blocks // 2)
    patterns = ops_ref.shape[0] // width
    per = LANES // fanin
    tiles = code_ref.shape[0]
    span = 2 * boxes
    pages = blocks // 2
    table = jnp.concatenate(
        [
            jnp.concatenate(
                [mine_ref[j * boxes : (j + 1) * boxes], other_ref[j * boxes : (j + 1) * boxes]], axis=0
            )
            for j in range(pages)
        ],
        axis=1,
    )
    codes = code_ref[...]
    cols = code_columns(codes)
    eye = iota((per, LANES), 0) == (iota((per, LANES), 1) >> log2(fanin))
    batch = 4
    for base in range(0, tiles, batch):
        picks = [
            jnp.broadcast_to(cols[:, i : i + 1], (LANES, LANES)) for i in range(base, base + batch)
        ]
        wide = dot(jnp.concatenate([onehot(c & (span - 1), span) for c in picks], axis=0), table)
        for n in range(batch):
            i = base + n
            page = (picks[n] >> log2(span)) & (pages - 1)
            part = wide[n * LANES : (n + 1) * LANES]
            got = part[:, 0:width]
            for j in range(1, pages):
                got = jnp.where(page == j, part[:, j * width : (j + 1) * width], got)
            pat = pattern_matrix(codes[i : i + 1, :] >> log2(blocks * boxes), eye, patterns)
            s = dot(pat, got.astype(BF16)).astype(BF16)
            for p in range(patterns):
                sums[i * per : (i + 1) * per, p * width : (p + 1) * width] = s[
                    p * per : (p + 1) * per
                ]
    near_local = dot(sums[...], ops_ref[...])
    hits = []
    values = []
    for pay in pay_refs:
        depth = pay.shape[0] - 16
        target = pay[depth : depth + 16, :].astype(F32)[0:1]
        box = iota((boxes, depth), 0).astype(F32)
        hits.append(jnp.where(box == target, 1.0, 0.0).astype(BF16))
        values.append(pay[0:depth, :])
    local = near_local + dot(jnp.concatenate(hits, axis=1), jnp.concatenate(values, axis=0))
    far = dot(local.astype(BF16), eval_ref[...])
    near = jnp.concatenate([ref[...] for ref in near_refs], axis=0)
    total = near * (1.0 / (4.0 * math.pi)) + far
    live = iota((boxes, LANES), 1) < count_columns(cnt_ref, boxes)
    out_ref[...] = jnp.where(live, total, 0.0)


VMEM = pl.BlockSpec(memory_space=pltpu.VMEM)
SMEM = pl.BlockSpec(memory_space=pltpu.SMEM)
MIB = 1024 * 1024
PIECES = 4


def body(
    n_oct,
    n_cube,
    charges,
    panel_counts,
    positions,
    moment_map,
    translations,
    evaluation,
    near_boxes,
    group_sources,
    group_patterns,
    remote_sources,
    remote_patterns,
    remote_targets,
):
    boxes, panels = charges.shape
    width = moment_map.shape[1]
    patterns = translations.shape[0]
    operators = translations.reshape(patterns * width, width)
    counts = panel_counts.reshape(boxes // LANES, LANES)
    slot_index = jnp.arange(panels, dtype=jnp.int32)
    live = slot_index[None, :] < panel_counts[:, None]
    strength = jnp.where(live, charges, jnp.zeros_like(charges))
    multipole = jnp.dot(strength, moment_map, preferred_element_type=F32).astype(BF16)

    me = lax.axis_index("cube")
    octant = lax.axis_index("oct")

    def over_cube(value, k):
        return lax.ppermute(value, "cube", [(i, i ^ k) for i in range(n_cube)])

    def over_oct(value, k):
        return lax.ppermute(value, "oct", [(i, i ^ k) for i in range(n_oct)])

    def after(value, *earlier):
        return lax.optimization_barrier((value, *earlier))[0]

    steps = list(range(2, n_cube, 2))
    tables = pl.pallas_call(
        table_kernel,
        out_shape=(
            jax.ShapeDtypeStruct((2, boxes, panels), F32),
            jax.ShapeDtypeStruct((boxes, 48, panels), BF16),
            jax.ShapeDtypeStruct((boxes // 8, panels, LANES), BF16),
        ),
        in_specs=[VMEM] * 3,
        out_specs=(VMEM,) * 3,
        scratch_shapes=[pltpu.VMEM((6, boxes, panels), F32)],
        compiler_params=pltpu.CompilerParams(vmem_limit_bytes=24 * MIB),
        cost_estimate=pl.CostEstimate(
            flops=1_000_000_000, bytes_accessed=1_000_000, transcendentals=0
        ),
        name="tables",
    )(counts, charges, positions)

    neighbours = near_boxes.T
    size = boxes // PIECES

    def near_piece(i, tables):
        return pl.pallas_call(
            functools.partial(near_kernel, start=i * size // 8),
            out_shape=jax.ShapeDtypeStruct((size, panels), F32),
            in_specs=[SMEM, VMEM, VMEM, VMEM],
            out_specs=VMEM,
            compiler_params=pltpu.CompilerParams(vmem_limit_bytes=16 * MIB),
            cost_estimate=pl.CostEstimate(
                flops=4_000_000_000, bytes_accessed=1_000_000, transcendentals=4_000_000
            ),
            name="near",
        )(neighbours, *tables)

    first, *rest = steps
    along = {0: multipole, first: over_cube(multipole, first)}
    held = after(multipole, *tables)
    for k in rest[: (len(rest) + 1) // 2]:
        along[k] = over_cube(held, k)
    near = [near_piece(0, tables)]
    held = after(multipole, near[0])
    for k in rest[(len(rest) + 1) // 2 :]:
        along[k] = over_cube(held, k)

    slots, fanin = remote_sources.shape[3:]
    sent = pl.pallas_call(
        slot_kernel,
        out_shape=jax.ShapeDtypeStruct((n_oct, 2 * slots + 16, width), BF16),
        in_specs=[VMEM] * 5,
        out_specs=VMEM,
        scratch_shapes=[pltpu.VMEM((n_oct * slots, patterns * width), BF16)],
        compiler_params=pltpu.CompilerParams(vmem_limit_bytes=16 * MIB),
        cost_estimate=pl.CostEstimate(
            flops=1_000_000_000, bytes_accessed=1_000_000, transcendentals=0
        ),
        name="slots",
    )(
        held,
        remote_sources[0, 0].transpose(0, 2, 1),
        remote_patterns[0, 0].transpose(0, 2, 1),
        remote_targets[0, 0],
        operators,
    )
    parts = [
        lax.dynamic_index_in_dim(sent, octant ^ k, 0, keepdims=False) for k in range(n_oct)
    ]
    third = -(-(n_oct - 1) // 3)
    got = {0: parts[0]}
    for k in range(1, min(1 + third, n_oct)):
        got[k] = over_oct(parts[k], k)
    tables = lax.optimization_barrier((*tables, sent, near[0]))[:3]
    near.append(near_piece(1, tables))

    held = lax.optimization_barrier((*[along[k] for k in sorted(along)], near[1]))[:-1]
    mine = jnp.concatenate(held, axis=0)
    other = over_cube(mine, 1)
    for k in range(1 + third, min(1 + 2 * third, n_oct)):
        got[k] = over_oct(after(parts[k], near[1]), k)
    tables = lax.optimization_barrier((*tables, mine))[:3]
    near.append(near_piece(2, tables))
    for k in range(1 + 2 * third, n_oct):
        got[k] = over_oct(after(parts[k], near[2]), k)
    tables = lax.optimization_barrier((*tables, near[2]))[:3]
    near.append(near_piece(3, tables))
    other, *payloads, last = lax.optimization_barrier(
        (other, *[got[k] for k in range(n_oct)], near[3])
    )
    near[3] = last

    klist = group_sources.shape[1]
    group = n_cube * boxes
    code = (group_sources ^ (me * boxes)) + group * group_patterns
    return pl.pallas_call(
        functools.partial(far_kernel, blocks=n_cube, fanin=klist, pieces=PIECES),
        out_shape=jax.ShapeDtypeStruct((boxes, panels), F32),
        in_specs=[VMEM] * (6 + PIECES + n_oct),
        out_specs=VMEM,
        scratch_shapes=[pltpu.VMEM((boxes, patterns * width), BF16)],
        compiler_params=pltpu.CompilerParams(vmem_limit_bytes=24 * MIB),
        cost_estimate=pl.CostEstimate(
            flops=3_000_000_000, bytes_accessed=2_000_000, transcendentals=0
        ),
        name="far",
    )(code.reshape(-1, LANES), counts, operators, evaluation, mine, other, *near, *payloads)


def solution(mesh):
    n_oct = mesh.shape["oct"]
    n_cube = mesh.shape["cube"]

    def run(*arrays):
        return body(n_oct, n_cube, *arrays)

    return jax.shard_map(
        run,
        mesh=mesh,
        in_specs=(
            P(("oct", "cube"), None),
            P(("oct", "cube")),
            P(None, ("oct", "cube"), None),
            P(),
            P(),
            P(),
            P(("oct", "cube"), None),
            P(("oct", "cube"), None),
            P(("oct", "cube"), None),
            P("oct", "cube", None, None, None),
            P("oct", "cube", None, None, None),
            P("oct", "cube", None, None),
        ),
        out_specs=P(("oct", "cube"), None),
        check_vma=False,
    )
```

```python
import functools
import math

import jax
import jax.numpy as jnp
from jax import lax
from jax.experimental import pallas as pl
from jax.experimental.pallas import tpu as pltpu
from jax.sharding import PartitionSpec as P

F32 = jnp.float32
BF16 = jnp.bfloat16
LANES = 128
EPS = 0.0025


def iota(shape, dim):
    return lax.broadcasted_iota(jnp.int32, shape, dim)


def count_columns(cnt_ref, boxes):
    eye = iota((LANES, LANES), 0) == iota((LANES, LANES), 1)
    cols = [
        jnp.sum(jnp.where(eye, cnt_ref[i : i + 1, :], 0), axis=1, keepdims=True)
        for i in range(boxes // LANES)
    ]
    return jnp.concatenate(cols, axis=0)


def log2(value):
    return value.bit_length() - 1


def code_columns(codes):
    rows = codes.shape[0]
    padded = jnp.concatenate([codes, jnp.zeros((LANES - rows, LANES), codes.dtype)], axis=0)
    return padded.T


def onehot(local, width):
    lane = iota((LANES, LANES), 1)
    parts = [
        jnp.where(local == lane + LANES * i, 1.0, 0.0).astype(BF16) for i in range(width // LANES)
    ]
    return jnp.concatenate(parts, axis=1)


def pattern_matrix(pattern_row, eye, patterns):
    own = jnp.where(eye, jnp.broadcast_to(pattern_row, eye.shape), -1)
    parts = [jnp.where(own == p, 1.0, 0.0).astype(BF16) for p in range(patterns)]
    return jnp.concatenate(parts, axis=0)


def dot(a, b):
    return jnp.dot(a, b, preferred_element_type=F32)


def slot_kernel(m_ref, src_ref, pat_ref, tgt_ref, ops_ref, out_ref, sums):
    boxes, width = m_ref.shape
    patterns = ops_ref.shape[0] // width
    groups, fanin, slots = src_ref.shape
    rows = out_ref.shape[1]
    pack = LANES // slots
    tiles = fanin // pack
    m = m_ref[...]

    def packed(ref, d, h):
        return jnp.concatenate([ref[d, h * pack + i : h * pack + i + 1, :] for i in range(pack)], axis=1)

    sources = [packed(src_ref, d, h) for d in range(groups) for h in range(tiles)]
    cols = code_columns(jnp.concatenate(sources, axis=0))
    eye = iota((slots, LANES), 0) == (iota((slots, LANES), 1) & (slots - 1))
    for d in range(groups):
        ones = []
        pats = []
        for h in range(tiles):
            i = d * tiles + h
            ones.append(onehot(jnp.broadcast_to(cols[:, i : i + 1], (LANES, LANES)), boxes))
            pats.append(pattern_matrix(packed(pat_ref, d, h), eye, patterns))
        got = dot(jnp.concatenate(ones, axis=0), m).astype(BF16)
        s = dot(jnp.concatenate(pats, axis=1), got).astype(BF16)
        for p in range(patterns):
            sums[d * slots : (d + 1) * slots, p * width : (p + 1) * width] = s[
                p * slots : (p + 1) * slots
            ]
    result = dot(sums[...], ops_ref[...])
    hi = result.astype(BF16)
    lo = (result - hi.astype(F32)).astype(BF16)
    for d in range(groups):
        target = tgt_ref[d : d + 1, :].astype(F32)
        out_ref[d, 0:slots, :] = hi[d * slots : (d + 1) * slots]
        out_ref[d, slots : 2 * slots, :] = lo[d * slots : (d + 1) * slots]
        out_ref[d, 2 * slots : rows, :] = jnp.broadcast_to(
            jnp.concatenate([target, target], axis=1), (rows - 2 * slots, 2 * slots)
        ).astype(BF16)


def table_kernel(cnt_ref, chg_ref, pos_ref, rows_ref, right_ref, left_ref, feat):
    boxes = chg_ref.shape[0]
    live = iota((boxes, LANES), 1) < count_columns(cnt_ref, boxes)
    rows_ref[1] = jnp.where(live, chg_ref[...].astype(F32), 0.0)
    norm = jnp.zeros((boxes, LANES), F32)
    for c in range(3):
        u = pos_ref[c] - 1.0
        h = u.astype(BF16).astype(F32)
        m = (u - h).astype(BF16).astype(F32)
        feat[2 * c] = h
        feat[2 * c + 1] = m
        v = h + m
        norm = norm + v * v
    rows_ref[0] = norm

    def build(g, carry):
        rows = pl.ds(pl.multiple_of(g * 8, 8), 8)
        tile = [feat[f, rows, :] for f in range(6)]
        parts = []
        for c in range(3):
            h = -2.0 * tile[2 * c]
            m = -2.0 * tile[2 * c + 1]
            parts += [h, h, m, m]
        n = rows_ref[0, rows, :] + EPS
        n1 = n.astype(BF16).astype(F32)
        n2 = (n - n1).astype(BF16).astype(F32)
        parts += [n1, n2, n - n1 - n2, jnp.zeros((8, LANES), F32)]
        left_ref[g] = jnp.concatenate(parts, axis=0).T.astype(BF16)
        for r in range(8):
            for c in range(3):
                h = jnp.broadcast_to(tile[2 * c][r : r + 1], (8, LANES))
                m = jnp.broadcast_to(tile[2 * c + 1][r : r + 1], (8, LANES))
                right_ref[g * 8 + r, 16 * c : 16 * c + 16, :] = jnp.concatenate(
                    [h, m], axis=0
                ).astype(BF16)
        return carry

    lax.fori_loop(0, boxes // 8, build, 0, unroll=4)


def near_kernel(nb_ref, rows_ref, right_ref, left_ref, out_ref, *buffers, start):
    masks = [
        jnp.where((iota((LANES, LANES), 1) & 7) == j, 1.0, 0.0).astype(BF16) for j in range(8)
    ]
    eye = iota((LANES, LANES), 0) == iota((LANES, LANES), 1)
    ones = jnp.where(iota((32, LANES), 0) < 24, 1.0, 0.0).astype(BF16)

    def operand(box):
        x, y, z = [right_ref[box, 16 * c : 16 * c + 16, :] for c in range(3)]
        return jnp.concatenate([x, x, y, y, z, z, ones], axis=0)

    count = out_ref.shape[0] // 8
    last = start + count - 1

    def product(g, r, half, buffer):
        box = g * 8 + r
        lhs = left_ref[g] * masks[r]
        pair = [operand(nb_ref[2 * half + i, box]) for i in range(2)]
        buffer[...] = dot(lhs, jnp.concatenate(pair, axis=1))

    def terms(g, r, half, buffer):
        acc = None
        for i in range(2):
            source = nb_ref[2 * half + i, g * 8 + r]
            shift = rows_ref[0, pl.ds(source, 1), :]
            q = rows_ref[1, pl.ds(source, 1), :]
            term = lax.rsqrt(buffer[:, i * LANES : (i + 1) * LANES] + shift) * q
            acc = term if acc is None else acc + term
        return acc

    halves = nb_ref.shape[0] // 2
    for half in range(halves):
        product(start, 0, half, buffers[half])

    def group(i, carry):
        g = i + start
        outs = []
        for r in range(8):
            after_g, after_r = (g, r + 1) if r < 7 else (jnp.minimum(g + 1, last), 0)
            here, there = (r % 2) * halves, ((r + 1) % 2) * halves
            acc = None
            for half in range(halves):
                product(after_g, after_r, half, buffers[there + half])
                part = terms(g, r, half, buffers[here + half])
                acc = part if acc is None else acc + part
            total = jnp.sum(acc, axis=1, keepdims=True)
            outs.append(jnp.sum(jnp.where(eye, total, 0.0), axis=0, keepdims=True))
        out_ref[pl.ds(pl.multiple_of((g - start) * 8, 8), 8), :] = jnp.concatenate(outs, axis=0)
        return carry

    lax.fori_loop(0, count, group, 0)


def far_kernel(*refs, blocks, fanin, pieces):
    code_ref, cnt_ref, ops_ref, eval_ref, mine_ref, other_ref = refs[:6]
    near_refs = refs[6 : 6 + pieces]
    pay_refs = refs[6 + pieces : -2]
    out_ref, sums = refs[-2:]
    width = mine_ref.shape[1]
    boxes = mine_ref.shape[0] // (blocks // 2)
    patterns = ops_ref.shape[0] // width
    per = LANES // fanin
    tiles = code_ref.shape[0]
    span = 2 * boxes
    pages = blocks // 2
    table = jnp.concatenate(
        [
            jnp.concatenate(
                [mine_ref[j * boxes : (j + 1) * boxes], other_ref[j * boxes : (j + 1) * boxes]], axis=0
            )
            for j in range(pages)
        ],
        axis=1,
    )
    codes = code_ref[...]
    cols = code_columns(codes)
    eye = iota((per, LANES), 0) == (iota((per, LANES), 1) >> log2(fanin))
    batch = 4
    for base in range(0, tiles, batch):
        picks = [
            jnp.broadcast_to(cols[:, i : i + 1], (LANES, LANES)) for i in range(base, base + batch)
        ]
        wide = dot(jnp.concatenate([onehot(c & (span - 1), span) for c in picks], axis=0), table)
        for n in range(batch):
            i = base + n
            page = (picks[n] >> log2(span)) & (pages - 1)
            part = wide[n * LANES : (n + 1) * LANES]
            got = part[:, 0:width]
            for j in range(1, pages):
                got = jnp.where(page == j, part[:, j * width : (j + 1) * width], got)
            pat = pattern_matrix(codes[i : i + 1, :] >> log2(blocks * boxes), eye, patterns)
            s = dot(pat, got.astype(BF16)).astype(BF16)
            for p in range(patterns):
                sums[i * per : (i + 1) * per, p * width : (p + 1) * width] = s[
                    p * per : (p + 1) * per
                ]
    near_local = dot(sums[...], ops_ref[...])
    hits = []
    values = []
    for pay in pay_refs:
        depth = pay.shape[0] - 16
        target = pay[depth : depth + 16, :].astype(F32)[0:1]
        box = iota((boxes, depth), 0).astype(F32)
        hits.append(jnp.where(box == target, 1.0, 0.0).astype(BF16))
        values.append(pay[0:depth, :])
    local = near_local + dot(jnp.concatenate(hits, axis=1), jnp.concatenate(values, axis=0))
    far = dot(local.astype(BF16), eval_ref[...])
    near = jnp.concatenate([ref[...] for ref in near_refs], axis=0)
    total = near * (1.0 / (4.0 * math.pi)) + far
    live = iota((boxes, LANES), 1) < count_columns(cnt_ref, boxes)
    out_ref[...] = jnp.where(live, total, 0.0)


VMEM = pl.BlockSpec(memory_space=pltpu.VMEM)
SMEM = pl.BlockSpec(memory_space=pltpu.SMEM)
MIB = 1024 * 1024
PIECES = 4


def body(
    n_oct,
    n_cube,
    charges,
    panel_counts,
    positions,
    moment_map,
    translations,
    evaluation,
    near_boxes,
    group_sources,
    group_patterns,
    remote_sources,
    remote_patterns,
    remote_targets,
):
    boxes, panels = charges.shape
    width = moment_map.shape[1]
    patterns = translations.shape[0]
    operators = translations.reshape(patterns * width, width)
    counts = panel_counts.reshape(boxes // LANES, LANES)
    slot_index = jnp.arange(panels, dtype=jnp.int32)
    live = slot_index[None, :] < panel_counts[:, None]
    strength = jnp.where(live, charges, jnp.zeros_like(charges))
    multipole = jnp.dot(strength, moment_map, preferred_element_type=F32).astype(BF16)

    me = lax.axis_index("cube")
    octant = lax.axis_index("oct")

    def over_cube(value, k):
        return lax.ppermute(value, "cube", [(i, i ^ k) for i in range(n_cube)])

    def over_oct(value, k):
        return lax.ppermute(value, "oct", [(i, i ^ k) for i in range(n_oct)])

    def after(value, *earlier):
        return lax.optimization_barrier((value, *earlier))[0]

    steps = list(range(2, n_cube, 2))
    tables = pl.pallas_call(
        table_kernel,
        out_shape=(
            jax.ShapeDtypeStruct((2, boxes, panels), F32),
            jax.ShapeDtypeStruct((boxes, 48, panels), BF16),
            jax.ShapeDtypeStruct((boxes // 8, panels, LANES), BF16),
        ),
        in_specs=[VMEM] * 3,
        out_specs=(VMEM,) * 3,
        scratch_shapes=[pltpu.VMEM((6, boxes, panels), F32)],
        compiler_params=pltpu.CompilerParams(vmem_limit_bytes=10 * MIB),
        cost_estimate=pl.CostEstimate(
            flops=1_000_000_000, bytes_accessed=1_000_000, transcendentals=0
        ),
        name="tables",
    )(counts, charges, positions)

    neighbours = near_boxes.T
    size = boxes // PIECES

    def near_piece(i, tables):
        return pl.pallas_call(
            functools.partial(near_kernel, start=i * size // 8),
            out_shape=jax.ShapeDtypeStruct((size, panels), F32),
            in_specs=[SMEM, VMEM, VMEM, VMEM],
            out_specs=VMEM,
            scratch_shapes=[pltpu.VMEM((panels, 2 * LANES), F32)] * near_boxes.shape[1],
            compiler_params=pltpu.CompilerParams(vmem_limit_bytes=8 * MIB),
            cost_estimate=pl.CostEstimate(
                flops=4_000_000_000, bytes_accessed=1_000_000, transcendentals=4_000_000
            ),
            name="near",
        )(neighbours, *tables)

    first, *rest = steps
    along = {0: multipole, first: over_cube(multipole, first)}
    held = after(multipole, *tables)
    for k in rest[: (len(rest) + 1) // 2]:
        along[k] = over_cube(held, k)
    near = [near_piece(0, tables)]
    held = after(multipole, near[0])
    for k in rest[(len(rest) + 1) // 2 :]:
        along[k] = over_cube(held, k)

    slots, fanin = remote_sources.shape[3:]
    sent = pl.pallas_call(
        slot_kernel,
        out_shape=jax.ShapeDtypeStruct((n_oct, 2 * slots + 16, width), BF16),
        in_specs=[VMEM] * 5,
        out_specs=VMEM,
        scratch_shapes=[pltpu.VMEM((n_oct * slots, patterns * width), BF16)],
        compiler_params=pltpu.CompilerParams(vmem_limit_bytes=8 * MIB),
        cost_estimate=pl.CostEstimate(
            flops=1_000_000_000, bytes_accessed=1_000_000, transcendentals=0
        ),
        name="slots",
    )(
        held,
        remote_sources[0, 0].transpose(0, 2, 1),
        remote_patterns[0, 0].transpose(0, 2, 1),
        remote_targets[0, 0],
        operators,
    )
    parts = [
        lax.dynamic_index_in_dim(sent, octant ^ k, 0, keepdims=False) for k in range(n_oct)
    ]
    third = -(-(n_oct - 1) // 3)
    got = {0: parts[0]}
    for k in range(1, min(1 + third, n_oct)):
        got[k] = over_oct(parts[k], k)
    tables = lax.optimization_barrier((*tables, sent, near[0]))[:3]
    near.append(near_piece(1, tables))

    held = lax.optimization_barrier((*[along[k] for k in sorted(along)], near[1]))[:-1]
    mine = jnp.concatenate(held, axis=0)
    other = over_cube(mine, 1)
    for k in range(1 + third, min(1 + 2 * third, n_oct)):
        got[k] = over_oct(after(parts[k], near[1]), k)
    tables = lax.optimization_barrier((*tables, mine))[:3]
    near.append(near_piece(2, tables))
    for k in range(1 + 2 * third, n_oct):
        got[k] = over_oct(after(parts[k], near[2]), k)
    tables = lax.optimization_barrier((*tables, near[2]))[:3]
    near.append(near_piece(3, tables))
    other, *payloads, last = lax.optimization_barrier(
        (other, *[got[k] for k in range(n_oct)], near[3])
    )
    near[3] = last

    klist = group_sources.shape[1]
    group = n_cube * boxes
    code = (group_sources ^ (me * boxes)) + group * group_patterns
    return pl.pallas_call(
        functools.partial(far_kernel, blocks=n_cube, fanin=klist, pieces=PIECES),
        out_shape=jax.ShapeDtypeStruct((boxes, panels), F32),
        in_specs=[VMEM] * (6 + PIECES + n_oct),
        out_specs=VMEM,
        scratch_shapes=[pltpu.VMEM((boxes, patterns * width), BF16)],
        compiler_params=pltpu.CompilerParams(vmem_limit_bytes=10 * MIB),
        cost_estimate=pl.CostEstimate(
            flops=3_000_000_000, bytes_accessed=2_000_000, transcendentals=0
        ),
        name="far",
    )(code.reshape(-1, LANES), counts, operators, evaluation, mine, other, *near, *payloads)


def solution(mesh):
    n_oct = mesh.shape["oct"]
    n_cube = mesh.shape["cube"]

    def run(*arrays):
        return body(n_oct, n_cube, *arrays)

    return jax.shard_map(
        run,
        mesh=mesh,
        in_specs=(
            P(("oct", "cube"), None),
            P(("oct", "cube")),
            P(None, ("oct", "cube"), None),
            P(),
            P(),
            P(),
            P(("oct", "cube"), None),
            P(("oct", "cube"), None),
            P(("oct", "cube"), None),
            P("oct", "cube", None, None, None),
            P("oct", "cube", None, None, None),
            P("oct", "cube", None, None),
        ),
        out_specs=P(("oct", "cube"), None),
        check_vma=False,
    )
```

```python
import functools
import math

import jax
import jax.numpy as jnp
from jax import lax
from jax.experimental import pallas as pl
from jax.experimental.pallas import tpu as pltpu
from jax.sharding import PartitionSpec as P

F32 = jnp.float32
BF16 = jnp.bfloat16
LANES = 128
EPS = 0.0025


def iota(shape, dim):
    return lax.broadcasted_iota(jnp.int32, shape, dim)


def count_columns(cnt_ref, boxes):
    eye = iota((LANES, LANES), 0) == iota((LANES, LANES), 1)
    cols = [
        jnp.sum(jnp.where(eye, cnt_ref[i : i + 1, :], 0), axis=1, keepdims=True)
        for i in range(boxes // LANES)
    ]
    return jnp.concatenate(cols, axis=0)


def log2(value):
    return value.bit_length() - 1


def code_columns(codes):
    rows = codes.shape[0]
    padded = jnp.concatenate([codes, jnp.zeros((LANES - rows, LANES), codes.dtype)], axis=0)
    return padded.T


def onehot(local, width):
    lane = iota((LANES, LANES), 1)
    parts = [
        jnp.where(local == lane + LANES * i, 1.0, 0.0).astype(BF16) for i in range(width // LANES)
    ]
    return jnp.concatenate(parts, axis=1)


def pattern_matrix(pattern_row, eye, patterns):
    own = jnp.where(eye, jnp.broadcast_to(pattern_row, eye.shape), -1)
    parts = [jnp.where(own == p, 1.0, 0.0).astype(BF16) for p in range(patterns)]
    return jnp.concatenate(parts, axis=0)


def dot(a, b):
    return jnp.dot(a, b, preferred_element_type=F32)


def slot_kernel(m_ref, src_ref, pat_ref, tgt_ref, ops_ref, out_ref, sums):
    boxes, width = m_ref.shape
    patterns = ops_ref.shape[0] // width
    groups, fanin, slots = src_ref.shape
    rows = out_ref.shape[1]
    pack = LANES // slots
    tiles = fanin // pack
    m = m_ref[...]

    def packed(ref, d, h):
        return jnp.concatenate([ref[d, h * pack + i : h * pack + i + 1, :] for i in range(pack)], axis=1)

    sources = [packed(src_ref, d, h) for d in range(groups) for h in range(tiles)]
    cols = code_columns(jnp.concatenate(sources, axis=0))
    eye = iota((slots, LANES), 0) == (iota((slots, LANES), 1) & (slots - 1))
    for d in range(groups):
        ones = []
        pats = []
        for h in range(tiles):
            i = d * tiles + h
            ones.append(onehot(jnp.broadcast_to(cols[:, i : i + 1], (LANES, LANES)), boxes))
            pats.append(pattern_matrix(packed(pat_ref, d, h), eye, patterns))
        got = dot(jnp.concatenate(ones, axis=0), m).astype(BF16)
        s = dot(jnp.concatenate(pats, axis=1), got).astype(BF16)
        for p in range(patterns):
            sums[d * slots : (d + 1) * slots, p * width : (p + 1) * width] = s[
                p * slots : (p + 1) * slots
            ]
    result = dot(sums[...], ops_ref[...])
    hi = result.astype(BF16)
    lo = (result - hi.astype(F32)).astype(BF16)
    for d in range(groups):
        target = tgt_ref[d : d + 1, :].astype(F32)
        out_ref[d, 0:slots, :] = hi[d * slots : (d + 1) * slots]
        out_ref[d, slots : 2 * slots, :] = lo[d * slots : (d + 1) * slots]
        out_ref[d, 2 * slots : rows, :] = jnp.broadcast_to(
            jnp.concatenate([target, target], axis=1), (rows - 2 * slots, 2 * slots)
        ).astype(BF16)


def plan_kernel(
    nb_ref, cnt_ref, chg_ref, pos_ref, plan_ref, rows_ref, coords_ref, left_ref, ranked
):
    boxes = chg_ref.shape[0]
    column = count_columns(cnt_ref, boxes)
    row = jnp.concatenate([cnt_ref[i : i + 1, :] for i in range(boxes // LANES)], axis=1)
    rows_ref[1] = jnp.where(iota((boxes, LANES), 1) < column, chg_ref[...].astype(F32), 0.0)

    down, across = iota((boxes, boxes), 0), iota((boxes, boxes), 1)
    ahead = (column < row) | ((column == row) & (down < across))
    rank_row = jnp.sum(jnp.where(ahead, 1.0, 0.0), axis=0, keepdims=True)
    behind = (row < column) | ((row == column) & (across < down))
    rank_column = jnp.sum(jnp.where(behind, 1.0, 0.0), axis=1, keepdims=True)
    to_rank = jnp.where(rank_row == down.astype(F32), 1.0, 0.0).astype(BF16)
    from_rank = jnp.where(rank_column == across.astype(F32), 1.0, 0.0).astype(BF16)

    lists = jnp.concatenate(
        [
            nb_ref[...].astype(F32),
            row.astype(F32),
            across[0:1].astype(F32),
            jnp.zeros((16 - 2 - nb_ref.shape[0], boxes), F32),
        ],
        axis=0,
    )
    plan = dot(lists.astype(BF16), from_rank)[0:8].astype(jnp.int32)
    within = jnp.where(column <= STEP * across, 1.0, 0.0)
    ends = jnp.sum(within, axis=0, keepdims=True).astype(jnp.int32) >> log2(TEAM)
    plan_ref[...] = jnp.where(iota((8, boxes), 0) == nb_ref.shape[0] + 2, ends, plan)

    norm = jnp.zeros((boxes, LANES), F32)
    parts = []
    for c in range(3):
        u = pos_ref[c] - 1.0
        h = u.astype(BF16).astype(F32)
        m = (u - h).astype(BF16).astype(F32)
        coords_ref[2 * c] = h
        coords_ref[2 * c + 1] = m
        parts += [-2.0 * h, -2.0 * m]
        v = h + m
        norm = norm + v * v
    rows_ref[0] = norm
    n = norm + EPS
    n1 = n.astype(BF16).astype(F32)
    n2 = (n - n1).astype(BF16).astype(F32)
    parts += [n1, n2, n - n1 - n2]
    ranked[...] = dot(to_rank, jnp.concatenate([p.astype(BF16) for p in parts], axis=1))

    def build(g, carry):
        rows = pl.ds(pl.multiple_of(g * 8, 8), 8)
        f = [ranked[rows, i * LANES : (i + 1) * LANES] for i in range(9)]
        stack = []
        for c in range(3):
            stack += [f[2 * c], f[2 * c], f[2 * c + 1], f[2 * c + 1]]
        stack += f[6:9] + [jnp.zeros((8, LANES), F32)]
        left_ref[g] = jnp.concatenate(stack, axis=0).T.astype(BF16)
        return carry

    lax.fori_loop(0, boxes // 8, build, 0, unroll=4)


def near_kernel(plan_ref, rows_ref, coords_ref, left_ref, out_ref, right, *, start, stop):
    boxes = out_ref.shape[0]
    knear = 4
    out_ref[...] = jnp.zeros_like(out_ref)

    def build(g, carry):
        rows = pl.ds(pl.multiple_of(g * 8, 8), 8)
        tile = [coords_ref[f, rows, :] for f in range(6)]
        for r in range(8):
            for c in range(3):
                h = jnp.broadcast_to(tile[2 * c][r : r + 1], (8, LANES))
                m = jnp.broadcast_to(tile[2 * c + 1][r : r + 1], (8, LANES))
                right[g * 8 + r, 16 * c : 16 * c + 16, :] = jnp.concatenate(
                    [h, m], axis=0
                ).astype(BF16)
        return carry

    lax.fori_loop(0, boxes // 8, build, 0, unroll=4)

    ones = jnp.where(iota((32, LANES), 0) < 24, 1.0, 0.0).astype(BF16)

    def operand(box):
        x, y, z = [right[box, 16 * c : 16 * c + 16, :] for c in range(3)]
        return jnp.concatenate([x, x, y, y, z, z, ones], axis=0)

    def team(depth, g, carry):
        masks = [
            jnp.where((iota((depth, LANES), 1) & 7) == j, 1.0, 0.0).astype(BF16) for j in range(8)
        ]
        eye = iota((depth, LANES), 0) == iota((depth, LANES), 1)
        for e in range(TEAM // 8):
            turned = left_ref[g * (TEAM // 8) + e, 0:depth, :]
            for r in range(8):
                place = g * TEAM + e * 8 + r
                lhs = turned * masks[r]
                acc = None
                for k in range(0, knear, 2):
                    pair = [plan_ref[k + i, place] for i in range(2)]
                    dist = dot(lhs, jnp.concatenate([operand(b) for b in pair], axis=1))
                    for i in range(2):
                        shift = rows_ref[0, pl.ds(pair[i], 1), :]
                        q = rows_ref[1, pl.ds(pair[i], 1), :]
                        term = lax.rsqrt(dist[:, i * LANES : (i + 1) * LANES] + shift) * q
                        acc = term if acc is None else acc + term
                total = jnp.sum(acc, axis=1, keepdims=True)
                out_ref[pl.ds(plan_ref[knear + 1, place], 1), :] = jnp.sum(
                    jnp.where(eye, total, 0.0), axis=0, keepdims=True
                )
        return carry

    done = start
    for step in range(1, LANES // STEP + 1):
        until = jnp.clip(plan_ref[knear + 2, step], done, stop)
        lax.fori_loop(done, until, functools.partial(team, step * STEP), 0)
        done = until


def far_kernel(*refs, blocks, fanin, pieces):
    code_ref, cnt_ref, ops_ref, eval_ref, mine_ref, other_ref = refs[:6]
    near_refs = refs[6 : 6 + pieces]
    pay_refs = refs[6 + pieces : -2]
    out_ref, sums = refs[-2:]
    width = mine_ref.shape[1]
    boxes = mine_ref.shape[0] // (blocks // 2)
    patterns = ops_ref.shape[0] // width
    per = LANES // fanin
    tiles = code_ref.shape[0]
    span = 2 * boxes
    pages = blocks // 2
    table = jnp.concatenate(
        [
            jnp.concatenate(
                [mine_ref[j * boxes : (j + 1) * boxes], other_ref[j * boxes : (j + 1) * boxes]], axis=0
            )
            for j in range(pages)
        ],
        axis=1,
    )
    codes = code_ref[...]
    cols = code_columns(codes)
    eye = iota((per, LANES), 0) == (iota((per, LANES), 1) >> log2(fanin))
    batch = 4
    for base in range(0, tiles, batch):
        picks = [
            jnp.broadcast_to(cols[:, i : i + 1], (LANES, LANES)) for i in range(base, base + batch)
        ]
        wide = dot(jnp.concatenate([onehot(c & (span - 1), span) for c in picks], axis=0), table)
        for n in range(batch):
            i = base + n
            page = (picks[n] >> log2(span)) & (pages - 1)
            part = wide[n * LANES : (n + 1) * LANES]
            got = part[:, 0:width]
            for j in range(1, pages):
                got = jnp.where(page == j, part[:, j * width : (j + 1) * width], got)
            pat = pattern_matrix(codes[i : i + 1, :] >> log2(blocks * boxes), eye, patterns)
            s = dot(pat, got.astype(BF16)).astype(BF16)
            for p in range(patterns):
                sums[i * per : (i + 1) * per, p * width : (p + 1) * width] = s[
                    p * per : (p + 1) * per
                ]
    near_local = dot(sums[...], ops_ref[...])
    hits = []
    values = []
    for pay in pay_refs:
        depth = pay.shape[0] - 16
        target = pay[depth : depth + 16, :].astype(F32)[0:1]
        box = iota((boxes, depth), 0).astype(F32)
        hits.append(jnp.where(box == target, 1.0, 0.0).astype(BF16))
        values.append(pay[0:depth, :])
    local = near_local + dot(jnp.concatenate(hits, axis=1), jnp.concatenate(values, axis=0))
    far = dot(local.astype(BF16), eval_ref[...])
    near = near_refs[0][...]
    for ref in near_refs[1:]:
        near = near + ref[...]
    total = near * (1.0 / (4.0 * math.pi)) + far
    live = iota((boxes, LANES), 1) < count_columns(cnt_ref, boxes)
    out_ref[...] = jnp.where(live, total, 0.0)


VMEM = pl.BlockSpec(memory_space=pltpu.VMEM)
SMEM = pl.BlockSpec(memory_space=pltpu.SMEM)
MIB = 1024 * 1024
PIECES = 2
TEAM = 16
STEP = 16


def body(
    n_oct,
    n_cube,
    charges,
    panel_counts,
    positions,
    moment_map,
    translations,
    evaluation,
    near_boxes,
    group_sources,
    group_patterns,
    remote_sources,
    remote_patterns,
    remote_targets,
):
    boxes, panels = charges.shape
    width = moment_map.shape[1]
    patterns = translations.shape[0]
    operators = translations.reshape(patterns * width, width)
    counts = panel_counts.reshape(boxes // LANES, LANES)
    slot_index = jnp.arange(panels, dtype=jnp.int32)
    live = slot_index[None, :] < panel_counts[:, None]
    strength = jnp.where(live, charges, jnp.zeros_like(charges))
    multipole = jnp.dot(strength, moment_map, preferred_element_type=F32).astype(BF16)

    me = lax.axis_index("cube")
    octant = lax.axis_index("oct")

    def over_cube(value, k):
        return lax.ppermute(value, "cube", [(i, i ^ k) for i in range(n_cube)])

    def over_oct(value, k):
        return lax.ppermute(value, "oct", [(i, i ^ k) for i in range(n_oct)])

    def after(value, *earlier):
        return lax.optimization_barrier((value, *earlier))[0]

    plan, *tables = pl.pallas_call(
        plan_kernel,
        out_shape=(
            jax.ShapeDtypeStruct((8, boxes), jnp.int32),
            jax.ShapeDtypeStruct((2, boxes, panels), F32),
            jax.ShapeDtypeStruct((6, boxes, panels), F32),
            jax.ShapeDtypeStruct((boxes // 8, panels, LANES), BF16),
        ),
        in_specs=[VMEM] * 4,
        out_specs=(VMEM,) * 4,
        scratch_shapes=[pltpu.VMEM((boxes, 9 * LANES), F32)],
        compiler_params=pltpu.CompilerParams(vmem_limit_bytes=12 * MIB),
        cost_estimate=pl.CostEstimate(
            flops=1_000_000_000, bytes_accessed=1_000_000, transcendentals=0
        ),
        name="plan",
    )(near_boxes.T, counts, charges, positions)

    teams = boxes // TEAM
    cut = teams * 5 // 8

    def near_piece(start, stop, tables):
        return pl.pallas_call(
            functools.partial(near_kernel, start=start, stop=stop),
            out_shape=jax.ShapeDtypeStruct((boxes, panels), F32),
            in_specs=[SMEM, VMEM, VMEM, VMEM],
            out_specs=VMEM,
            scratch_shapes=[pltpu.VMEM((boxes, 48, panels), BF16)],
            compiler_params=pltpu.CompilerParams(vmem_limit_bytes=12 * MIB),
            cost_estimate=pl.CostEstimate(
                flops=200_000_000, bytes_accessed=1_000_000, transcendentals=0
            ),
            name="near",
        )(plan, *tables)

    slots, fanin = remote_sources.shape[3:]
    sent = pl.pallas_call(
        slot_kernel,
        out_shape=jax.ShapeDtypeStruct((n_oct, 2 * slots + 16, width), BF16),
        in_specs=[VMEM] * 5,
        out_specs=VMEM,
        scratch_shapes=[pltpu.VMEM((n_oct * slots, patterns * width), BF16)],
        compiler_params=pltpu.CompilerParams(vmem_limit_bytes=8 * MIB),
        cost_estimate=pl.CostEstimate(
            flops=1_000_000_000, bytes_accessed=1_000_000, transcendentals=0
        ),
        name="slots",
    )(
        multipole,
        remote_sources[0, 0].transpose(0, 2, 1),
        remote_patterns[0, 0].transpose(0, 2, 1),
        remote_targets[0, 0],
        operators,
    )
    box = {k: lax.dynamic_index_in_dim(sent, octant ^ k, 0, keepdims=False) for k in range(n_oct)}

    def oct_step(bit):
        moving = [k for k in range(n_oct) if k & bit]
        load = jnp.concatenate([box[k] for k in moving], axis=0)
        return load, over_oct(load, bit)

    def unpack(bit, came):
        moving = [k for k in range(n_oct) if k & bit]
        rows = came.shape[0] // len(moving)
        for i, k in enumerate(moving):
            box[k] = came[i * rows : (i + 1) * rows]

    def cube_step(bit, mine):
        return jnp.concatenate([mine, over_cube(mine, bit)], axis=0)

    oct_bits = [1 << i for i in range(log2(n_oct))]
    cube_bits = [1 << i for i in range(1, log2(n_cube))]
    mine = cube_step(cube_bits[0], multipole)
    mine = after(mine, plan, sent)
    anchor = [mine]
    for bit in oct_bits[:-1]:
        load, came = oct_step(bit)
        unpack(bit, came)
        anchor.append(load)
    for bit in cube_bits[1:]:
        mine = cube_step(bit, mine)
    tables = lax.optimization_barrier((*tables, *anchor))[: len(tables)]
    first = near_piece(0, cut, tables)

    mine = after(mine, first)
    other = over_cube(mine, 1)
    for k in range(n_oct):
        box[k] = after(box[k], first) if k > 0 else box[k]
    load, came = oct_step(oct_bits[-1])
    tables = lax.optimization_barrier((*tables, mine, load))[: len(tables)]
    second = near_piece(cut, teams, tables)
    other, second, came = lax.optimization_barrier((other, second, came))
    unpack(oct_bits[-1], came)
    payloads = [box[k] for k in range(n_oct)]
    near = [first, second]

    klist = group_sources.shape[1]
    group = n_cube * boxes
    code = (group_sources ^ (me * boxes)) + group * group_patterns
    return pl.pallas_call(
        functools.partial(far_kernel, blocks=n_cube, fanin=klist, pieces=PIECES),
        out_shape=jax.ShapeDtypeStruct((boxes, panels), F32),
        in_specs=[VMEM] * (6 + PIECES + n_oct),
        out_specs=VMEM,
        scratch_shapes=[pltpu.VMEM((boxes, patterns * width), BF16)],
        compiler_params=pltpu.CompilerParams(vmem_limit_bytes=24 * MIB),
        cost_estimate=pl.CostEstimate(
            flops=3_000_000_000, bytes_accessed=2_000_000, transcendentals=0
        ),
        name="far",
    )(code.reshape(-1, LANES), counts, operators, evaluation, mine, other, *near, *payloads)


def solution(mesh):
    n_oct = mesh.shape["oct"]
    n_cube = mesh.shape["cube"]

    def run(*arrays):
        return body(n_oct, n_cube, *arrays)

    return jax.shard_map(
        run,
        mesh=mesh,
        in_specs=(
            P(("oct", "cube"), None),
            P(("oct", "cube")),
            P(None, ("oct", "cube"), None),
            P(),
            P(),
            P(),
            P(("oct", "cube"), None),
            P(("oct", "cube"), None),
            P(("oct", "cube"), None),
            P("oct", "cube", None, None, None),
            P("oct", "cube", None, None, None),
            P("oct", "cube", None, None),
        ),
        out_specs=P(("oct", "cube"), None),
        check_vma=False,
    )
```

```python
import functools
import math

import jax
import jax.numpy as jnp
from jax import lax
from jax.experimental import pallas as pl
from jax.experimental.pallas import tpu as pltpu
from jax.sharding import PartitionSpec as P

F32 = jnp.float32
BF16 = jnp.bfloat16
LANES = 128
EPS = 0.0025


def iota(shape, dim):
    return lax.broadcasted_iota(jnp.int32, shape, dim)


def count_columns(cnt_ref, boxes):
    eye = iota((LANES, LANES), 0) == iota((LANES, LANES), 1)
    cols = [
        jnp.sum(jnp.where(eye, cnt_ref[i : i + 1, :], 0), axis=1, keepdims=True)
        for i in range(boxes // LANES)
    ]
    return jnp.concatenate(cols, axis=0)


def log2(value):
    return value.bit_length() - 1


def code_columns(codes):
    rows = codes.shape[0]
    padded = jnp.concatenate([codes, jnp.zeros((LANES - rows, LANES), codes.dtype)], axis=0)
    return padded.T


def onehot(local, width):
    lane = iota((LANES, LANES), 1)
    parts = [
        jnp.where(local == lane + LANES * i, 1.0, 0.0).astype(BF16) for i in range(width // LANES)
    ]
    return jnp.concatenate(parts, axis=1)


def pattern_matrix(pattern_row, eye, patterns):
    own = jnp.where(eye, jnp.broadcast_to(pattern_row, eye.shape), -1)
    parts = [jnp.where(own == p, 1.0, 0.0).astype(BF16) for p in range(patterns)]
    return jnp.concatenate(parts, axis=0)


def dot(a, b):
    return jnp.dot(a, b, preferred_element_type=F32)


def front_kernel(*refs):
    strength_ref, count_ref, out_ref = refs[3:6]
    chg_ref, cnt_ref, map_ref = refs[6:9]
    for copy in fetch(refs[:3], refs[6:9], refs[9]):
        copy.wait()
    boxes = chg_ref.shape[0]
    live = iota((boxes, LANES), 1) < count_columns(cnt_ref, boxes)
    strength = jnp.where(live, chg_ref[...].astype(F32), 0.0)
    strength_ref[...] = strength
    count_ref[...] = cnt_ref[...]
    out_ref[...] = dot(strength.astype(BF16), map_ref[...]).astype(BF16)


def fetch(sources, targets, sems):
    copies = [
        pltpu.make_async_copy(s, t, sems.at[i]) for i, (s, t) in enumerate(zip(sources, targets))
    ]
    for copy in copies:
        copy.start()
    return copies


def slot_stage(m_ref, src_ref, pat_ref, tgt_ref, ops_ref, out_ref, sums, operators_here):
    boxes, width = m_ref.shape
    patterns = ops_ref.shape[0] // width
    groups, fanin, slots = src_ref.shape
    rows = out_ref.shape[1]
    pack = LANES // slots
    tiles = fanin // pack
    m = m_ref[...]

    def packed(ref, d, h):
        return jnp.concatenate([ref[d, h * pack + i : h * pack + i + 1, :] for i in range(pack)], axis=1)

    sources = [packed(src_ref, d, h) for d in range(groups) for h in range(tiles)]
    cols = code_columns(jnp.concatenate(sources, axis=0))
    eye = iota((slots, LANES), 0) == (iota((slots, LANES), 1) & (slots - 1))
    for d in range(groups):
        ones = []
        pats = []
        for h in range(tiles):
            i = d * tiles + h
            ones.append(onehot(jnp.broadcast_to(cols[:, i : i + 1], (LANES, LANES)), boxes))
            pats.append(pattern_matrix(packed(pat_ref, d, h), eye, patterns))
        got = dot(jnp.concatenate(ones, axis=0), m).astype(BF16)
        s = dot(jnp.concatenate(pats, axis=1), got).astype(BF16)
        for p in range(patterns):
            sums[d * slots : (d + 1) * slots, p * width : (p + 1) * width] = s[
                p * slots : (p + 1) * slots
            ]
    operators_here.wait()
    result = dot(sums[...], ops_ref[...])
    hi = result.astype(BF16)
    lo = (result - hi.astype(F32)).astype(BF16)
    for d in range(groups):
        target = tgt_ref[d : d + 1, :].astype(F32)
        out_ref[d, 0:slots, :] = hi[d * slots : (d + 1) * slots]
        out_ref[d, slots : 2 * slots, :] = lo[d * slots : (d + 1) * slots]
        out_ref[d, 2 * slots : rows, :] = jnp.broadcast_to(
            jnp.concatenate([target, target], axis=1), (rows - 2 * slots, 2 * slots)
        ).astype(BF16)


def plan_kernel(*refs):
    cnt_ref, strength_ref, m_ref = refs[:3]
    plan_ref, rows_ref, coords_ref, left_ref, sent_ref = refs[9:14]
    ranked, sums = refs[14:16]
    here = refs[16:22]
    nb_ref, pos_ref, src_ref, pat_ref, tgt_ref, ops_ref = here
    copies = fetch(refs[3:9], here, refs[22])
    boxes = strength_ref.shape[0]
    column = count_columns(cnt_ref, boxes)
    row = jnp.concatenate([cnt_ref[i : i + 1, :] for i in range(boxes // LANES)], axis=1)
    rows_ref[1] = strength_ref[...]

    down, across = iota((boxes, boxes), 0), iota((boxes, boxes), 1)
    ahead = (column < row) | ((column == row) & (down < across))
    rank_row = jnp.sum(jnp.where(ahead, 1.0, 0.0), axis=0, keepdims=True)
    behind = (row < column) | ((row == column) & (across < down))
    rank_column = jnp.sum(jnp.where(behind, 1.0, 0.0), axis=1, keepdims=True)
    to_rank = jnp.where(rank_row == down.astype(F32), 1.0, 0.0).astype(BF16)
    from_rank = jnp.where(rank_column == across.astype(F32), 1.0, 0.0).astype(BF16)

    copies[0].wait()
    lists = jnp.concatenate(
        [
            nb_ref[...].astype(F32),
            row.astype(F32),
            across[0:1].astype(F32),
            jnp.zeros((16 - 2 - nb_ref.shape[0], boxes), F32),
        ],
        axis=0,
    )
    plan = dot(lists.astype(BF16), from_rank)[0:8].astype(jnp.int32)
    within = jnp.where(column <= STEP * across, 1.0, 0.0)
    ends = jnp.sum(within, axis=0, keepdims=True).astype(jnp.int32) >> log2(TEAM)
    plan_ref[...] = jnp.where(iota((8, boxes), 0) == nb_ref.shape[0] + 2, ends, plan)

    copies[1].wait()
    norm = jnp.zeros((boxes, LANES), F32)
    parts = []
    for c in range(3):
        u = pos_ref[c] - 1.0
        h = u.astype(BF16).astype(F32)
        m = (u - h).astype(BF16).astype(F32)
        coords_ref[2 * c] = h
        coords_ref[2 * c + 1] = m
        parts += [-2.0 * h, -2.0 * m]
        v = h + m
        norm = norm + v * v
    rows_ref[0] = norm
    n = norm + EPS
    n1 = n.astype(BF16).astype(F32)
    n2 = (n - n1).astype(BF16).astype(F32)
    parts += [n1, n2, n - n1 - n2]
    ranked[...] = dot(to_rank, jnp.concatenate([p.astype(BF16) for p in parts], axis=1))

    def build(g, carry):
        rows = pl.ds(pl.multiple_of(g * 8, 8), 8)
        f = [ranked[rows, i * LANES : (i + 1) * LANES] for i in range(9)]
        stack = []
        for c in range(3):
            stack += [f[2 * c], f[2 * c], f[2 * c + 1], f[2 * c + 1]]
        stack += f[6:9] + [jnp.zeros((8, LANES), F32)]
        left_ref[g] = jnp.concatenate(stack, axis=0).T.astype(BF16)
        return carry

    lax.fori_loop(0, boxes // 8, build, 0, unroll=4)
    for copy in copies[2:5]:
        copy.wait()
    slot_stage(m_ref, src_ref, pat_ref, tgt_ref, ops_ref, sent_ref, sums, copies[5])


def near_kernel(plan_ref, rows_ref, coords_ref, left_ref, out_ref, right, *, start, stop):
    boxes = out_ref.shape[0]
    knear = 4
    out_ref[...] = jnp.zeros_like(out_ref)

    def build(g, carry):
        rows = pl.ds(pl.multiple_of(g * 8, 8), 8)
        tile = [coords_ref[f, rows, :] for f in range(6)]
        for r in range(8):
            for c in range(3):
                h = jnp.broadcast_to(tile[2 * c][r : r + 1], (8, LANES))
                m = jnp.broadcast_to(tile[2 * c + 1][r : r + 1], (8, LANES))
                right[g * 8 + r, 16 * c : 16 * c + 16, :] = jnp.concatenate(
                    [h, m], axis=0
                ).astype(BF16)
        return carry

    lax.fori_loop(0, boxes // 8, build, 0, unroll=4)

    ones = jnp.where(iota((32, LANES), 0) < 24, 1.0, 0.0).astype(BF16)

    def operand(box):
        x, y, z = [right[box, 16 * c : 16 * c + 16, :] for c in range(3)]
        return jnp.concatenate([x, x, y, y, z, z, ones], axis=0)

    def team(depth, g, carry):
        masks = [
            jnp.where((iota((depth, LANES), 1) & 7) == j, 1.0, 0.0).astype(BF16) for j in range(8)
        ]
        eye = iota((depth, LANES), 0) == iota((depth, LANES), 1)
        for e in range(TEAM // 8):
            turned = left_ref[g * (TEAM // 8) + e, 0:depth, :]
            for r in range(8):
                place = g * TEAM + e * 8 + r
                lhs = turned * masks[r]
                acc = None
                for k in range(0, knear, 2):
                    pair = [plan_ref[k + i, place] for i in range(2)]
                    dist = dot(lhs, jnp.concatenate([operand(b) for b in pair], axis=1))
                    for i in range(2):
                        shift = rows_ref[0, pl.ds(pair[i], 1), :]
                        q = rows_ref[1, pl.ds(pair[i], 1), :]
                        term = lax.rsqrt(dist[:, i * LANES : (i + 1) * LANES] + shift) * q
                        acc = term if acc is None else acc + term
                total = jnp.sum(acc, axis=1, keepdims=True)
                out_ref[pl.ds(plan_ref[knear + 1, place], 1), :] = jnp.sum(
                    jnp.where(eye, total, 0.0), axis=0, keepdims=True
                )
        return carry

    done = start
    for step in range(1, LANES // STEP + 1):
        until = jnp.clip(plan_ref[knear + 2, step], done, stop)
        lax.fori_loop(done, until, functools.partial(team, step * STEP), 0)
        done = until


def far_kernel(*refs, blocks, fanin, pieces):
    code_ref, cnt_ref, ops_hbm, eval_hbm, mine_ref, other_ref = refs[:6]
    near_refs = refs[6 : 6 + pieces]
    pay_refs = refs[6 + pieces : -5]
    out_ref, sums, ops_ref, eval_ref, sems = refs[-5:]
    copies = fetch((ops_hbm, eval_hbm), (ops_ref, eval_ref), sems)
    width = mine_ref.shape[1]
    boxes = mine_ref.shape[0] // (blocks // 2)
    patterns = ops_ref.shape[0] // width
    per = LANES // fanin
    tiles = code_ref.shape[0]
    span = 2 * boxes
    pages = blocks // 2
    table = jnp.concatenate(
        [
            jnp.concatenate(
                [mine_ref[j * boxes : (j + 1) * boxes], other_ref[j * boxes : (j + 1) * boxes]], axis=0
            )
            for j in range(pages)
        ],
        axis=1,
    )
    codes = code_ref[...]
    cols = code_columns(codes)
    eye = iota((per, LANES), 0) == (iota((per, LANES), 1) >> log2(fanin))
    batch = 4
    for base in range(0, tiles, batch):
        picks = [
            jnp.broadcast_to(cols[:, i : i + 1], (LANES, LANES)) for i in range(base, base + batch)
        ]
        wide = dot(jnp.concatenate([onehot(c & (span - 1), span) for c in picks], axis=0), table)
        for n in range(batch):
            i = base + n
            page = (picks[n] >> log2(span)) & (pages - 1)
            part = wide[n * LANES : (n + 1) * LANES]
            got = part[:, 0:width]
            for j in range(1, pages):
                got = jnp.where(page == j, part[:, j * width : (j + 1) * width], got)
            pat = pattern_matrix(codes[i : i + 1, :] >> log2(blocks * boxes), eye, patterns)
            s = dot(pat, got.astype(BF16)).astype(BF16)
            for p in range(patterns):
                sums[i * per : (i + 1) * per, p * width : (p + 1) * width] = s[
                    p * per : (p + 1) * per
                ]
    for copy in copies:
        copy.wait()
    near_local = dot(sums[...], ops_ref[...])
    hits = []
    values = []
    for pay in pay_refs:
        depth = pay.shape[0] - 16
        target = pay[depth : depth + 16, :].astype(F32)[0:1]
        box = iota((boxes, depth), 0).astype(F32)
        hits.append(jnp.where(box == target, 1.0, 0.0).astype(BF16))
        values.append(pay[0:depth, :])
    local = near_local + dot(jnp.concatenate(hits, axis=1), jnp.concatenate(values, axis=0))
    far = dot(local.astype(BF16), eval_ref[...])
    near = near_refs[0][...]
    for ref in near_refs[1:]:
        near = near + ref[...]
    total = near * (1.0 / (4.0 * math.pi)) + far
    live = iota((boxes, LANES), 1) < count_columns(cnt_ref, boxes)
    out_ref[...] = jnp.where(live, total, 0.0)


VMEM = pl.BlockSpec(memory_space=pltpu.VMEM)
HBM = pl.BlockSpec(memory_space=pltpu.HBM)
SMEM = pl.BlockSpec(memory_space=pltpu.SMEM)
MIB = 1024 * 1024


def in_hbm(value):
    return pltpu.with_memory_space_constraint(value, pltpu.HBM)


PIECES = 2
TEAM = 16
STEP = 16


def body(
    n_oct,
    n_cube,
    charges,
    panel_counts,
    positions,
    moment_map,
    translations,
    evaluation,
    near_boxes,
    group_sources,
    group_patterns,
    remote_sources,
    remote_patterns,
    remote_targets,
):
    boxes, panels = charges.shape
    width = moment_map.shape[1]
    patterns = translations.shape[0]
    operators = translations.reshape(patterns * width, width)
    counts = panel_counts.reshape(boxes // LANES, LANES)
    strength, counts, multipole = pl.pallas_call(
        front_kernel,
        out_shape=(
            jax.ShapeDtypeStruct((boxes, panels), F32),
            jax.ShapeDtypeStruct(counts.shape, jnp.int32),
            jax.ShapeDtypeStruct((boxes, width), BF16),
        ),
        in_specs=[HBM] * 3,
        out_specs=(VMEM,) * 3,
        scratch_shapes=[pltpu.VMEM(v.shape, v.dtype) for v in (charges, counts, moment_map)]
        + [pltpu.SemaphoreType.DMA((3,))],
        compiler_params=pltpu.CompilerParams(vmem_limit_bytes=8 * MIB),
        cost_estimate=pl.CostEstimate(
            flops=10_000_000, bytes_accessed=300_000, transcendentals=0
        ),
        name="front",
    )(in_hbm(charges), in_hbm(counts), in_hbm(moment_map))

    me = lax.axis_index("cube")
    octant = lax.axis_index("oct")

    def over_cube(value, k):
        return lax.ppermute(value, "cube", [(i, i ^ k) for i in range(n_cube)])

    def over_oct(value, k):
        return lax.ppermute(value, "oct", [(i, i ^ k) for i in range(n_oct)])

    def after(value, *earlier):
        return lax.optimization_barrier((value, *earlier))[0]

    slots, fanin = remote_sources.shape[3:]
    fetched = (
        near_boxes.T,
        positions,
        remote_sources[0, 0].transpose(0, 2, 1),
        remote_patterns[0, 0].transpose(0, 2, 1),
        remote_targets[0, 0],
        operators,
    )
    plan, *tables, sent = pl.pallas_call(
        plan_kernel,
        out_shape=(
            jax.ShapeDtypeStruct((8, boxes), jnp.int32),
            jax.ShapeDtypeStruct((2, boxes, panels), F32),
            jax.ShapeDtypeStruct((6, boxes, panels), F32),
            jax.ShapeDtypeStruct((boxes // 8, panels, LANES), BF16),
            jax.ShapeDtypeStruct((n_oct, 2 * slots + 16, width), BF16),
        ),
        in_specs=[VMEM] * 3 + [HBM] * len(fetched),
        out_specs=(VMEM,) * 5,
        scratch_shapes=[
            pltpu.VMEM((boxes, 9 * LANES), F32),
            pltpu.VMEM((n_oct * slots, patterns * width), BF16),
        ]
        + [pltpu.VMEM(v.shape, v.dtype) for v in fetched]
        + [pltpu.SemaphoreType.DMA((len(fetched),))],
        compiler_params=pltpu.CompilerParams(vmem_limit_bytes=16 * MIB),
        cost_estimate=pl.CostEstimate(
            flops=1_000_000_000, bytes_accessed=2_000_000, transcendentals=0
        ),
        name="plan",
    )(counts, strength, multipole, *map(in_hbm, fetched))

    teams = boxes // TEAM
    cut = teams * 5 // 8

    def near_piece(start, stop, tables):
        return pl.pallas_call(
            functools.partial(near_kernel, start=start, stop=stop),
            out_shape=jax.ShapeDtypeStruct((boxes, panels), F32),
            in_specs=[SMEM, VMEM, VMEM, VMEM],
            out_specs=VMEM,
            scratch_shapes=[pltpu.VMEM((boxes, 48, panels), BF16)],
            compiler_params=pltpu.CompilerParams(vmem_limit_bytes=12 * MIB),
            cost_estimate=pl.CostEstimate(
                flops=200_000_000, bytes_accessed=1_000_000, transcendentals=0
            ),
            name="near",
        )(plan, *tables)

    box = {k: lax.dynamic_index_in_dim(sent, octant ^ k, 0, keepdims=False) for k in range(n_oct)}

    def oct_step(bit):
        moving = [k for k in range(n_oct) if k & bit]
        load = jnp.concatenate([box[k] for k in moving], axis=0)
        return load, over_oct(load, bit)

    def unpack(bit, came):
        moving = [k for k in range(n_oct) if k & bit]
        rows = came.shape[0] // len(moving)
        for i, k in enumerate(moving):
            box[k] = came[i * rows : (i + 1) * rows]

    def cube_step(bit, mine):
        return jnp.concatenate([mine, over_cube(mine, bit)], axis=0)

    oct_bits = [1 << i for i in range(log2(n_oct))]
    cube_bits = [1 << i for i in range(1, log2(n_cube))]
    mine = cube_step(cube_bits[0], multipole)
    mine = after(mine, plan, sent)
    anchor = [mine]
    for bit in oct_bits[:-1]:
        load, came = oct_step(bit)
        unpack(bit, came)
        anchor.append(load)
    for bit in cube_bits[1:]:
        mine = cube_step(bit, mine)
    tables = lax.optimization_barrier((*tables, *anchor))[: len(tables)]
    first = near_piece(0, cut, tables)

    mine = after(mine, first)
    other = over_cube(mine, 1)
    for k in range(n_oct):
        box[k] = after(box[k], first) if k > 0 else box[k]
    load, came = oct_step(oct_bits[-1])
    tables = lax.optimization_barrier((*tables, mine, load))[: len(tables)]
    second = near_piece(cut, teams, tables)
    other, second, came = lax.optimization_barrier((other, second, came))
    unpack(oct_bits[-1], came)
    payloads = [box[k] for k in range(n_oct)]
    near = [first, second]

    klist = group_sources.shape[1]
    group = n_cube * boxes
    code = (group_sources ^ (me * boxes)) + group * group_patterns
    return pl.pallas_call(
        functools.partial(far_kernel, blocks=n_cube, fanin=klist, pieces=PIECES),
        out_shape=jax.ShapeDtypeStruct((boxes, panels), F32),
        in_specs=[VMEM] * 2 + [HBM] * 2 + [VMEM] * (2 + PIECES + n_oct),
        out_specs=VMEM,
        scratch_shapes=[
            pltpu.VMEM((boxes, patterns * width), BF16),
            pltpu.VMEM(operators.shape, BF16),
            pltpu.VMEM(evaluation.shape, BF16),
            pltpu.SemaphoreType.DMA((2,)),
        ],
        compiler_params=pltpu.CompilerParams(vmem_limit_bytes=24 * MIB),
        cost_estimate=pl.CostEstimate(
            flops=3_000_000_000, bytes_accessed=2_000_000, transcendentals=0
        ),
        name="far",
    )(
        code.reshape(-1, LANES),
        counts,
        in_hbm(operators),
        in_hbm(evaluation),
        mine,
        other,
        *near,
        *payloads,
    )


def solution(mesh):
    n_oct = mesh.shape["oct"]
    n_cube = mesh.shape["cube"]

    def run(*arrays):
        return body(n_oct, n_cube, *arrays)

    return jax.shard_map(
        run,
        mesh=mesh,
        in_specs=(
            P(("oct", "cube"), None),
            P(("oct", "cube")),
            P(None, ("oct", "cube"), None),
            P(),
            P(),
            P(),
            P(("oct", "cube"), None),
            P(("oct", "cube"), None),
            P(("oct", "cube"), None),
            P("oct", "cube", None, None, None),
            P("oct", "cube", None, None, None),
            P("oct", "cube", None, None),
        ),
        out_specs=P(("oct", "cube"), None),
        check_vma=False,
    )
```

```python
import functools
import math

import jax
import jax.numpy as jnp
from jax import lax
from jax.experimental import pallas as pl
from jax.experimental.pallas import tpu as pltpu
from jax.sharding import PartitionSpec as P

F32 = jnp.float32
BF16 = jnp.bfloat16
LANES = 128
EPS = 0.0025


def iota(shape, dim):
    return lax.broadcasted_iota(jnp.int32, shape, dim)


def count_columns(cnt_ref, boxes):
    eye = iota((LANES, LANES), 0) == iota((LANES, LANES), 1)
    cols = [
        jnp.sum(jnp.where(eye, cnt_ref[i : i + 1, :], 0), axis=1, keepdims=True)
        for i in range(boxes // LANES)
    ]
    return jnp.concatenate(cols, axis=0)


def log2(value):
    return value.bit_length() - 1


def code_columns(codes):
    rows = codes.shape[0]
    padded = jnp.concatenate([codes, jnp.zeros((LANES - rows, LANES), codes.dtype)], axis=0)
    return padded.T


def onehot(local, width):
    lane = iota((LANES, LANES), 1)
    parts = [
        jnp.where(local == lane + LANES * i, 1.0, 0.0).astype(BF16) for i in range(width // LANES)
    ]
    return jnp.concatenate(parts, axis=1)


def pattern_matrix(pattern_row, eye, patterns):
    own = jnp.where(eye, jnp.broadcast_to(pattern_row, eye.shape), -1)
    parts = [jnp.where(own == p, 1.0, 0.0).astype(BF16) for p in range(patterns)]
    return jnp.concatenate(parts, axis=0)


def dot(a, b):
    return jnp.dot(a, b, preferred_element_type=F32)


def front_kernel(*refs, extra):
    strength_ref, count_ref, out_ref = refs[3 + extra : 6 + extra]
    chg_ref, cnt_ref, map_ref = refs[6 + 2 * extra : 9 + 2 * extra]
    copies = fetch(
        refs[: 3 + extra],
        (chg_ref, cnt_ref, map_ref, *refs[6 + extra : 6 + 2 * extra]),
        refs[-1],
    )
    for copy in copies[:3]:
        copy.wait()
    boxes = chg_ref.shape[0]
    live = iota((boxes, LANES), 1) < count_columns(cnt_ref, boxes)
    strength = jnp.where(live, chg_ref[...].astype(F32), 0.0)
    strength_ref[...] = strength
    count_ref[...] = cnt_ref[...]
    out_ref[...] = dot(strength.astype(BF16), map_ref[...]).astype(BF16)
    for copy in copies[3:]:
        copy.wait()


def fetch(sources, targets, sems):
    copies = [
        pltpu.make_async_copy(s, t, sems.at[i]) for i, (s, t) in enumerate(zip(sources, targets))
    ]
    for copy in copies:
        copy.start()
    return copies


def slot_stage(m_ref, src_ref, pat_ref, tgt_ref, ops_ref, out_ref, sums, operators_here):
    boxes, width = m_ref.shape
    patterns = ops_ref.shape[0] // width
    groups, fanin, slots = src_ref.shape
    rows = out_ref.shape[1]
    pack = LANES // slots
    tiles = fanin // pack
    m = m_ref[...]

    def packed(ref, d, h):
        return jnp.concatenate([ref[d, h * pack + i : h * pack + i + 1, :] for i in range(pack)], axis=1)

    sources = [packed(src_ref, d, h) for d in range(groups) for h in range(tiles)]
    cols = code_columns(jnp.concatenate(sources, axis=0))
    eye = iota((slots, LANES), 0) == (iota((slots, LANES), 1) & (slots - 1))
    for d in range(groups):
        ones = []
        pats = []
        for h in range(tiles):
            i = d * tiles + h
            ones.append(onehot(jnp.broadcast_to(cols[:, i : i + 1], (LANES, LANES)), boxes))
            pats.append(pattern_matrix(packed(pat_ref, d, h), eye, patterns))
        got = dot(jnp.concatenate(ones, axis=0), m).astype(BF16)
        s = dot(jnp.concatenate(pats, axis=1), got).astype(BF16)
        for p in range(patterns):
            sums[d * slots : (d + 1) * slots, p * width : (p + 1) * width] = s[
                p * slots : (p + 1) * slots
            ]
    operators_here.wait()
    result = dot(sums[...], ops_ref[...])
    hi = result.astype(BF16)
    lo = (result - hi.astype(F32)).astype(BF16)
    for d in range(groups):
        target = tgt_ref[d : d + 1, :].astype(F32)
        out_ref[d, 0:slots, :] = hi[d * slots : (d + 1) * slots]
        out_ref[d, slots : 2 * slots, :] = lo[d * slots : (d + 1) * slots]
        out_ref[d, 2 * slots : rows, :] = jnp.broadcast_to(
            jnp.concatenate([target, target], axis=1), (rows - 2 * slots, 2 * slots)
        ).astype(BF16)


def plan_kernel(*refs):
    cnt_ref, strength_ref, m_ref, nb_ref, pos_ref, src_ref, pat_ref, tgt_ref, ops_hbm = refs[:9]
    plan_ref, rows_ref, coords_ref, left_ref, sent_ref = refs[9:14]
    ranked, sums, ops_ref, sem = refs[14:]
    operators_here = pltpu.make_async_copy(ops_hbm, ops_ref, sem)
    operators_here.start()
    boxes = strength_ref.shape[0]
    column = count_columns(cnt_ref, boxes)
    row = jnp.concatenate([cnt_ref[i : i + 1, :] for i in range(boxes // LANES)], axis=1)
    rows_ref[1] = strength_ref[...]

    down, across = iota((boxes, boxes), 0), iota((boxes, boxes), 1)
    ahead = (column < row) | ((column == row) & (down < across))
    rank_row = jnp.sum(jnp.where(ahead, 1.0, 0.0), axis=0, keepdims=True)
    behind = (row < column) | ((row == column) & (across < down))
    rank_column = jnp.sum(jnp.where(behind, 1.0, 0.0), axis=1, keepdims=True)
    to_rank = jnp.where(rank_row == down.astype(F32), 1.0, 0.0).astype(BF16)
    from_rank = jnp.where(rank_column == across.astype(F32), 1.0, 0.0).astype(BF16)

    lists = jnp.concatenate(
        [
            nb_ref[...].astype(F32),
            row.astype(F32),
            across[0:1].astype(F32),
            jnp.zeros((16 - 2 - nb_ref.shape[0], boxes), F32),
        ],
        axis=0,
    )
    plan = dot(lists.astype(BF16), from_rank)[0:8].astype(jnp.int32)
    within = jnp.where(column <= STEP * across, 1.0, 0.0)
    ends = jnp.sum(within, axis=0, keepdims=True).astype(jnp.int32) >> log2(TEAM)
    plan_ref[...] = jnp.where(iota((8, boxes), 0) == nb_ref.shape[0] + 2, ends, plan)

    norm = jnp.zeros((boxes, LANES), F32)
    parts = []
    for c in range(3):
        u = pos_ref[c] - 1.0
        h = u.astype(BF16).astype(F32)
        m = (u - h).astype(BF16).astype(F32)
        coords_ref[2 * c] = h
        coords_ref[2 * c + 1] = m
        parts += [-2.0 * h, -2.0 * m]
        v = h + m
        norm = norm + v * v
    rows_ref[0] = norm
    n = norm + EPS
    n1 = n.astype(BF16).astype(F32)
    n2 = (n - n1).astype(BF16).astype(F32)
    parts += [n1, n2, n - n1 - n2]
    ranked[...] = dot(to_rank, jnp.concatenate([p.astype(BF16) for p in parts], axis=1))

    def build(g, carry):
        rows = pl.ds(pl.multiple_of(g * 8, 8), 8)
        f = [ranked[rows, i * LANES : (i + 1) * LANES] for i in range(9)]
        stack = []
        for c in range(3):
            stack += [f[2 * c], f[2 * c], f[2 * c + 1], f[2 * c + 1]]
        stack += f[6:9] + [jnp.zeros((8, LANES), F32)]
        left_ref[g] = jnp.concatenate(stack, axis=0).T.astype(BF16)
        return carry

    lax.fori_loop(0, boxes // 8, build, 0, unroll=4)
    slot_stage(m_ref, src_ref, pat_ref, tgt_ref, ops_ref, sent_ref, sums, operators_here)


def near_kernel(plan_ref, rows_ref, coords_ref, left_ref, out_ref, right, *, start, stop):
    boxes = out_ref.shape[0]
    knear = 4
    out_ref[...] = jnp.zeros_like(out_ref)

    def build(g, carry):
        rows = pl.ds(pl.multiple_of(g * 8, 8), 8)
        tile = [coords_ref[f, rows, :] for f in range(6)]
        for r in range(8):
            for c in range(3):
                h = jnp.broadcast_to(tile[2 * c][r : r + 1], (8, LANES))
                m = jnp.broadcast_to(tile[2 * c + 1][r : r + 1], (8, LANES))
                right[g * 8 + r, 16 * c : 16 * c + 16, :] = jnp.concatenate(
                    [h, m], axis=0
                ).astype(BF16)
        return carry

    lax.fori_loop(0, boxes // 8, build, 0, unroll=4)

    ones = jnp.where(iota((32, LANES), 0) < 24, 1.0, 0.0).astype(BF16)

    def operand(box):
        x, y, z = [right[box, 16 * c : 16 * c + 16, :] for c in range(3)]
        return jnp.concatenate([x, x, y, y, z, z, ones], axis=0)

    def team(depth, g, carry):
        masks = [
            jnp.where((iota((depth, LANES), 1) & 7) == j, 1.0, 0.0).astype(BF16) for j in range(8)
        ]
        eye = iota((depth, LANES), 0) == iota((depth, LANES), 1)
        for e in range(TEAM // 8):
            turned = left_ref[g * (TEAM // 8) + e, 0:depth, :]
            for r in range(8):
                place = g * TEAM + e * 8 + r
                lhs = turned * masks[r]
                acc = None
                for k in range(0, knear, 2):
                    pair = [plan_ref[k + i, place] for i in range(2)]
                    dist = dot(lhs, jnp.concatenate([operand(b) for b in pair], axis=1))
                    for i in range(2):
                        shift = rows_ref[0, pl.ds(pair[i], 1), :]
                        q = rows_ref[1, pl.ds(pair[i], 1), :]
                        term = lax.rsqrt(dist[:, i * LANES : (i + 1) * LANES] + shift) * q
                        acc = term if acc is None else acc + term
                total = jnp.sum(acc, axis=1, keepdims=True)
                out_ref[pl.ds(plan_ref[knear + 1, place], 1), :] = jnp.sum(
                    jnp.where(eye, total, 0.0), axis=0, keepdims=True
                )
        return carry

    done = start
    for step in range(1, LANES // STEP + 1):
        until = jnp.clip(plan_ref[knear + 2, step], done, stop)
        lax.fori_loop(done, until, functools.partial(team, step * STEP), 0)
        done = until


def far_kernel(*refs, blocks, fanin, pieces):
    code_ref, cnt_ref, ops_hbm, eval_hbm, mine_ref, other_ref = refs[:6]
    near_refs = refs[6 : 6 + pieces]
    pay_refs = refs[6 + pieces : -5]
    out_ref, sums, ops_ref, eval_ref, sems = refs[-5:]
    copies = fetch((ops_hbm, eval_hbm), (ops_ref, eval_ref), sems)
    width = mine_ref.shape[1]
    boxes = mine_ref.shape[0] // (blocks // 2)
    patterns = ops_ref.shape[0] // width
    per = LANES // fanin
    tiles = code_ref.shape[0]
    span = 2 * boxes
    pages = blocks // 2
    table = jnp.concatenate(
        [
            jnp.concatenate(
                [mine_ref[j * boxes : (j + 1) * boxes], other_ref[j * boxes : (j + 1) * boxes]], axis=0
            )
            for j in range(pages)
        ],
        axis=1,
    )
    codes = code_ref[...]
    cols = code_columns(codes)
    eye = iota((per, LANES), 0) == (iota((per, LANES), 1) >> log2(fanin))
    batch = 4
    for base in range(0, tiles, batch):
        picks = [
            jnp.broadcast_to(cols[:, i : i + 1], (LANES, LANES)) for i in range(base, base + batch)
        ]
        wide = dot(jnp.concatenate([onehot(c & (span - 1), span) for c in picks], axis=0), table)
        for n in range(batch):
            i = base + n
            page = (picks[n] >> log2(span)) & (pages - 1)
            part = wide[n * LANES : (n + 1) * LANES]
            got = part[:, 0:width]
            for j in range(1, pages):
                got = jnp.where(page == j, part[:, j * width : (j + 1) * width], got)
            pat = pattern_matrix(codes[i : i + 1, :] >> log2(blocks * boxes), eye, patterns)
            s = dot(pat, got.astype(BF16)).astype(BF16)
            for p in range(patterns):
                sums[i * per : (i + 1) * per, p * width : (p + 1) * width] = s[
                    p * per : (p + 1) * per
                ]
    hits = []
    values = []
    for pay in pay_refs:
        depth = pay.shape[0] - 16
        target = pay[depth : depth + 16, :].astype(F32)[0:1]
        box = iota((boxes, depth), 0).astype(F32)
        hits.append(jnp.where(box == target, 1.0, 0.0).astype(BF16))
        values.append(pay[0:depth, :])
    remote_local = dot(jnp.concatenate(hits, axis=1), jnp.concatenate(values, axis=0))
    near = near_refs[0][...]
    for ref in near_refs[1:]:
        near = near + ref[...]
    live = iota((boxes, LANES), 1) < count_columns(cnt_ref, boxes)
    for copy in copies:
        copy.wait()
    local = dot(sums[...], ops_ref[...]) + remote_local
    far = dot(local.astype(BF16), eval_ref[...])
    total = near * (1.0 / (4.0 * math.pi)) + far
    out_ref[...] = jnp.where(live, total, 0.0)


VMEM = pl.BlockSpec(memory_space=pltpu.VMEM)
HBM = pl.BlockSpec(memory_space=pltpu.HBM)
SMEM = pl.BlockSpec(memory_space=pltpu.SMEM)
MIB = 1024 * 1024


def in_hbm(value):
    return pltpu.with_memory_space_constraint(value, pltpu.HBM)


PIECES = 2
TEAM = 16
STEP = 16


def body(
    n_oct,
    n_cube,
    charges,
    panel_counts,
    positions,
    moment_map,
    translations,
    evaluation,
    near_boxes,
    group_sources,
    group_patterns,
    remote_sources,
    remote_patterns,
    remote_targets,
):
    boxes, panels = charges.shape
    width = moment_map.shape[1]
    patterns = translations.shape[0]
    operators = translations.reshape(patterns * width, width)
    counts = panel_counts.reshape(boxes // LANES, LANES)
    handed = (
        near_boxes.T,
        positions,
        remote_sources[0, 0].transpose(0, 2, 1),
        remote_patterns[0, 0].transpose(0, 2, 1),
        remote_targets[0, 0],
    )
    strength, counts, multipole, *handed = pl.pallas_call(
        functools.partial(front_kernel, extra=len(handed)),
        out_shape=(
            jax.ShapeDtypeStruct((boxes, panels), F32),
            jax.ShapeDtypeStruct(counts.shape, jnp.int32),
            jax.ShapeDtypeStruct((boxes, width), BF16),
            *[jax.ShapeDtypeStruct(v.shape, v.dtype) for v in handed],
        ),
        in_specs=[HBM] * (3 + len(handed)),
        out_specs=(VMEM,) * (3 + len(handed)),
        scratch_shapes=[pltpu.VMEM(v.shape, v.dtype) for v in (charges, counts, moment_map)]
        + [pltpu.SemaphoreType.DMA((3 + len(handed),))],
        compiler_params=pltpu.CompilerParams(vmem_limit_bytes=8 * MIB),
        cost_estimate=pl.CostEstimate(
            flops=10_000_000, bytes_accessed=300_000, transcendentals=0
        ),
        name="front",
    )(in_hbm(charges), in_hbm(counts), in_hbm(moment_map), *map(in_hbm, handed))

    me = lax.axis_index("cube")
    octant = lax.axis_index("oct")

    def over_cube(value, k):
        return lax.ppermute(value, "cube", [(i, i ^ k) for i in range(n_cube)])

    def over_oct(value, k):
        return lax.ppermute(value, "oct", [(i, i ^ k) for i in range(n_oct)])

    def after(value, *earlier):
        return lax.optimization_barrier((value, *earlier))[0]

    slots = remote_sources.shape[3]
    plan, *tables, sent = pl.pallas_call(
        plan_kernel,
        out_shape=(
            jax.ShapeDtypeStruct((8, boxes), jnp.int32),
            jax.ShapeDtypeStruct((2, boxes, panels), F32),
            jax.ShapeDtypeStruct((6, boxes, panels), F32),
            jax.ShapeDtypeStruct((boxes // 8, panels, LANES), BF16),
            jax.ShapeDtypeStruct((n_oct, 2 * slots + 16, width), BF16),
        ),
        in_specs=[VMEM] * (3 + len(handed)) + [HBM],
        out_specs=(VMEM,) * 5,
        scratch_shapes=[
            pltpu.VMEM((boxes, 9 * LANES), F32),
            pltpu.VMEM((n_oct * slots, patterns * width), BF16),
            pltpu.VMEM(operators.shape, BF16),
            pltpu.SemaphoreType.DMA,
        ],
        compiler_params=pltpu.CompilerParams(vmem_limit_bytes=16 * MIB),
        cost_estimate=pl.CostEstimate(
            flops=1_000_000_000, bytes_accessed=2_000_000, transcendentals=0
        ),
        name="plan",
    )(counts, strength, multipole, *handed, in_hbm(operators))

    teams = boxes // TEAM
    cut = teams * 11 // 16

    def near_piece(start, stop, tables):
        return pl.pallas_call(
            functools.partial(near_kernel, start=start, stop=stop),
            out_shape=jax.ShapeDtypeStruct((boxes, panels), F32),
            in_specs=[SMEM, VMEM, VMEM, VMEM],
            out_specs=VMEM,
            scratch_shapes=[pltpu.VMEM((boxes, 48, panels), BF16)],
            compiler_params=pltpu.CompilerParams(vmem_limit_bytes=12 * MIB),
            cost_estimate=pl.CostEstimate(
                flops=200_000_000, bytes_accessed=1_000_000, transcendentals=0
            ),
            name="near",
        )(plan, *tables)

    box = {k: lax.dynamic_index_in_dim(sent, octant ^ k, 0, keepdims=False) for k in range(n_oct)}

    def oct_step(bit):
        moving = [k for k in range(n_oct) if k & bit]
        load = jnp.concatenate([box[k] for k in moving], axis=0)
        return load, over_oct(load, bit)

    def unpack(bit, came):
        moving = [k for k in range(n_oct) if k & bit]
        rows = came.shape[0] // len(moving)
        for i, k in enumerate(moving):
            box[k] = came[i * rows : (i + 1) * rows]

    def cube_step(bit, mine):
        return jnp.concatenate([mine, over_cube(mine, bit)], axis=0)

    oct_bits = [1 << i for i in range(log2(n_oct))]
    cube_bits = [1 << i for i in range(log2(n_cube) - 1, 0, -1)]
    mine = cube_step(cube_bits[0], multipole)
    mine = after(mine, plan, sent)
    anchor = [mine]
    for bit in oct_bits[:-1]:
        load, came = oct_step(bit)
        unpack(bit, came)
        anchor.append(load)
    for bit in cube_bits[1:]:
        mine = cube_step(bit, mine)
    tables = lax.optimization_barrier((*tables, *anchor))[: len(tables)]
    first = near_piece(0, cut, tables)

    mine = after(mine, first)
    other = over_cube(mine, 1)
    for k in range(n_oct):
        box[k] = after(box[k], first) if k > 0 else box[k]
    load, came = oct_step(oct_bits[-1])
    tables = lax.optimization_barrier((*tables, mine, load))[: len(tables)]
    second = near_piece(cut, teams, tables)
    other, second, came = lax.optimization_barrier((other, second, came))
    unpack(oct_bits[-1], came)
    payloads = [box[k] for k in range(n_oct)]
    near = [first, second]

    klist = group_sources.shape[1]
    group = n_cube * boxes
    away = group_sources ^ (me * boxes)
    code = (away & (2 * boxes - 1)) + group * group_patterns
    for i in range(1, log2(n_cube)):
        code = code + (((away // boxes) >> i) & 1) * ((n_cube >> i) * boxes)
    return pl.pallas_call(
        functools.partial(far_kernel, blocks=n_cube, fanin=klist, pieces=PIECES),
        out_shape=jax.ShapeDtypeStruct((boxes, panels), F32),
        in_specs=[VMEM] * 2 + [HBM] * 2 + [VMEM] * (2 + PIECES + n_oct),
        out_specs=VMEM,
        scratch_shapes=[
            pltpu.VMEM((boxes, patterns * width), BF16),
            pltpu.VMEM(operators.shape, BF16),
            pltpu.VMEM(evaluation.shape, BF16),
            pltpu.SemaphoreType.DMA((2,)),
        ],
        compiler_params=pltpu.CompilerParams(vmem_limit_bytes=24 * MIB),
        cost_estimate=pl.CostEstimate(
            flops=3_000_000_000, bytes_accessed=2_000_000, transcendentals=0
        ),
        name="far",
    )(
        code.reshape(-1, LANES),
        counts,
        in_hbm(operators),
        in_hbm(evaluation),
        mine,
        other,
        *near,
        *payloads,
    )


def solution(mesh):
    n_oct = mesh.shape["oct"]
    n_cube = mesh.shape["cube"]

    def run(*arrays):
        return body(n_oct, n_cube, *arrays)

    return jax.shard_map(
        run,
        mesh=mesh,
        in_specs=(
            P(("oct", "cube"), None),
            P(("oct", "cube")),
            P(None, ("oct", "cube"), None),
            P(),
            P(),
            P(),
            P(("oct", "cube"), None),
            P(("oct", "cube"), None),
            P(("oct", "cube"), None),
            P("oct", "cube", None, None, None),
            P("oct", "cube", None, None, None),
            P("oct", "cube", None, None),
        ),
        out_specs=P(("oct", "cube"), None),
        check_vma=False,
    )
```

```python
import functools
import math

import jax
import jax.numpy as jnp
from jax import lax
from jax.experimental import pallas as pl
from jax.experimental.pallas import tpu as pltpu
from jax.sharding import PartitionSpec as P

F32 = jnp.float32
BF16 = jnp.bfloat16
LANES = 128
EPS = 0.0025


def iota(shape, dim):
    return lax.broadcasted_iota(jnp.int32, shape, dim)


def count_columns(cnt_ref, boxes):
    eye = iota((LANES, LANES), 0) == iota((LANES, LANES), 1)
    cols = [
        jnp.sum(jnp.where(eye, cnt_ref[i : i + 1, :], 0), axis=1, keepdims=True)
        for i in range(boxes // LANES)
    ]
    return jnp.concatenate(cols, axis=0)


def log2(value):
    return value.bit_length() - 1


def code_columns(codes):
    rows = codes.shape[0]
    padded = jnp.concatenate([codes, jnp.zeros((LANES - rows, LANES), codes.dtype)], axis=0)
    return padded.T


def onehot(local, width):
    lane = iota((LANES, LANES), 1)
    parts = [
        jnp.where(local == lane + LANES * i, 1.0, 0.0).astype(BF16) for i in range(width // LANES)
    ]
    return jnp.concatenate(parts, axis=1)


def pattern_matrix(pattern_row, eye, patterns):
    own = jnp.where(eye, jnp.broadcast_to(pattern_row, eye.shape), -1)
    parts = [jnp.where(own == p, 1.0, 0.0).astype(BF16) for p in range(patterns)]
    return jnp.concatenate(parts, axis=0)


def dot(a, b):
    return jnp.dot(a, b, preferred_element_type=F32)


def front_kernel(*refs, extra):
    strength_ref, count_ref, out_ref = refs[3 + extra : 6 + extra]
    chg_ref, cnt_ref, map_ref = refs[6 + 2 * extra : 9 + 2 * extra]
    copies = fetch(
        refs[: 3 + extra],
        (chg_ref, cnt_ref, map_ref, *refs[6 + extra : 6 + 2 * extra]),
        refs[-1],
    )
    for copy in copies[:3]:
        copy.wait()
    boxes = chg_ref.shape[0]
    live = iota((boxes, LANES), 1) < count_columns(cnt_ref, boxes)
    strength = jnp.where(live, chg_ref[...].astype(F32), 0.0)
    strength_ref[...] = strength
    count_ref[...] = cnt_ref[...]
    out_ref[...] = dot(strength.astype(BF16), map_ref[...]).astype(BF16)
    for copy in copies[3:]:
        copy.wait()


def fetch(sources, targets, sems):
    copies = [
        pltpu.make_async_copy(s, t, sems.at[i]) for i, (s, t) in enumerate(zip(sources, targets))
    ]
    for copy in copies:
        copy.start()
    return copies


def slot_stage(m_ref, src_ref, pat_ref, tgt_ref, ops_ref, out_ref, sums, operators_here):
    boxes, width = m_ref.shape
    patterns = ops_ref.shape[0] // width
    groups, fanin, slots = src_ref.shape
    rows = out_ref.shape[1]
    pack = LANES // slots
    tiles = fanin // pack
    m = m_ref[...]

    def packed(ref, d, h):
        return jnp.concatenate([ref[d, h * pack + i : h * pack + i + 1, :] for i in range(pack)], axis=1)

    sources = [packed(src_ref, d, h) for d in range(groups) for h in range(tiles)]
    cols = code_columns(jnp.concatenate(sources, axis=0))
    eye = iota((slots, LANES), 0) == (iota((slots, LANES), 1) & (slots - 1))
    for d in range(groups):
        ones = []
        pats = []
        for h in range(tiles):
            i = d * tiles + h
            ones.append(onehot(jnp.broadcast_to(cols[:, i : i + 1], (LANES, LANES)), boxes))
            pats.append(pattern_matrix(packed(pat_ref, d, h), eye, patterns))
        got = dot(jnp.concatenate(ones, axis=0), m).astype(BF16)
        s = dot(jnp.concatenate(pats, axis=1), got).astype(BF16)
        for p in range(patterns):
            sums[d * slots : (d + 1) * slots, p * width : (p + 1) * width] = s[
                p * slots : (p + 1) * slots
            ]
    operators_here.wait()
    result = dot(sums[...], ops_ref[...])
    hi = result.astype(BF16)
    lo = (result - hi.astype(F32)).astype(BF16)
    for d in range(groups):
        target = tgt_ref[d : d + 1, :].astype(F32)
        out_ref[d, 0:slots, :] = hi[d * slots : (d + 1) * slots]
        out_ref[d, slots : 2 * slots, :] = lo[d * slots : (d + 1) * slots]
        out_ref[d, 2 * slots : rows, :] = jnp.broadcast_to(
            jnp.concatenate([target, target], axis=1), (rows - 2 * slots, 2 * slots)
        ).astype(BF16)


def plan_kernel(*refs):
    cnt_ref, strength_ref, m_ref, nb_ref, pos_ref, src_ref, pat_ref, tgt_ref, ops_hbm = refs[:9]
    plan_ref, rows_ref, coords_ref, left_ref, sent_ref = refs[9:14]
    ranked, sums, ops_ref, sem = refs[14:]
    operators_here = pltpu.make_async_copy(ops_hbm, ops_ref, sem)
    operators_here.start()
    boxes = strength_ref.shape[0]
    column = count_columns(cnt_ref, boxes)
    row = jnp.concatenate([cnt_ref[i : i + 1, :] for i in range(boxes // LANES)], axis=1)
    rows_ref[1] = strength_ref[...]

    down, across = iota((boxes, boxes), 0), iota((boxes, boxes), 1)
    ahead = (column < row) | ((column == row) & (down < across))
    rank_row = jnp.sum(jnp.where(ahead, 1.0, 0.0), axis=0, keepdims=True)
    behind = (row < column) | ((row == column) & (across < down))
    rank_column = jnp.sum(jnp.where(behind, 1.0, 0.0), axis=1, keepdims=True)
    to_rank = jnp.where(rank_row == down.astype(F32), 1.0, 0.0).astype(BF16)
    from_rank = jnp.where(rank_column == across.astype(F32), 1.0, 0.0).astype(BF16)

    lists = jnp.concatenate(
        [
            nb_ref[...].astype(F32),
            row.astype(F32),
            across[0:1].astype(F32),
            jnp.zeros((16 - 2 - nb_ref.shape[0], boxes), F32),
        ],
        axis=0,
    )
    plan = dot(lists.astype(BF16), from_rank)[0:8].astype(jnp.int32)
    within = jnp.where(column <= STEP * across, 1.0, 0.0)
    ends = jnp.sum(within, axis=0, keepdims=True).astype(jnp.int32) >> log2(TEAM)
    plan_ref[...] = jnp.where(iota((8, boxes), 0) == nb_ref.shape[0] + 2, ends, plan)

    norm = jnp.zeros((boxes, LANES), F32)
    parts = []
    for c in range(3):
        u = pos_ref[c] - 1.0
        h = u.astype(BF16).astype(F32)
        m = (u - h).astype(BF16).astype(F32)
        coords_ref[2 * c] = h
        coords_ref[2 * c + 1] = m
        parts += [-2.0 * h, -2.0 * m]
        v = h + m
        norm = norm + v * v
    rows_ref[0] = norm
    n = norm + EPS
    n1 = n.astype(BF16).astype(F32)
    n2 = (n - n1).astype(BF16).astype(F32)
    parts += [n1, n2, n - n1 - n2]
    ranked[...] = dot(to_rank, jnp.concatenate([p.astype(BF16) for p in parts], axis=1))

    def build(g, carry):
        rows = pl.ds(pl.multiple_of(g * 8, 8), 8)
        f = [ranked[rows, i * LANES : (i + 1) * LANES] for i in range(9)]
        stack = []
        for c in range(3):
            stack += [f[2 * c], f[2 * c], f[2 * c + 1], f[2 * c + 1]]
        stack += f[6:9] + [jnp.zeros((8, LANES), F32)]
        left_ref[g] = jnp.concatenate(stack, axis=0).T.astype(BF16)
        return carry

    lax.fori_loop(0, boxes // 8, build, 0, unroll=4)
    slot_stage(m_ref, src_ref, pat_ref, tgt_ref, ops_ref, sent_ref, sums, operators_here)


def near_kernel(plan_ref, rows_ref, coords_ref, left_ref, out_ref, right, *, start, stop):
    boxes = out_ref.shape[0]
    knear = 4
    out_ref[...] = jnp.zeros_like(out_ref)

    def build(g, carry):
        rows = pl.ds(pl.multiple_of(g * 8, 8), 8)
        tile = [coords_ref[f, rows, :] for f in range(6)]
        for r in range(8):
            for c in range(3):
                h = jnp.broadcast_to(tile[2 * c][r : r + 1], (8, LANES))
                m = jnp.broadcast_to(tile[2 * c + 1][r : r + 1], (8, LANES))
                right[g * 8 + r, 16 * c : 16 * c + 16, :] = jnp.concatenate(
                    [h, m], axis=0
                ).astype(BF16)
        return carry

    lax.fori_loop(0, boxes // 8, build, 0, unroll=4)

    ones = jnp.where(iota((32, LANES), 0) < 24, 1.0, 0.0).astype(BF16)

    def operand(box):
        x, y, z = [right[box, 16 * c : 16 * c + 16, :] for c in range(3)]
        return jnp.concatenate([x, x, y, y, z, z, ones], axis=0)

    def team(depth, g, carry):
        masks = [
            jnp.where((iota((depth, LANES), 1) & 7) == j, 1.0, 0.0).astype(BF16) for j in range(8)
        ]
        eye = iota((depth, LANES), 0) == iota((depth, LANES), 1)
        for e in range(TEAM // 8):
            turned = left_ref[g * (TEAM // 8) + e, 0:depth, :]
            for r in range(8):
                place = g * TEAM + e * 8 + r
                lhs = turned * masks[r]
                acc = None
                for k in range(0, knear, 2):
                    pair = [plan_ref[k + i, place] for i in range(2)]
                    dist = dot(lhs, jnp.concatenate([operand(b) for b in pair], axis=1))
                    for i in range(2):
                        shift = rows_ref[0, pl.ds(pair[i], 1), :]
                        q = rows_ref[1, pl.ds(pair[i], 1), :]
                        term = lax.rsqrt(dist[:, i * LANES : (i + 1) * LANES] + shift) * q
                        acc = term if acc is None else acc + term
                total = jnp.sum(acc, axis=1, keepdims=True)
                out_ref[pl.ds(plan_ref[knear + 1, place], 1), :] = jnp.sum(
                    jnp.where(eye, total, 0.0), axis=0, keepdims=True
                )
        return carry

    done = start
    for step in range(1, LANES // STEP + 1):
        until = jnp.clip(plan_ref[knear + 2, step], done, stop)
        lax.fori_loop(done, until, functools.partial(team, step * STEP), 0)
        done = until


def far_kernel(*refs, blocks, fanin, pieces):
    code_ref, cnt_ref, ops_ref, eval_ref, mine_ref, other_ref = refs[:6]
    near_refs = refs[6 : 6 + pieces]
    pay_refs = refs[6 + pieces : -2]
    out_ref, sums = refs[-2:]
    width = mine_ref.shape[1]
    boxes = mine_ref.shape[0] // (blocks // 2)
    patterns = ops_ref.shape[0] // width
    per = LANES // fanin
    tiles = code_ref.shape[0]
    span = 2 * boxes
    pages = blocks // 2
    table = jnp.concatenate(
        [
            jnp.concatenate(
                [mine_ref[j * boxes : (j + 1) * boxes], other_ref[j * boxes : (j + 1) * boxes]], axis=0
            )
            for j in range(pages)
        ],
        axis=1,
    )
    codes = code_ref[...]
    cols = code_columns(codes)
    eye = iota((per, LANES), 0) == (iota((per, LANES), 1) >> log2(fanin))
    batch = 4
    for base in range(0, tiles, batch):
        picks = [
            jnp.broadcast_to(cols[:, i : i + 1], (LANES, LANES)) for i in range(base, base + batch)
        ]
        wide = dot(jnp.concatenate([onehot(c & (span - 1), span) for c in picks], axis=0), table)
        for n in range(batch):
            i = base + n
            page = (picks[n] >> log2(span)) & (pages - 1)
            part = wide[n * LANES : (n + 1) * LANES]
            got = part[:, 0:width]
            for j in range(1, pages):
                got = jnp.where(page == j, part[:, j * width : (j + 1) * width], got)
            pat = pattern_matrix(codes[i : i + 1, :] >> log2(blocks * boxes), eye, patterns)
            s = dot(pat, got.astype(BF16)).astype(BF16)
            for p in range(patterns):
                sums[i * per : (i + 1) * per, p * width : (p + 1) * width] = s[
                    p * per : (p + 1) * per
                ]
    hits = []
    values = []
    for pay in pay_refs:
        depth = pay.shape[0] - 16
        target = pay[depth : depth + 16, :].astype(F32)[0:1]
        box = iota((boxes, depth), 0).astype(F32)
        hits.append(jnp.where(box == target, 1.0, 0.0).astype(BF16))
        values.append(pay[0:depth, :])
    remote_local = dot(jnp.concatenate(hits, axis=1), jnp.concatenate(values, axis=0))
    near = near_refs[0][...]
    for ref in near_refs[1:]:
        near = near + ref[...]
    live = iota((boxes, LANES), 1) < count_columns(cnt_ref, boxes)
    local = dot(sums[...], ops_ref[...]) + remote_local
    far = dot(local.astype(BF16), eval_ref[...])
    total = near * (1.0 / (4.0 * math.pi)) + far
    out_ref[...] = jnp.where(live, total, 0.0)


VMEM = pl.BlockSpec(memory_space=pltpu.VMEM)
HBM = pl.BlockSpec(memory_space=pltpu.HBM)
SMEM = pl.BlockSpec(memory_space=pltpu.SMEM)
MIB = 1024 * 1024


def in_hbm(value):
    return pltpu.with_memory_space_constraint(value, pltpu.HBM)


PIECES = 2
TEAM = 16
STEP = 16


def body(
    n_oct,
    n_cube,
    charges,
    panel_counts,
    positions,
    moment_map,
    translations,
    evaluation,
    near_boxes,
    group_sources,
    group_patterns,
    remote_sources,
    remote_patterns,
    remote_targets,
):
    boxes, panels = charges.shape
    width = moment_map.shape[1]
    patterns = translations.shape[0]
    operators = translations.reshape(patterns * width, width)
    counts = panel_counts.reshape(boxes // LANES, LANES)
    handed = (
        near_boxes.T,
        positions,
        remote_sources[0, 0].transpose(0, 2, 1),
        remote_patterns[0, 0].transpose(0, 2, 1),
        remote_targets[0, 0],
        evaluation,
    )
    strength, counts, multipole, *handed, evaluation = pl.pallas_call(
        functools.partial(front_kernel, extra=len(handed)),
        out_shape=(
            jax.ShapeDtypeStruct((boxes, panels), F32),
            jax.ShapeDtypeStruct(counts.shape, jnp.int32),
            jax.ShapeDtypeStruct((boxes, width), BF16),
            *[jax.ShapeDtypeStruct(v.shape, v.dtype) for v in handed],
        ),
        in_specs=[HBM] * (3 + len(handed)),
        out_specs=(VMEM,) * (3 + len(handed)),
        scratch_shapes=[pltpu.VMEM(v.shape, v.dtype) for v in (charges, counts, moment_map)]
        + [pltpu.SemaphoreType.DMA((3 + len(handed),))],
        compiler_params=pltpu.CompilerParams(vmem_limit_bytes=8 * MIB),
        cost_estimate=pl.CostEstimate(
            flops=10_000_000, bytes_accessed=300_000, transcendentals=0
        ),
        name="front",
    )(in_hbm(charges), in_hbm(counts), in_hbm(moment_map), *map(in_hbm, handed))

    me = lax.axis_index("cube")
    octant = lax.axis_index("oct")

    def over_cube(value, k):
        return lax.ppermute(value, "cube", [(i, i ^ k) for i in range(n_cube)])

    def over_oct(value, k):
        return lax.ppermute(value, "oct", [(i, i ^ k) for i in range(n_oct)])

    def after(value, *earlier):
        return lax.optimization_barrier((value, *earlier))[0]

    slots = remote_sources.shape[3]
    plan, *tables, sent = pl.pallas_call(
        plan_kernel,
        out_shape=(
            jax.ShapeDtypeStruct((8, boxes), jnp.int32),
            jax.ShapeDtypeStruct((2, boxes, panels), F32),
            jax.ShapeDtypeStruct((6, boxes, panels), F32),
            jax.ShapeDtypeStruct((boxes // 8, panels, LANES), BF16),
            jax.ShapeDtypeStruct((n_oct, 2 * slots + 16, width), BF16),
        ),
        in_specs=[VMEM] * (3 + len(handed)) + [HBM],
        out_specs=(VMEM,) * 5,
        scratch_shapes=[
            pltpu.VMEM((boxes, 9 * LANES), F32),
            pltpu.VMEM((n_oct * slots, patterns * width), BF16),
            pltpu.VMEM(operators.shape, BF16),
            pltpu.SemaphoreType.DMA,
        ],
        compiler_params=pltpu.CompilerParams(vmem_limit_bytes=16 * MIB),
        cost_estimate=pl.CostEstimate(
            flops=1_000_000_000, bytes_accessed=2_000_000, transcendentals=0
        ),
        name="plan",
    )(counts, strength, multipole, *handed, in_hbm(operators))

    teams = boxes // TEAM
    cut = teams * 11 // 16

    def near_piece(start, stop, tables):
        return pl.pallas_call(
            functools.partial(near_kernel, start=start, stop=stop),
            out_shape=jax.ShapeDtypeStruct((boxes, panels), F32),
            in_specs=[SMEM, VMEM, VMEM, VMEM],
            out_specs=VMEM,
            scratch_shapes=[pltpu.VMEM((boxes, 48, panels), BF16)],
            compiler_params=pltpu.CompilerParams(vmem_limit_bytes=12 * MIB),
            cost_estimate=pl.CostEstimate(
                flops=200_000_000, bytes_accessed=1_000_000, transcendentals=0
            ),
            name="near",
        )(plan, *tables)

    box = {k: lax.dynamic_index_in_dim(sent, octant ^ k, 0, keepdims=False) for k in range(n_oct)}

    def oct_step(bit):
        moving = [k for k in range(n_oct) if k & bit]
        load = jnp.concatenate([box[k] for k in moving], axis=0)
        return load, over_oct(load, bit)

    def unpack(bit, came):
        moving = [k for k in range(n_oct) if k & bit]
        rows = came.shape[0] // len(moving)
        for i, k in enumerate(moving):
            box[k] = came[i * rows : (i + 1) * rows]

    def cube_step(bit, mine):
        return jnp.concatenate([mine, over_cube(mine, bit)], axis=0)

    oct_bits = [1 << i for i in range(log2(n_oct))]
    cube_bits = [1 << i for i in range(1, log2(n_cube))]
    mine = cube_step(cube_bits[0], multipole)
    mine = after(mine, plan, sent)
    anchor = [mine]
    for bit in oct_bits[:-1]:
        load, came = oct_step(bit)
        unpack(bit, came)
        anchor.append(load)
    for bit in cube_bits[1:]:
        mine = cube_step(bit, mine)
    tables = lax.optimization_barrier((*tables, *anchor))[: len(tables)]
    first = near_piece(0, cut, tables)

    mine = after(mine, first)
    other = over_cube(mine, 1)
    for k in range(n_oct):
        box[k] = after(box[k], first) if k > 0 else box[k]
    load, came = oct_step(oct_bits[-1])
    tables = lax.optimization_barrier((*tables, mine, load))[: len(tables)]
    second = near_piece(cut, teams, tables)
    other, second, came = lax.optimization_barrier((other, second, came))
    unpack(oct_bits[-1], came)
    payloads = [box[k] for k in range(n_oct)]
    near = [first, second]

    klist = group_sources.shape[1]
    group = n_cube * boxes
    code = (group_sources ^ (me * boxes)) + group * group_patterns
    return pl.pallas_call(
        functools.partial(far_kernel, blocks=n_cube, fanin=klist, pieces=PIECES),
        out_shape=jax.ShapeDtypeStruct((boxes, panels), F32),
        in_specs=[VMEM] * (6 + PIECES + n_oct),
        out_specs=VMEM,
        scratch_shapes=[pltpu.VMEM((boxes, patterns * width), BF16)],
        compiler_params=pltpu.CompilerParams(vmem_limit_bytes=24 * MIB),
        cost_estimate=pl.CostEstimate(
            flops=3_000_000_000, bytes_accessed=2_000_000, transcendentals=0
        ),
        name="far",
    )(
        code.reshape(-1, LANES),
        counts,
        operators,
        evaluation,
        mine,
        other,
        *near,
        *payloads,
    )


def solution(mesh):
    n_oct = mesh.shape["oct"]
    n_cube = mesh.shape["cube"]

    def run(*arrays):
        return body(n_oct, n_cube, *arrays)

    return jax.shard_map(
        run,
        mesh=mesh,
        in_specs=(
            P(("oct", "cube"), None),
            P(("oct", "cube")),
            P(None, ("oct", "cube"), None),
            P(),
            P(),
            P(),
            P(("oct", "cube"), None),
            P(("oct", "cube"), None),
            P(("oct", "cube"), None),
            P("oct", "cube", None, None, None),
            P("oct", "cube", None, None, None),
            P("oct", "cube", None, None),
        ),
        out_specs=P(("oct", "cube"), None),
        check_vma=False,
    )
```

```python
import functools
import math

import jax
import jax.numpy as jnp
from jax import lax
from jax.experimental import pallas as pl
from jax.experimental.pallas import tpu as pltpu
from jax.sharding import PartitionSpec as P

F32 = jnp.float32
BF16 = jnp.bfloat16
LANES = 128
EPS = 0.0025


def iota(shape, dim):
    return lax.broadcasted_iota(jnp.int32, shape, dim)


def count_columns(cnt_ref, boxes):
    eye = iota((LANES, LANES), 0) == iota((LANES, LANES), 1)
    cols = [
        jnp.sum(jnp.where(eye, cnt_ref[i : i + 1, :], 0), axis=1, keepdims=True)
        for i in range(boxes // LANES)
    ]
    return jnp.concatenate(cols, axis=0)


def log2(value):
    return value.bit_length() - 1


def code_columns(codes):
    rows = codes.shape[0]
    padded = jnp.concatenate([codes, jnp.zeros((LANES - rows, LANES), codes.dtype)], axis=0)
    return padded.T


def onehot(local, width):
    lane = iota((LANES, LANES), 1)
    parts = [
        jnp.where(local == lane + LANES * i, 1.0, 0.0).astype(BF16) for i in range(width // LANES)
    ]
    return jnp.concatenate(parts, axis=1)


def pattern_matrix(pattern_row, eye, patterns):
    own = jnp.where(eye, jnp.broadcast_to(pattern_row, eye.shape), -1)
    parts = [jnp.where(own == p, 1.0, 0.0).astype(BF16) for p in range(patterns)]
    return jnp.concatenate(parts, axis=0)


def dot(a, b):
    return jnp.dot(a, b, preferred_element_type=F32)


def front_kernel(*refs, extra):
    strength_ref, count_ref, out_ref = refs[3 + extra : 6 + extra]
    chg_ref, cnt_ref, map_ref = refs[6 + 2 * extra : 9 + 2 * extra]
    copies = fetch(
        refs[: 3 + extra],
        (chg_ref, cnt_ref, map_ref, *refs[6 + extra : 6 + 2 * extra]),
        refs[-1],
    )
    for copy in copies[:3]:
        copy.wait()
    boxes = chg_ref.shape[0]
    live = iota((boxes, LANES), 1) < count_columns(cnt_ref, boxes)
    strength = jnp.where(live, chg_ref[...].astype(F32), 0.0)
    strength_ref[...] = strength
    count_ref[...] = cnt_ref[...]
    out_ref[...] = dot(strength.astype(BF16), map_ref[...]).astype(BF16)
    for copy in copies[3:]:
        copy.wait()


def fetch(sources, targets, sems):
    copies = [
        pltpu.make_async_copy(s, t, sems.at[i]) for i, (s, t) in enumerate(zip(sources, targets))
    ]
    for copy in copies:
        copy.start()
    return copies


def slot_stage(m_ref, src_ref, pat_ref, tgt_ref, ops_ref, out_ref, sums, operators_here):
    boxes, width = m_ref.shape
    patterns = ops_ref.shape[0] // width
    groups, fanin, slots = src_ref.shape
    rows = out_ref.shape[1]
    pack = LANES // slots
    tiles = fanin // pack
    m = m_ref[...]

    def packed(ref, d, h):
        return jnp.concatenate([ref[d, h * pack + i : h * pack + i + 1, :] for i in range(pack)], axis=1)

    sources = [packed(src_ref, d, h) for d in range(groups) for h in range(tiles)]
    cols = code_columns(jnp.concatenate(sources, axis=0))
    eye = iota((slots, LANES), 0) == (iota((slots, LANES), 1) & (slots - 1))
    for d in range(groups):
        ones = []
        pats = []
        for h in range(tiles):
            i = d * tiles + h
            ones.append(onehot(jnp.broadcast_to(cols[:, i : i + 1], (LANES, LANES)), boxes))
            pats.append(pattern_matrix(packed(pat_ref, d, h), eye, patterns))
        got = dot(jnp.concatenate(ones, axis=0), m).astype(BF16)
        s = dot(jnp.concatenate(pats, axis=1), got).astype(BF16)
        for p in range(patterns):
            sums[d * slots : (d + 1) * slots, p * width : (p + 1) * width] = s[
                p * slots : (p + 1) * slots
            ]
    operators_here.wait()
    result = dot(sums[...], ops_ref[...])
    hi = result.astype(BF16)
    lo = (result - hi.astype(F32)).astype(BF16)
    for d in range(groups):
        target = tgt_ref[d : d + 1, :].astype(F32)
        out_ref[d, 0:slots, :] = hi[d * slots : (d + 1) * slots]
        out_ref[d, slots : 2 * slots, :] = lo[d * slots : (d + 1) * slots]
        out_ref[d, 2 * slots : rows, :] = jnp.broadcast_to(
            jnp.concatenate([target, target], axis=1), (rows - 2 * slots, 2 * slots)
        ).astype(BF16)


def plan_kernel(*refs):
    cnt_ref, strength_ref, m_ref, nb_ref, pos_ref, src_ref, pat_ref, tgt_ref, ops_hbm = refs[:9]
    plan_ref, rows_ref, coords_ref, left_ref, sent_ref = refs[9:14]
    ranked, sums, ops_ref, sem = refs[14:]
    operators_here = pltpu.make_async_copy(ops_hbm, ops_ref, sem)
    operators_here.start()
    boxes = strength_ref.shape[0]
    column = count_columns(cnt_ref, boxes)
    row = jnp.concatenate([cnt_ref[i : i + 1, :] for i in range(boxes // LANES)], axis=1)
    rows_ref[1] = strength_ref[...]

    down, across = iota((boxes, boxes), 0), iota((boxes, boxes), 1)
    ahead = (column < row) | ((column == row) & (down < across))
    rank_row = jnp.sum(jnp.where(ahead, 1.0, 0.0), axis=0, keepdims=True)
    behind = (row < column) | ((row == column) & (across < down))
    rank_column = jnp.sum(jnp.where(behind, 1.0, 0.0), axis=1, keepdims=True)
    to_rank = jnp.where(rank_row == down.astype(F32), 1.0, 0.0).astype(BF16)
    from_rank = jnp.where(rank_column == across.astype(F32), 1.0, 0.0).astype(BF16)

    lists = jnp.concatenate(
        [
            nb_ref[...].astype(F32),
            row.astype(F32),
            across[0:1].astype(F32),
            jnp.zeros((16 - 2 - nb_ref.shape[0], boxes), F32),
        ],
        axis=0,
    )
    plan = dot(lists.astype(BF16), from_rank)[0:8].astype(jnp.int32)
    within = jnp.where(column <= STEP * across, 1.0, 0.0)
    ends = jnp.sum(within, axis=0, keepdims=True).astype(jnp.int32) >> log2(TEAM)
    plan_ref[...] = jnp.where(iota((8, boxes), 0) == nb_ref.shape[0] + 2, ends, plan)

    norm = jnp.zeros((boxes, LANES), F32)
    parts = []
    for c in range(3):
        u = pos_ref[c] - 1.0
        h = u.astype(BF16).astype(F32)
        m = (u - h).astype(BF16).astype(F32)
        coords_ref[2 * c] = h
        coords_ref[2 * c + 1] = m
        parts += [-2.0 * h, -2.0 * m]
        v = h + m
        norm = norm + v * v
    rows_ref[0] = norm
    n = norm + EPS
    n1 = n.astype(BF16).astype(F32)
    n2 = (n - n1).astype(BF16).astype(F32)
    parts += [n1, n2, n - n1 - n2]
    ranked[...] = dot(to_rank, jnp.concatenate([p.astype(BF16) for p in parts], axis=1))

    def build(g, carry):
        rows = pl.ds(pl.multiple_of(g * 8, 8), 8)
        f = [ranked[rows, i * LANES : (i + 1) * LANES] for i in range(9)]
        stack = []
        for c in range(3):
            stack += [f[2 * c], f[2 * c], f[2 * c + 1], f[2 * c + 1]]
        stack += f[6:9] + [jnp.zeros((8, LANES), F32)]
        left_ref[g] = jnp.concatenate(stack, axis=0).T.astype(BF16)
        return carry

    lax.fori_loop(0, boxes // 8, build, 0, unroll=4)
    slot_stage(m_ref, src_ref, pat_ref, tgt_ref, ops_ref, sent_ref, sums, operators_here)


def near_kernel(plan_ref, rows_ref, coords_ref, left_ref, out_ref, right, *, start, stop):
    boxes = out_ref.shape[0]
    knear = 4
    out_ref[...] = jnp.zeros_like(out_ref)

    def build(g, carry):
        rows = pl.ds(pl.multiple_of(g * 8, 8), 8)
        tile = [coords_ref[f, rows, :] for f in range(6)]
        for r in range(8):
            for c in range(3):
                h = jnp.broadcast_to(tile[2 * c][r : r + 1], (8, LANES))
                m = jnp.broadcast_to(tile[2 * c + 1][r : r + 1], (8, LANES))
                right[g * 8 + r, 16 * c : 16 * c + 16, :] = jnp.concatenate(
                    [h, m], axis=0
                ).astype(BF16)
        return carry

    lax.fori_loop(0, boxes // 8, build, 0, unroll=4)

    ones = jnp.where(iota((32, LANES), 0) < 24, 1.0, 0.0).astype(BF16)

    def operand(box):
        x, y, z = [right[box, 16 * c : 16 * c + 16, :] for c in range(3)]
        return jnp.concatenate([x, x, y, y, z, z, ones], axis=0)

    def team(depth, g, carry):
        masks = [
            jnp.where((iota((depth, LANES), 1) & 7) == j, 1.0, 0.0).astype(BF16) for j in range(8)
        ]
        eye = iota((depth, LANES), 0) == iota((depth, LANES), 1)
        for e in range(TEAM // 8):
            turned = left_ref[g * (TEAM // 8) + e, 0:depth, :]
            for r in range(8):
                place = g * TEAM + e * 8 + r
                lhs = turned * masks[r]
                acc = None
                for k in range(0, knear, 2):
                    pair = [plan_ref[k + i, place] for i in range(2)]
                    dist = dot(lhs, jnp.concatenate([operand(b) for b in pair], axis=1))
                    for i in range(2):
                        shift = rows_ref[0, pl.ds(pair[i], 1), :]
                        q = rows_ref[1, pl.ds(pair[i], 1), :]
                        square = dist[:, i * LANES : (i + 1) * LANES] + shift
                        term = lax.rsqrt(square.astype(BF16)).astype(F32) * q
                        acc = term if acc is None else acc + term
                total = jnp.sum(acc, axis=1, keepdims=True)
                out_ref[pl.ds(plan_ref[knear + 1, place], 1), :] = jnp.sum(
                    jnp.where(eye, total, 0.0), axis=0, keepdims=True
                )
        return carry

    done = start
    for step in range(1, LANES // STEP + 1):
        until = jnp.clip(plan_ref[knear + 2, step], done, stop)
        lax.fori_loop(done, until, functools.partial(team, step * STEP), 0)
        done = until


def far_kernel(*refs, blocks, fanin, pieces):
    code_ref, cnt_ref, ops_ref, eval_ref, mine_ref, other_ref = refs[:6]
    near_refs = refs[6 : 6 + pieces]
    pay_refs = refs[6 + pieces : -2]
    out_ref, sums = refs[-2:]
    width = mine_ref.shape[1]
    boxes = mine_ref.shape[0] // (blocks // 2)
    patterns = ops_ref.shape[0] // width
    per = LANES // fanin
    tiles = code_ref.shape[0]
    span = 2 * boxes
    pages = blocks // 2
    table = jnp.concatenate(
        [
            jnp.concatenate(
                [mine_ref[j * boxes : (j + 1) * boxes], other_ref[j * boxes : (j + 1) * boxes]], axis=0
            )
            for j in range(pages)
        ],
        axis=1,
    )
    codes = code_ref[...]
    cols = code_columns(codes)
    eye = iota((per, LANES), 0) == (iota((per, LANES), 1) >> log2(fanin))
    batch = 4
    for base in range(0, tiles, batch):
        picks = [
            jnp.broadcast_to(cols[:, i : i + 1], (LANES, LANES)) for i in range(base, base + batch)
        ]
        wide = dot(jnp.concatenate([onehot(c & (span - 1), span) for c in picks], axis=0), table)
        for n in range(batch):
            i = base + n
            page = (picks[n] >> log2(span)) & (pages - 1)
            part = wide[n * LANES : (n + 1) * LANES]
            got = part[:, 0:width]
            for j in range(1, pages):
                got = jnp.where(page == j, part[:, j * width : (j + 1) * width], got)
            pat = pattern_matrix(codes[i : i + 1, :] >> log2(blocks * boxes), eye, patterns)
            s = dot(pat, got.astype(BF16)).astype(BF16)
            for p in range(patterns):
                sums[i * per : (i + 1) * per, p * width : (p + 1) * width] = s[
                    p * per : (p + 1) * per
                ]
    hits = []
    values = []
    for pay in pay_refs:
        depth = pay.shape[0] - 16
        target = pay[depth : depth + 16, :].astype(F32)[0:1]
        box = iota((boxes, depth), 0).astype(F32)
        hits.append(jnp.where(box == target, 1.0, 0.0).astype(BF16))
        values.append(pay[0:depth, :])
    remote_local = dot(jnp.concatenate(hits, axis=1), jnp.concatenate(values, axis=0))
    near = near_refs[0][...]
    for ref in near_refs[1:]:
        near = near + ref[...]
    live = iota((boxes, LANES), 1) < count_columns(cnt_ref, boxes)
    local = dot(sums[...], ops_ref[...]) + remote_local
    far = dot(local.astype(BF16), eval_ref[...])
    total = near * (1.0 / (4.0 * math.pi)) + far
    out_ref[...] = jnp.where(live, total, 0.0)


VMEM = pl.BlockSpec(memory_space=pltpu.VMEM)
HBM = pl.BlockSpec(memory_space=pltpu.HBM)
SMEM = pl.BlockSpec(memory_space=pltpu.SMEM)
MIB = 1024 * 1024


def in_hbm(value):
    return pltpu.with_memory_space_constraint(value, pltpu.HBM)


PIECES = 2
TEAM = 16
STEP = 16


def body(
    n_oct,
    n_cube,
    charges,
    panel_counts,
    positions,
    moment_map,
    translations,
    evaluation,
    near_boxes,
    group_sources,
    group_patterns,
    remote_sources,
    remote_patterns,
    remote_targets,
):
    boxes, panels = charges.shape
    width = moment_map.shape[1]
    patterns = translations.shape[0]
    operators = translations.reshape(patterns * width, width)
    counts = panel_counts.reshape(boxes // LANES, LANES)
    handed = (
        near_boxes.T,
        positions,
        remote_sources[0, 0].transpose(0, 2, 1),
        remote_patterns[0, 0].transpose(0, 2, 1),
        remote_targets[0, 0],
        evaluation,
    )
    strength, counts, multipole, *handed, evaluation = pl.pallas_call(
        functools.partial(front_kernel, extra=len(handed)),
        out_shape=(
            jax.ShapeDtypeStruct((boxes, panels), F32),
            jax.ShapeDtypeStruct(counts.shape, jnp.int32),
            jax.ShapeDtypeStruct((boxes, width), BF16),
            *[jax.ShapeDtypeStruct(v.shape, v.dtype) for v in handed],
        ),
        in_specs=[HBM] * (3 + len(handed)),
        out_specs=(VMEM,) * (3 + len(handed)),
        scratch_shapes=[pltpu.VMEM(v.shape, v.dtype) for v in (charges, counts, moment_map)]
        + [pltpu.SemaphoreType.DMA((3 + len(handed),))],
        compiler_params=pltpu.CompilerParams(vmem_limit_bytes=8 * MIB),
        cost_estimate=pl.CostEstimate(
            flops=10_000_000, bytes_accessed=300_000, transcendentals=0
        ),
        name="front",
    )(in_hbm(charges), in_hbm(counts), in_hbm(moment_map), *map(in_hbm, handed))

    me = lax.axis_index("cube")
    octant = lax.axis_index("oct")

    def over_cube(value, k):
        return lax.ppermute(value, "cube", [(i, i ^ k) for i in range(n_cube)])

    def over_oct(value, k):
        return lax.ppermute(value, "oct", [(i, i ^ k) for i in range(n_oct)])

    def after(value, *earlier):
        return lax.optimization_barrier((value, *earlier))[0]

    slots = remote_sources.shape[3]
    plan, *tables, sent = pl.pallas_call(
        plan_kernel,
        out_shape=(
            jax.ShapeDtypeStruct((8, boxes), jnp.int32),
            jax.ShapeDtypeStruct((2, boxes, panels), F32),
            jax.ShapeDtypeStruct((6, boxes, panels), F32),
            jax.ShapeDtypeStruct((boxes // 8, panels, LANES), BF16),
            jax.ShapeDtypeStruct((n_oct, 2 * slots + 16, width), BF16),
        ),
        in_specs=[VMEM] * (3 + len(handed)) + [HBM],
        out_specs=(VMEM,) * 5,
        scratch_shapes=[
            pltpu.VMEM((boxes, 9 * LANES), F32),
            pltpu.VMEM((n_oct * slots, patterns * width), BF16),
            pltpu.VMEM(operators.shape, BF16),
            pltpu.SemaphoreType.DMA,
        ],
        compiler_params=pltpu.CompilerParams(vmem_limit_bytes=16 * MIB),
        cost_estimate=pl.CostEstimate(
            flops=1_000_000_000, bytes_accessed=2_000_000, transcendentals=0
        ),
        name="plan",
    )(counts, strength, multipole, *handed, in_hbm(operators))

    teams = boxes // TEAM
    cut = teams * 11 // 16

    def near_piece(start, stop, tables):
        return pl.pallas_call(
            functools.partial(near_kernel, start=start, stop=stop),
            out_shape=jax.ShapeDtypeStruct((boxes, panels), F32),
            in_specs=[SMEM, VMEM, VMEM, VMEM],
            out_specs=VMEM,
            scratch_shapes=[pltpu.VMEM((boxes, 48, panels), BF16)],
            compiler_params=pltpu.CompilerParams(vmem_limit_bytes=12 * MIB),
            cost_estimate=pl.CostEstimate(
                flops=200_000_000, bytes_accessed=1_000_000, transcendentals=0
            ),
            name="near",
        )(plan, *tables)

    box = {k: lax.dynamic_index_in_dim(sent, octant ^ k, 0, keepdims=False) for k in range(n_oct)}

    def oct_step(bit):
        moving = [k for k in range(n_oct) if k & bit]
        load = jnp.concatenate([box[k] for k in moving], axis=0)
        return load, over_oct(load, bit)

    def unpack(bit, came):
        moving = [k for k in range(n_oct) if k & bit]
        rows = came.shape[0] // len(moving)
        for i, k in enumerate(moving):
            box[k] = came[i * rows : (i + 1) * rows]

    def cube_step(bit, mine):
        return jnp.concatenate([mine, over_cube(mine, bit)], axis=0)

    oct_bits = [1 << i for i in range(log2(n_oct))]
    cube_bits = [1 << i for i in range(1, log2(n_cube))]
    mine = cube_step(cube_bits[0], multipole)
    mine = after(mine, plan, sent)
    anchor = [mine]
    for bit in oct_bits[:-1]:
        load, came = oct_step(bit)
        unpack(bit, came)
        anchor.append(load)
    for bit in cube_bits[1:]:
        mine = cube_step(bit, mine)
    tables = lax.optimization_barrier((*tables, *anchor))[: len(tables)]
    first = near_piece(0, cut, tables)

    mine = after(mine, first)
    other = over_cube(mine, 1)
    for k in range(n_oct):
        box[k] = after(box[k], first) if k > 0 else box[k]
    load, came = oct_step(oct_bits[-1])
    tables = lax.optimization_barrier((*tables, mine, load))[: len(tables)]
    second = near_piece(cut, teams, tables)
    other, second, came = lax.optimization_barrier((other, second, came))
    unpack(oct_bits[-1], came)
    payloads = [box[k] for k in range(n_oct)]
    near = [first, second]

    klist = group_sources.shape[1]
    group = n_cube * boxes
    code = (group_sources ^ (me * boxes)) + group * group_patterns
    return pl.pallas_call(
        functools.partial(far_kernel, blocks=n_cube, fanin=klist, pieces=PIECES),
        out_shape=jax.ShapeDtypeStruct((boxes, panels), F32),
        in_specs=[VMEM] * (6 + PIECES + n_oct),
        out_specs=VMEM,
        scratch_shapes=[pltpu.VMEM((boxes, patterns * width), BF16)],
        compiler_params=pltpu.CompilerParams(vmem_limit_bytes=24 * MIB),
        cost_estimate=pl.CostEstimate(
            flops=3_000_000_000, bytes_accessed=2_000_000, transcendentals=0
        ),
        name="far",
    )(
        code.reshape(-1, LANES),
        counts,
        operators,
        evaluation,
        mine,
        other,
        *near,
        *payloads,
    )


def solution(mesh):
    n_oct = mesh.shape["oct"]
    n_cube = mesh.shape["cube"]

    def run(*arrays):
        return body(n_oct, n_cube, *arrays)

    return jax.shard_map(
        run,
        mesh=mesh,
        in_specs=(
            P(("oct", "cube"), None),
            P(("oct", "cube")),
            P(None, ("oct", "cube"), None),
            P(),
            P(),
            P(),
            P(("oct", "cube"), None),
            P(("oct", "cube"), None),
            P(("oct", "cube"), None),
            P("oct", "cube", None, None, None),
            P("oct", "cube", None, None, None),
            P("oct", "cube", None, None),
        ),
        out_specs=P(("oct", "cube"), None),
        check_vma=False,
    )
```

```python
import functools
import math

import jax
import jax.numpy as jnp
from jax import lax
from jax.experimental import pallas as pl
from jax.experimental.pallas import tpu as pltpu
from jax.sharding import PartitionSpec as P

F32 = jnp.float32
BF16 = jnp.bfloat16
LANES = 128
EPS = 0.0025


def iota(shape, dim):
    return lax.broadcasted_iota(jnp.int32, shape, dim)


def count_columns(cnt_ref, boxes):
    eye = iota((LANES, LANES), 0) == iota((LANES, LANES), 1)
    cols = [
        jnp.sum(jnp.where(eye, cnt_ref[i : i + 1, :], 0), axis=1, keepdims=True)
        for i in range(boxes // LANES)
    ]
    return jnp.concatenate(cols, axis=0)


def log2(value):
    return value.bit_length() - 1


def code_columns(codes):
    rows = codes.shape[0]
    padded = jnp.concatenate([codes, jnp.zeros((LANES - rows, LANES), codes.dtype)], axis=0)
    return padded.T


def onehot(local, width):
    lane = iota((LANES, LANES), 1)
    parts = [
        jnp.where(local == lane + LANES * i, 1.0, 0.0).astype(BF16) for i in range(width // LANES)
    ]
    return jnp.concatenate(parts, axis=1)


def pattern_matrix(pattern_row, eye, patterns):
    own = jnp.where(eye, jnp.broadcast_to(pattern_row, eye.shape), -1)
    parts = [jnp.where(own == p, 1.0, 0.0).astype(BF16) for p in range(patterns)]
    return jnp.concatenate(parts, axis=0)


def dot(a, b):
    return jnp.dot(a, b, preferred_element_type=F32)


def front_kernel(*refs, extra):
    strength_ref, count_ref, out_ref = refs[3 + extra : 6 + extra]
    chg_ref, cnt_ref, map_ref = refs[6 + 2 * extra : 9 + 2 * extra]
    copies = fetch(
        refs[: 3 + extra],
        (chg_ref, cnt_ref, map_ref, *refs[6 + extra : 6 + 2 * extra]),
        refs[-1],
    )
    for copy in copies[:3]:
        copy.wait()
    boxes = chg_ref.shape[0]
    live = iota((boxes, LANES), 1) < count_columns(cnt_ref, boxes)
    strength = jnp.where(live, chg_ref[...].astype(F32), 0.0)
    strength_ref[...] = strength
    count_ref[...] = cnt_ref[...]
    out_ref[...] = dot(strength.astype(BF16), map_ref[...]).astype(BF16)
    for copy in copies[3:]:
        copy.wait()


def fetch(sources, targets, sems):
    copies = [
        pltpu.make_async_copy(s, t, sems.at[i]) for i, (s, t) in enumerate(zip(sources, targets))
    ]
    for copy in copies:
        copy.start()
    return copies


def slot_stage(m_ref, src_ref, pat_ref, tgt_ref, ops_ref, out_ref, sums, operators_here):
    boxes, width = m_ref.shape
    patterns = ops_ref.shape[0] // width
    groups, fanin, slots = src_ref.shape
    rows = out_ref.shape[1]
    pack = LANES // slots
    tiles = fanin // pack
    m = m_ref[...]

    def packed(ref, d, h):
        return jnp.concatenate([ref[d, h * pack + i : h * pack + i + 1, :] for i in range(pack)], axis=1)

    sources = [packed(src_ref, d, h) for d in range(groups) for h in range(tiles)]
    cols = code_columns(jnp.concatenate(sources, axis=0))
    eye = iota((slots, LANES), 0) == (iota((slots, LANES), 1) & (slots - 1))
    for d in range(groups):
        ones = []
        pats = []
        for h in range(tiles):
            i = d * tiles + h
            ones.append(onehot(jnp.broadcast_to(cols[:, i : i + 1], (LANES, LANES)), boxes))
            pats.append(pattern_matrix(packed(pat_ref, d, h), eye, patterns))
        got = dot(jnp.concatenate(ones, axis=0), m).astype(BF16)
        s = dot(jnp.concatenate(pats, axis=1), got).astype(BF16)
        for p in range(patterns):
            sums[d * slots : (d + 1) * slots, p * width : (p + 1) * width] = s[
                p * slots : (p + 1) * slots
            ]
    operators_here.wait()
    result = dot(sums[...], ops_ref[...])
    hi = result.astype(BF16)
    lo = (result - hi.astype(F32)).astype(BF16)
    for d in range(groups):
        target = tgt_ref[d : d + 1, :].astype(F32)
        out_ref[d, 0:slots, :] = hi[d * slots : (d + 1) * slots]
        out_ref[d, slots : 2 * slots, :] = lo[d * slots : (d + 1) * slots]
        out_ref[d, 2 * slots : rows, :] = jnp.broadcast_to(
            jnp.concatenate([target, target], axis=1), (rows - 2 * slots, 2 * slots)
        ).astype(BF16)


def plan_kernel(*refs):
    cnt_ref, strength_ref, m_ref, nb_ref, pos_ref, src_ref, pat_ref, tgt_ref, ops_hbm = refs[:9]
    plan_ref, rows_ref, coords_ref, left_ref, sent_ref = refs[9:14]
    ranked, sums, ops_ref, sem = refs[14:]
    operators_here = pltpu.make_async_copy(ops_hbm, ops_ref, sem)
    operators_here.start()
    boxes = strength_ref.shape[0]
    column = count_columns(cnt_ref, boxes)
    row = jnp.concatenate([cnt_ref[i : i + 1, :] for i in range(boxes // LANES)], axis=1)
    rows_ref[1] = strength_ref[...]

    down, across = iota((boxes, boxes), 0), iota((boxes, boxes), 1)
    ahead = (column < row) | ((column == row) & (down < across))
    rank_row = jnp.sum(jnp.where(ahead, 1.0, 0.0), axis=0, keepdims=True)
    behind = (row < column) | ((row == column) & (across < down))
    rank_column = jnp.sum(jnp.where(behind, 1.0, 0.0), axis=1, keepdims=True)
    to_rank = jnp.where(rank_row == down.astype(F32), 1.0, 0.0).astype(BF16)
    from_rank = jnp.where(rank_column == across.astype(F32), 1.0, 0.0).astype(BF16)

    lists = jnp.concatenate(
        [
            nb_ref[...].astype(F32),
            row.astype(F32),
            across[0:1].astype(F32),
            jnp.zeros((16 - 2 - nb_ref.shape[0], boxes), F32),
        ],
        axis=0,
    )
    plan = dot(lists.astype(BF16), from_rank)[0:8].astype(jnp.int32)
    within = jnp.where(column <= STEP * across, 1.0, 0.0)
    ends = jnp.sum(within, axis=0, keepdims=True).astype(jnp.int32) >> log2(TEAM)
    plan_ref[...] = jnp.where(iota((8, boxes), 0) == nb_ref.shape[0] + 2, ends, plan)

    norm = jnp.zeros((boxes, LANES), F32)
    parts = []
    for c in range(3):
        u = pos_ref[c] - 1.0
        h = u.astype(BF16).astype(F32)
        m = (u - h).astype(BF16).astype(F32)
        coords_ref[2 * c] = h
        coords_ref[2 * c + 1] = m
        parts += [-2.0 * h, -2.0 * m]
        v = h + m
        norm = norm + v * v
    rows_ref[0] = norm
    n = norm + EPS
    n1 = n.astype(BF16).astype(F32)
    n2 = (n - n1).astype(BF16).astype(F32)
    parts += [n1, n2, n - n1 - n2]
    ranked[...] = dot(to_rank, jnp.concatenate([p.astype(BF16) for p in parts], axis=1))

    def build(g, carry):
        rows = pl.ds(pl.multiple_of(g * 8, 8), 8)
        f = [ranked[rows, i * LANES : (i + 1) * LANES] for i in range(9)]
        stack = []
        for c in range(3):
            stack += [f[2 * c], f[2 * c], f[2 * c + 1], f[2 * c + 1]]
        stack += f[6:9] + [jnp.zeros((8, LANES), F32)]
        left_ref[g] = jnp.concatenate(stack, axis=0).T.astype(BF16)
        return carry

    lax.fori_loop(0, boxes // 8, build, 0, unroll=4)
    slot_stage(m_ref, src_ref, pat_ref, tgt_ref, ops_ref, sent_ref, sums, operators_here)


def near_kernel(plan_ref, rows_ref, coords_ref, left_ref, out_ref, right, *, start, stop):
    boxes = out_ref.shape[0]
    knear = 4
    out_ref[...] = jnp.zeros_like(out_ref)

    def build(g, carry):
        for r in range(8):
            row = pl.ds(g * 8 + r, 1)
            for c in range(3):
                h = jnp.broadcast_to(coords_ref[2 * c, row, :], (8, LANES))
                m = jnp.broadcast_to(coords_ref[2 * c + 1, row, :], (8, LANES))
                right[g * 8 + r, 16 * c : 16 * c + 16, :] = jnp.concatenate(
                    [h, m], axis=0
                ).astype(BF16)
        return carry

    lax.fori_loop(0, boxes // 8, build, 0, unroll=4)

    ones = jnp.where(iota((32, LANES), 0) < 24, 1.0, 0.0).astype(BF16)

    def operand(box):
        x, y, z = [right[box, 16 * c : 16 * c + 16, :] for c in range(3)]
        return jnp.concatenate([x, x, y, y, z, z, ones], axis=0)

    def team(depth, g, carry):
        masks = [
            jnp.where((iota((depth, LANES), 1) & 7) == j, 1.0, 0.0).astype(BF16) for j in range(8)
        ]
        eye = iota((depth, LANES), 0) == iota((depth, LANES), 1)
        for e in range(TEAM // 8):
            turned = left_ref[g * (TEAM // 8) + e, 0:depth, :]
            for r in range(8):
                place = g * TEAM + e * 8 + r
                lhs = turned * masks[r]
                acc = None
                for k in range(0, knear, 2):
                    pair = [plan_ref[k + i, place] for i in range(2)]
                    dist = dot(lhs, jnp.concatenate([operand(b) for b in pair], axis=1))
                    for i in range(2):
                        shift = rows_ref[0, pl.ds(pair[i], 1), :]
                        q = rows_ref[1, pl.ds(pair[i], 1), :]
                        term = lax.rsqrt(dist[:, i * LANES : (i + 1) * LANES] + shift) * q
                        acc = term if acc is None else acc + term
                total = jnp.sum(acc, axis=1, keepdims=True)
                out_ref[pl.ds(plan_ref[knear + 1, place], 1), :] = jnp.sum(
                    jnp.where(eye, total, 0.0), axis=0, keepdims=True
                )
        return carry

    done = start
    for step in range(1, LANES // STEP + 1):
        until = jnp.clip(plan_ref[knear + 2, step], done, stop)
        lax.fori_loop(done, until, functools.partial(team, step * STEP), 0)
        done = until


def far_kernel(*refs, blocks, fanin, pieces):
    code_ref, cnt_ref, ops_ref, eval_ref, mine_ref, other_ref = refs[:6]
    near_refs = refs[6 : 6 + pieces]
    pay_refs = refs[6 + pieces : -2]
    out_ref, sums = refs[-2:]
    width = mine_ref.shape[1]
    boxes = mine_ref.shape[0] // (blocks // 2)
    patterns = ops_ref.shape[0] // width
    per = LANES // fanin
    tiles = code_ref.shape[0]
    span = 2 * boxes
    pages = blocks // 2
    table = jnp.concatenate(
        [
            jnp.concatenate(
                [mine_ref[j * boxes : (j + 1) * boxes], other_ref[j * boxes : (j + 1) * boxes]], axis=0
            )
            for j in range(pages)
        ],
        axis=1,
    )
    codes = code_ref[...]
    cols = code_columns(codes)
    eye = iota((per, LANES), 0) == (iota((per, LANES), 1) >> log2(fanin))
    batch = 4
    for base in range(0, tiles, batch):
        picks = [
            jnp.broadcast_to(cols[:, i : i + 1], (LANES, LANES)) for i in range(base, base + batch)
        ]
        wide = dot(jnp.concatenate([onehot(c & (span - 1), span) for c in picks], axis=0), table)
        for n in range(batch):
            i = base + n
            page = (picks[n] >> log2(span)) & (pages - 1)
            part = wide[n * LANES : (n + 1) * LANES]
            got = part[:, 0:width]
            for j in range(1, pages):
                got = jnp.where(page == j, part[:, j * width : (j + 1) * width], got)
            pat = pattern_matrix(codes[i : i + 1, :] >> log2(blocks * boxes), eye, patterns)
            s = dot(pat, got.astype(BF16)).astype(BF16)
            for p in range(patterns):
                sums[i * per : (i + 1) * per, p * width : (p + 1) * width] = s[
                    p * per : (p + 1) * per
                ]
    hits = []
    values = []
    for pay in pay_refs:
        depth = pay.shape[0] - 16
        target = pay[depth : depth + 16, :].astype(F32)[0:1]
        box = iota((boxes, depth), 0).astype(F32)
        hits.append(jnp.where(box == target, 1.0, 0.0).astype(BF16))
        values.append(pay[0:depth, :])
    remote_local = dot(jnp.concatenate(hits, axis=1), jnp.concatenate(values, axis=0))
    near = near_refs[0][...]
    for ref in near_refs[1:]:
        near = near + ref[...]
    live = iota((boxes, LANES), 1) < count_columns(cnt_ref, boxes)
    local = dot(sums[...], ops_ref[...]) + remote_local
    far = dot(local.astype(BF16), eval_ref[...])
    total = near * (1.0 / (4.0 * math.pi)) + far
    out_ref[...] = jnp.where(live, total, 0.0)


VMEM = pl.BlockSpec(memory_space=pltpu.VMEM)
HBM = pl.BlockSpec(memory_space=pltpu.HBM)
SMEM = pl.BlockSpec(memory_space=pltpu.SMEM)
MIB = 1024 * 1024


def in_hbm(value):
    return pltpu.with_memory_space_constraint(value, pltpu.HBM)


PIECES = 2
TEAM = 16
STEP = 16


def body(
    n_oct,
    n_cube,
    charges,
    panel_counts,
    positions,
    moment_map,
    translations,
    evaluation,
    near_boxes,
    group_sources,
    group_patterns,
    remote_sources,
    remote_patterns,
    remote_targets,
):
    boxes, panels = charges.shape
    width = moment_map.shape[1]
    patterns = translations.shape[0]
    operators = translations.reshape(patterns * width, width)
    counts = panel_counts.reshape(boxes // LANES, LANES)
    handed = (
        near_boxes.T,
        positions,
        remote_sources[0, 0].transpose(0, 2, 1),
        remote_patterns[0, 0].transpose(0, 2, 1),
        remote_targets[0, 0],
        evaluation,
    )
    strength, counts, multipole, *handed, evaluation = pl.pallas_call(
        functools.partial(front_kernel, extra=len(handed)),
        out_shape=(
            jax.ShapeDtypeStruct((boxes, panels), F32),
            jax.ShapeDtypeStruct(counts.shape, jnp.int32),
            jax.ShapeDtypeStruct((boxes, width), BF16),
            *[jax.ShapeDtypeStruct(v.shape, v.dtype) for v in handed],
        ),
        in_specs=[HBM] * (3 + len(handed)),
        out_specs=(VMEM,) * (3 + len(handed)),
        scratch_shapes=[pltpu.VMEM(v.shape, v.dtype) for v in (charges, counts, moment_map)]
        + [pltpu.SemaphoreType.DMA((3 + len(handed),))],
        compiler_params=pltpu.CompilerParams(vmem_limit_bytes=8 * MIB),
        cost_estimate=pl.CostEstimate(
            flops=10_000_000, bytes_accessed=300_000, transcendentals=0
        ),
        name="front",
    )(in_hbm(charges), in_hbm(counts), in_hbm(moment_map), *map(in_hbm, handed))

    me = lax.axis_index("cube")
    octant = lax.axis_index("oct")

    def over_cube(value, k):
        return lax.ppermute(value, "cube", [(i, i ^ k) for i in range(n_cube)])

    def over_oct(value, k):
        return lax.ppermute(value, "oct", [(i, i ^ k) for i in range(n_oct)])

    def after(value, *earlier):
        return lax.optimization_barrier((value, *earlier))[0]

    slots = remote_sources.shape[3]
    plan, *tables, sent = pl.pallas_call(
        plan_kernel,
        out_shape=(
            jax.ShapeDtypeStruct((8, boxes), jnp.int32),
            jax.ShapeDtypeStruct((2, boxes, panels), F32),
            jax.ShapeDtypeStruct((6, boxes, panels), F32),
            jax.ShapeDtypeStruct((boxes // 8, panels, LANES), BF16),
            jax.ShapeDtypeStruct((n_oct, 2 * slots + 16, width), BF16),
        ),
        in_specs=[VMEM] * (3 + len(handed)) + [HBM],
        out_specs=(VMEM,) * 5,
        scratch_shapes=[
            pltpu.VMEM((boxes, 9 * LANES), F32),
            pltpu.VMEM((n_oct * slots, patterns * width), BF16),
            pltpu.VMEM(operators.shape, BF16),
            pltpu.SemaphoreType.DMA,
        ],
        compiler_params=pltpu.CompilerParams(vmem_limit_bytes=16 * MIB),
        cost_estimate=pl.CostEstimate(
            flops=1_000_000_000, bytes_accessed=2_000_000, transcendentals=0
        ),
        name="plan",
    )(counts, strength, multipole, *handed, in_hbm(operators))

    teams = boxes // TEAM
    cut = teams * 11 // 16

    def near_piece(start, stop, tables):
        return pl.pallas_call(
            functools.partial(near_kernel, start=start, stop=stop),
            out_shape=jax.ShapeDtypeStruct((boxes, panels), F32),
            in_specs=[SMEM, VMEM, VMEM, VMEM],
            out_specs=VMEM,
            scratch_shapes=[pltpu.VMEM((boxes, 48, panels), BF16)],
            compiler_params=pltpu.CompilerParams(vmem_limit_bytes=12 * MIB),
            cost_estimate=pl.CostEstimate(
                flops=200_000_000, bytes_accessed=1_000_000, transcendentals=0
            ),
            name="near",
        )(plan, *tables)

    box = {k: lax.dynamic_index_in_dim(sent, octant ^ k, 0, keepdims=False) for k in range(n_oct)}

    def oct_step(bit):
        moving = [k for k in range(n_oct) if k & bit]
        load = jnp.concatenate([box[k] for k in moving], axis=0)
        return load, over_oct(load, bit)

    def unpack(bit, came):
        moving = [k for k in range(n_oct) if k & bit]
        rows = came.shape[0] // len(moving)
        for i, k in enumerate(moving):
            box[k] = came[i * rows : (i + 1) * rows]

    def cube_step(bit, mine):
        return jnp.concatenate([mine, over_cube(mine, bit)], axis=0)

    oct_bits = [1 << i for i in range(log2(n_oct))]
    cube_bits = [1 << i for i in range(1, log2(n_cube))]
    mine = cube_step(cube_bits[0], multipole)
    mine = after(mine, plan, sent)
    anchor = [mine]
    for bit in oct_bits[:-1]:
        load, came = oct_step(bit)
        unpack(bit, came)
        anchor.append(load)
    for bit in cube_bits[1:]:
        mine = cube_step(bit, mine)
    tables = lax.optimization_barrier((*tables, *anchor))[: len(tables)]
    first = near_piece(0, cut, tables)

    mine = after(mine, first)
    other = over_cube(mine, 1)
    for k in range(n_oct):
        box[k] = after(box[k], first) if k > 0 else box[k]
    load, came = oct_step(oct_bits[-1])
    tables = lax.optimization_barrier((*tables, mine, load))[: len(tables)]
    second = near_piece(cut, teams, tables)
    other, second, came = lax.optimization_barrier((other, second, came))
    unpack(oct_bits[-1], came)
    payloads = [box[k] for k in range(n_oct)]
    near = [first, second]

    klist = group_sources.shape[1]
    group = n_cube * boxes
    code = (group_sources ^ (me * boxes)) + group * group_patterns
    return pl.pallas_call(
        functools.partial(far_kernel, blocks=n_cube, fanin=klist, pieces=PIECES),
        out_shape=jax.ShapeDtypeStruct((boxes, panels), F32),
        in_specs=[VMEM] * (6 + PIECES + n_oct),
        out_specs=VMEM,
        scratch_shapes=[pltpu.VMEM((boxes, patterns * width), BF16)],
        compiler_params=pltpu.CompilerParams(vmem_limit_bytes=24 * MIB),
        cost_estimate=pl.CostEstimate(
            flops=3_000_000_000, bytes_accessed=2_000_000, transcendentals=0
        ),
        name="far",
    )(
        code.reshape(-1, LANES),
        counts,
        operators,
        evaluation,
        mine,
        other,
        *near,
        *payloads,
    )


def solution(mesh):
    n_oct = mesh.shape["oct"]
    n_cube = mesh.shape["cube"]

    def run(*arrays):
        return body(n_oct, n_cube, *arrays)

    return jax.shard_map(
        run,
        mesh=mesh,
        in_specs=(
            P(("oct", "cube"), None),
            P(("oct", "cube")),
            P(None, ("oct", "cube"), None),
            P(),
            P(),
            P(),
            P(("oct", "cube"), None),
            P(("oct", "cube"), None),
            P(("oct", "cube"), None),
            P("oct", "cube", None, None, None),
            P("oct", "cube", None, None, None),
            P("oct", "cube", None, None),
        ),
        out_specs=P(("oct", "cube"), None),
        check_vma=False,
    )
```

```python
import functools
import math

import jax
import jax.numpy as jnp
from jax import lax
from jax.experimental import pallas as pl
from jax.experimental.pallas import tpu as pltpu
from jax.sharding import PartitionSpec as P

F32 = jnp.float32
BF16 = jnp.bfloat16
LANES = 128
EPS = 0.0025


def iota(shape, dim):
    return lax.broadcasted_iota(jnp.int32, shape, dim)


def count_columns(cnt_ref, boxes):
    eye = iota((LANES, LANES), 0) == iota((LANES, LANES), 1)
    cols = [
        jnp.sum(jnp.where(eye, cnt_ref[i : i + 1, :], 0), axis=1, keepdims=True)
        for i in range(boxes // LANES)
    ]
    return jnp.concatenate(cols, axis=0)


def log2(value):
    return value.bit_length() - 1


def code_columns(codes):
    rows = codes.shape[0]
    padded = jnp.concatenate([codes, jnp.zeros((LANES - rows, LANES), codes.dtype)], axis=0)
    return padded.T


def onehot(local, width):
    lane = iota((LANES, LANES), 1)
    parts = [
        jnp.where(local == lane + LANES * i, 1.0, 0.0).astype(BF16) for i in range(width // LANES)
    ]
    return jnp.concatenate(parts, axis=1)


def pattern_matrix(pattern_row, eye, patterns):
    own = jnp.where(eye, jnp.broadcast_to(pattern_row, eye.shape), -1)
    parts = [jnp.where(own == p, 1.0, 0.0).astype(BF16) for p in range(patterns)]
    return jnp.concatenate(parts, axis=0)


def dot(a, b):
    return jnp.dot(a, b, preferred_element_type=F32)


def front_kernel(*refs, extra):
    strength_ref, count_ref, out_ref = refs[3 + extra : 6 + extra]
    chg_ref, cnt_ref, map_ref = refs[6 + 2 * extra : 9 + 2 * extra]
    copies = fetch(
        refs[: 3 + extra],
        (chg_ref, cnt_ref, map_ref, *refs[6 + extra : 6 + 2 * extra]),
        refs[-1],
    )
    for copy in copies[:3]:
        copy.wait()
    boxes = chg_ref.shape[0]
    live = iota((boxes, LANES), 1) < count_columns(cnt_ref, boxes)
    strength = jnp.where(live, chg_ref[...].astype(F32), 0.0)
    strength_ref[...] = strength
    count_ref[...] = cnt_ref[...]
    out_ref[...] = dot(strength.astype(BF16), map_ref[...]).astype(BF16)
    for copy in copies[3:]:
        copy.wait()


def fetch(sources, targets, sems):
    copies = [
        pltpu.make_async_copy(s, t, sems.at[i]) for i, (s, t) in enumerate(zip(sources, targets))
    ]
    for copy in copies:
        copy.start()
    return copies


def slot_stage(m_ref, src_ref, pat_ref, tgt_ref, ops_ref, out_ref, sums, operators_here):
    boxes, width = m_ref.shape
    patterns = ops_ref.shape[0] // width
    groups, fanin, slots = src_ref.shape
    rows = out_ref.shape[1]
    pack = LANES // slots
    tiles = fanin // pack
    m = m_ref[...]

    def packed(ref, d, h):
        return jnp.concatenate([ref[d, h * pack + i : h * pack + i + 1, :] for i in range(pack)], axis=1)

    sources = [packed(src_ref, d, h) for d in range(groups) for h in range(tiles)]
    cols = code_columns(jnp.concatenate(sources, axis=0))
    eye = iota((slots, LANES), 0) == (iota((slots, LANES), 1) & (slots - 1))
    for d in range(groups):
        ones = []
        pats = []
        for h in range(tiles):
            i = d * tiles + h
            ones.append(onehot(jnp.broadcast_to(cols[:, i : i + 1], (LANES, LANES)), boxes))
            pats.append(pattern_matrix(packed(pat_ref, d, h), eye, patterns))
        got = dot(jnp.concatenate(ones, axis=0), m).astype(BF16)
        s = dot(jnp.concatenate(pats, axis=1), got).astype(BF16)
        for p in range(patterns):
            sums[d * slots : (d + 1) * slots, p * width : (p + 1) * width] = s[
                p * slots : (p + 1) * slots
            ]
    operators_here.wait()
    result = dot(sums[...], ops_ref[...])
    hi = result.astype(BF16)
    lo = (result - hi.astype(F32)).astype(BF16)
    for d in range(groups):
        target = tgt_ref[d : d + 1, :].astype(F32)
        out_ref[d, 0:slots, :] = hi[d * slots : (d + 1) * slots]
        out_ref[d, slots : 2 * slots, :] = lo[d * slots : (d + 1) * slots]
        out_ref[d, 2 * slots : rows, :] = jnp.broadcast_to(
            jnp.concatenate([target, target], axis=1), (rows - 2 * slots, 2 * slots)
        ).astype(BF16)


def plan_kernel(*refs):
    cnt_ref, strength_ref, m_ref, nb_ref, pos_ref, src_ref, pat_ref, tgt_ref, ops_hbm = refs[:9]
    plan_ref, rows_ref, coords_ref, left_ref, sent_ref = refs[9:14]
    ranked, sums, ops_ref, sem = refs[14:]
    operators_here = pltpu.make_async_copy(ops_hbm, ops_ref, sem)
    operators_here.start()
    boxes = strength_ref.shape[0]
    column = count_columns(cnt_ref, boxes)
    row = jnp.concatenate([cnt_ref[i : i + 1, :] for i in range(boxes // LANES)], axis=1)
    rows_ref[1] = strength_ref[...]

    down, across = iota((boxes, boxes), 0), iota((boxes, boxes), 1)
    ahead = (column < row) | ((column == row) & (down < across))
    rank_row = jnp.sum(jnp.where(ahead, 1.0, 0.0), axis=0, keepdims=True)
    behind = (row < column) | ((row == column) & (across < down))
    rank_column = jnp.sum(jnp.where(behind, 1.0, 0.0), axis=1, keepdims=True)
    to_rank = jnp.where(rank_row == down.astype(F32), 1.0, 0.0).astype(BF16)
    from_rank = jnp.where(rank_column == across.astype(F32), 1.0, 0.0).astype(BF16)

    lists = jnp.concatenate(
        [
            nb_ref[...].astype(F32),
            row.astype(F32),
            across[0:1].astype(F32),
            jnp.zeros((16 - 2 - nb_ref.shape[0], boxes), F32),
        ],
        axis=0,
    )
    plan = dot(lists.astype(BF16), from_rank)[0:8].astype(jnp.int32)
    within = jnp.where(column <= STEP * across, 1.0, 0.0)
    ends = jnp.sum(within, axis=0, keepdims=True).astype(jnp.int32) >> log2(TEAM)
    plan_ref[...] = jnp.where(iota((8, boxes), 0) == nb_ref.shape[0] + 2, ends, plan)

    norm = jnp.zeros((boxes, LANES), F32)
    parts = []
    for c in range(3):
        u = pos_ref[c] - 1.0
        h = u.astype(BF16).astype(F32)
        m = (u - h).astype(BF16).astype(F32)
        coords_ref[2 * c] = h
        coords_ref[2 * c + 1] = m
        parts += [-2.0 * h, -2.0 * m]
        v = h + m
        norm = norm + v * v
    rows_ref[0] = norm
    n = norm + EPS
    n1 = n.astype(BF16).astype(F32)
    n2 = (n - n1).astype(BF16).astype(F32)
    parts += [n1, n2, n - n1 - n2]
    ranked[...] = dot(to_rank, jnp.concatenate([p.astype(BF16) for p in parts], axis=1))

    def build(g, carry):
        rows = pl.ds(pl.multiple_of(g * 8, 8), 8)
        f = [ranked[rows, i * LANES : (i + 1) * LANES] for i in range(9)]
        stack = []
        for c in range(3):
            stack += [f[2 * c], f[2 * c], f[2 * c + 1], f[2 * c + 1]]
        stack += f[6:9] + [jnp.zeros((8, LANES), F32)]
        left_ref[g] = jnp.concatenate(stack, axis=0).T.astype(BF16)
        return carry

    lax.fori_loop(0, boxes // 8, build, 0, unroll=4)
    slot_stage(m_ref, src_ref, pat_ref, tgt_ref, ops_ref, sent_ref, sums, operators_here)


def near_kernel(plan_ref, rows_ref, coords_ref, left_ref, out_ref, right, *, start, stop):
    boxes = out_ref.shape[0]
    knear = 4
    out_ref[...] = jnp.zeros_like(out_ref)

    zero8 = jnp.zeros((8, LANES), F32)

    def build(g, carry):
        n = rows_ref[0, pl.ds(pl.multiple_of(g * 8, 8), 8), :]
        n1 = n.astype(BF16).astype(F32)
        n2 = (n - n1).astype(BF16).astype(F32)
        norms = [n1, n2, n - n1 - n2]
        for r in range(8):
            row = pl.ds(g * 8 + r, 1)
            wide = [jnp.broadcast_to(coords_ref[f, row, :], (8, LANES)) for f in range(6)]
            wide += [jnp.broadcast_to(v[r : r + 1], (8, LANES)) for v in norms] + [zero8]
            for i in range(5):
                right[g * 8 + r, 16 * i : 16 * i + 16, :] = jnp.concatenate(
                    wide[2 * i : 2 * i + 2], axis=0
                ).astype(BF16)
        return carry

    lax.fori_loop(0, boxes // 8, build, 0, unroll=4)

    ones = jnp.where(iota((32, LANES), 0) < 24, 1.0, 0.0).astype(BF16)

    none = jnp.zeros((96, LANES), BF16)

    def operand(box):
        x, y, z, n, t = [right[box, 16 * c : 16 * c + 16, :] for c in range(5)]
        return jnp.concatenate([x, x, y, y, z, z, ones, n, t, none], axis=0)

    def team(depth, g, carry):
        masks = [
            jnp.where((iota((depth, LANES), 1) & 7) == j, 1.0, 0.0).astype(BF16) for j in range(8)
        ]
        lane = iota((depth, LANES), 1)
        units = [
            jnp.where(((lane & 7) == j) & (lane < 24), 1.0, 0.0).astype(BF16) for j in range(8)
        ]
        eye = iota((depth, LANES), 0) == lane
        for e in range(TEAM // 8):
            turned = left_ref[g * (TEAM // 8) + e, 0:depth, :]
            for r in range(8):
                place = g * TEAM + e * 8 + r
                lhs = jnp.concatenate([turned * masks[r], units[r]], axis=1)
                acc = None
                for k in range(0, knear, 2):
                    pair = [plan_ref[k + i, place] for i in range(2)]
                    dist = dot(lhs, jnp.concatenate([operand(b) for b in pair], axis=1))
                    for i in range(2):
                        q = rows_ref[1, pl.ds(pair[i], 1), :]
                        term = lax.rsqrt(dist[:, i * LANES : (i + 1) * LANES]) * q
                        acc = term if acc is None else acc + term
                total = jnp.sum(acc, axis=1, keepdims=True)
                out_ref[pl.ds(plan_ref[knear + 1, place], 1), :] = jnp.sum(
                    jnp.where(eye, total, 0.0), axis=0, keepdims=True
                )
        return carry

    done = start
    for step in range(1, LANES // STEP + 1):
        until = jnp.clip(plan_ref[knear + 2, step], done, stop)
        lax.fori_loop(done, until, functools.partial(team, step * STEP), 0)
        done = until


def far_kernel(*refs, blocks, fanin, pieces):
    code_ref, cnt_ref, ops_ref, eval_ref, mine_ref, other_ref = refs[:6]
    near_refs = refs[6 : 6 + pieces]
    pay_refs = refs[6 + pieces : -2]
    out_ref, sums = refs[-2:]
    width = mine_ref.shape[1]
    boxes = mine_ref.shape[0] // (blocks // 2)
    patterns = ops_ref.shape[0] // width
    per = LANES // fanin
    tiles = code_ref.shape[0]
    span = 2 * boxes
    pages = blocks // 2
    table = jnp.concatenate(
        [
            jnp.concatenate(
                [mine_ref[j * boxes : (j + 1) * boxes], other_ref[j * boxes : (j + 1) * boxes]], axis=0
            )
            for j in range(pages)
        ],
        axis=1,
    )
    codes = code_ref[...]
    cols = code_columns(codes)
    eye = iota((per, LANES), 0) == (iota((per, LANES), 1) >> log2(fanin))
    batch = 4
    for base in range(0, tiles, batch):
        picks = [
            jnp.broadcast_to(cols[:, i : i + 1], (LANES, LANES)) for i in range(base, base + batch)
        ]
        wide = dot(jnp.concatenate([onehot(c & (span - 1), span) for c in picks], axis=0), table)
        for n in range(batch):
            i = base + n
            page = (picks[n] >> log2(span)) & (pages - 1)
            part = wide[n * LANES : (n + 1) * LANES]
            got = part[:, 0:width]
            for j in range(1, pages):
                got = jnp.where(page == j, part[:, j * width : (j + 1) * width], got)
            pat = pattern_matrix(codes[i : i + 1, :] >> log2(blocks * boxes), eye, patterns)
            s = dot(pat, got.astype(BF16)).astype(BF16)
            for p in range(patterns):
                sums[i * per : (i + 1) * per, p * width : (p + 1) * width] = s[
                    p * per : (p + 1) * per
                ]
    hits = []
    values = []
    for pay in pay_refs:
        depth = pay.shape[0] - 16
        target = pay[depth : depth + 16, :].astype(F32)[0:1]
        box = iota((boxes, depth), 0).astype(F32)
        hits.append(jnp.where(box == target, 1.0, 0.0).astype(BF16))
        values.append(pay[0:depth, :])
    remote_local = dot(jnp.concatenate(hits, axis=1), jnp.concatenate(values, axis=0))
    near = near_refs[0][...]
    for ref in near_refs[1:]:
        near = near + ref[...]
    live = iota((boxes, LANES), 1) < count_columns(cnt_ref, boxes)
    local = dot(sums[...], ops_ref[...]) + remote_local
    far = dot(local.astype(BF16), eval_ref[...])
    total = near * (1.0 / (4.0 * math.pi)) + far
    out_ref[...] = jnp.where(live, total, 0.0)


VMEM = pl.BlockSpec(memory_space=pltpu.VMEM)
HBM = pl.BlockSpec(memory_space=pltpu.HBM)
SMEM = pl.BlockSpec(memory_space=pltpu.SMEM)
MIB = 1024 * 1024


def in_hbm(value):
    return pltpu.with_memory_space_constraint(value, pltpu.HBM)


PIECES = 2
TEAM = 16
STEP = 16


def body(
    n_oct,
    n_cube,
    charges,
    panel_counts,
    positions,
    moment_map,
    translations,
    evaluation,
    near_boxes,
    group_sources,
    group_patterns,
    remote_sources,
    remote_patterns,
    remote_targets,
):
    boxes, panels = charges.shape
    width = moment_map.shape[1]
    patterns = translations.shape[0]
    operators = translations.reshape(patterns * width, width)
    counts = panel_counts.reshape(boxes // LANES, LANES)
    handed = (
        near_boxes.T,
        positions,
        remote_sources[0, 0].transpose(0, 2, 1),
        remote_patterns[0, 0].transpose(0, 2, 1),
        remote_targets[0, 0],
        evaluation,
    )
    strength, counts, multipole, *handed, evaluation = pl.pallas_call(
        functools.partial(front_kernel, extra=len(handed)),
        out_shape=(
            jax.ShapeDtypeStruct((boxes, panels), F32),
            jax.ShapeDtypeStruct(counts.shape, jnp.int32),
            jax.ShapeDtypeStruct((boxes, width), BF16),
            *[jax.ShapeDtypeStruct(v.shape, v.dtype) for v in handed],
        ),
        in_specs=[HBM] * (3 + len(handed)),
        out_specs=(VMEM,) * (3 + len(handed)),
        scratch_shapes=[pltpu.VMEM(v.shape, v.dtype) for v in (charges, counts, moment_map)]
        + [pltpu.SemaphoreType.DMA((3 + len(handed),))],
        compiler_params=pltpu.CompilerParams(vmem_limit_bytes=8 * MIB),
        cost_estimate=pl.CostEstimate(
            flops=10_000_000, bytes_accessed=300_000, transcendentals=0
        ),
        name="front",
    )(in_hbm(charges), in_hbm(counts), in_hbm(moment_map), *map(in_hbm, handed))

    me = lax.axis_index("cube")
    octant = lax.axis_index("oct")

    def over_cube(value, k):
        return lax.ppermute(value, "cube", [(i, i ^ k) for i in range(n_cube)])

    def over_oct(value, k):
        return lax.ppermute(value, "oct", [(i, i ^ k) for i in range(n_oct)])

    def after(value, *earlier):
        return lax.optimization_barrier((value, *earlier))[0]

    slots = remote_sources.shape[3]
    plan, *tables, sent = pl.pallas_call(
        plan_kernel,
        out_shape=(
            jax.ShapeDtypeStruct((8, boxes), jnp.int32),
            jax.ShapeDtypeStruct((2, boxes, panels), F32),
            jax.ShapeDtypeStruct((6, boxes, panels), F32),
            jax.ShapeDtypeStruct((boxes // 8, panels, LANES), BF16),
            jax.ShapeDtypeStruct((n_oct, 2 * slots + 16, width), BF16),
        ),
        in_specs=[VMEM] * (3 + len(handed)) + [HBM],
        out_specs=(VMEM,) * 5,
        scratch_shapes=[
            pltpu.VMEM((boxes, 9 * LANES), F32),
            pltpu.VMEM((n_oct * slots, patterns * width), BF16),
            pltpu.VMEM(operators.shape, BF16),
            pltpu.SemaphoreType.DMA,
        ],
        compiler_params=pltpu.CompilerParams(vmem_limit_bytes=16 * MIB),
        cost_estimate=pl.CostEstimate(
            flops=1_000_000_000, bytes_accessed=2_000_000, transcendentals=0
        ),
        name="plan",
    )(counts, strength, multipole, *handed, in_hbm(operators))

    teams = boxes // TEAM
    cut = teams * 11 // 16

    def near_piece(start, stop, tables):
        return pl.pallas_call(
            functools.partial(near_kernel, start=start, stop=stop),
            out_shape=jax.ShapeDtypeStruct((boxes, panels), F32),
            in_specs=[SMEM, VMEM, VMEM, VMEM],
            out_specs=VMEM,
            scratch_shapes=[pltpu.VMEM((boxes, 80, panels), BF16)],
            compiler_params=pltpu.CompilerParams(vmem_limit_bytes=12 * MIB),
            cost_estimate=pl.CostEstimate(
                flops=200_000_000, bytes_accessed=1_000_000, transcendentals=0
            ),
            name="near",
        )(plan, *tables)

    box = {k: lax.dynamic_index_in_dim(sent, octant ^ k, 0, keepdims=False) for k in range(n_oct)}

    def oct_step(bit):
        moving = [k for k in range(n_oct) if k & bit]
        load = jnp.concatenate([box[k] for k in moving], axis=0)
        return load, over_oct(load, bit)

    def unpack(bit, came):
        moving = [k for k in range(n_oct) if k & bit]
        rows = came.shape[0] // len(moving)
        for i, k in enumerate(moving):
            box[k] = came[i * rows : (i + 1) * rows]

    def cube_step(bit, mine):
        return jnp.concatenate([mine, over_cube(mine, bit)], axis=0)

    oct_bits = [1 << i for i in range(log2(n_oct))]
    cube_bits = [1 << i for i in range(1, log2(n_cube))]
    mine = cube_step(cube_bits[0], multipole)
    mine = after(mine, plan, sent)
    anchor = [mine]
    for bit in oct_bits[:-1]:
        load, came = oct_step(bit)
        unpack(bit, came)
        anchor.append(load)
    for bit in cube_bits[1:]:
        mine = cube_step(bit, mine)
    tables = lax.optimization_barrier((*tables, *anchor))[: len(tables)]
    first = near_piece(0, cut, tables)

    mine = after(mine, first)
    other = over_cube(mine, 1)
    for k in range(n_oct):
        box[k] = after(box[k], first) if k > 0 else box[k]
    load, came = oct_step(oct_bits[-1])
    tables = lax.optimization_barrier((*tables, mine, load))[: len(tables)]
    second = near_piece(cut, teams, tables)
    other, second, came = lax.optimization_barrier((other, second, came))
    unpack(oct_bits[-1], came)
    payloads = [box[k] for k in range(n_oct)]
    near = [first, second]

    klist = group_sources.shape[1]
    group = n_cube * boxes
    code = (group_sources ^ (me * boxes)) + group * group_patterns
    return pl.pallas_call(
        functools.partial(far_kernel, blocks=n_cube, fanin=klist, pieces=PIECES),
        out_shape=jax.ShapeDtypeStruct((boxes, panels), F32),
        in_specs=[VMEM] * (6 + PIECES + n_oct),
        out_specs=VMEM,
        scratch_shapes=[pltpu.VMEM((boxes, patterns * width), BF16)],
        compiler_params=pltpu.CompilerParams(vmem_limit_bytes=24 * MIB),
        cost_estimate=pl.CostEstimate(
            flops=3_000_000_000, bytes_accessed=2_000_000, transcendentals=0
        ),
        name="far",
    )(
        code.reshape(-1, LANES),
        counts,
        operators,
        evaluation,
        mine,
        other,
        *near,
        *payloads,
    )


def solution(mesh):
    n_oct = mesh.shape["oct"]
    n_cube = mesh.shape["cube"]

    def run(*arrays):
        return body(n_oct, n_cube, *arrays)

    return jax.shard_map(
        run,
        mesh=mesh,
        in_specs=(
            P(("oct", "cube"), None),
            P(("oct", "cube")),
            P(None, ("oct", "cube"), None),
            P(),
            P(),
            P(),
            P(("oct", "cube"), None),
            P(("oct", "cube"), None),
            P(("oct", "cube"), None),
            P("oct", "cube", None, None, None),
            P("oct", "cube", None, None, None),
            P("oct", "cube", None, None),
        ),
        out_specs=P(("oct", "cube"), None),
        check_vma=False,
    )
```

```python
import functools
import math

import jax
import jax.numpy as jnp
from jax import lax
from jax.experimental import pallas as pl
from jax.experimental.pallas import tpu as pltpu
from jax.sharding import PartitionSpec as P

F32 = jnp.float32
BF16 = jnp.bfloat16
LANES = 128
EPS = 0.0025


def iota(shape, dim):
    return lax.broadcasted_iota(jnp.int32, shape, dim)


def count_columns(cnt_ref, boxes):
    eye = iota((LANES, LANES), 0) == iota((LANES, LANES), 1)
    cols = [
        jnp.sum(jnp.where(eye, cnt_ref[i : i + 1, :], 0), axis=1, keepdims=True)
        for i in range(boxes // LANES)
    ]
    return jnp.concatenate(cols, axis=0)


def log2(value):
    return value.bit_length() - 1


def code_columns(codes):
    rows = codes.shape[0]
    padded = jnp.concatenate([codes, jnp.zeros((LANES - rows, LANES), codes.dtype)], axis=0)
    return padded.T


def onehot(local, width):
    lane = iota((LANES, LANES), 1)
    parts = [
        jnp.where(local == lane + LANES * i, 1.0, 0.0).astype(BF16) for i in range(width // LANES)
    ]
    return jnp.concatenate(parts, axis=1)


def pattern_matrix(pattern_row, eye, patterns):
    own = jnp.where(eye, jnp.broadcast_to(pattern_row, eye.shape), -1)
    parts = [jnp.where(own == p, 1.0, 0.0).astype(BF16) for p in range(patterns)]
    return jnp.concatenate(parts, axis=0)


def dot(a, b):
    return jnp.dot(a, b, preferred_element_type=F32)


def front_kernel(*refs, extra):
    strength_ref, count_ref, out_ref = refs[3 + extra : 6 + extra]
    chg_ref, cnt_ref, map_ref = refs[6 + 2 * extra : 9 + 2 * extra]
    copies = fetch(
        refs[: 3 + extra],
        (chg_ref, cnt_ref, map_ref, *refs[6 + extra : 6 + 2 * extra]),
        refs[-1],
    )
    for copy in copies[:3]:
        copy.wait()
    boxes = chg_ref.shape[0]
    live = iota((boxes, LANES), 1) < count_columns(cnt_ref, boxes)
    strength = jnp.where(live, chg_ref[...].astype(F32), 0.0)
    strength_ref[...] = strength
    count_ref[...] = cnt_ref[...]
    out_ref[...] = dot(strength.astype(BF16), map_ref[...]).astype(BF16)
    for copy in copies[3:]:
        copy.wait()


def fetch(sources, targets, sems):
    copies = [
        pltpu.make_async_copy(s, t, sems.at[i]) for i, (s, t) in enumerate(zip(sources, targets))
    ]
    for copy in copies:
        copy.start()
    return copies


def slot_stage(m_ref, src_ref, pat_ref, tgt_ref, ops_ref, out_ref, sums, operators_here):
    boxes, width = m_ref.shape
    patterns = ops_ref.shape[0] // width
    groups, fanin, slots = src_ref.shape
    rows = out_ref.shape[1]
    pack = LANES // slots
    tiles = fanin // pack
    m = m_ref[...]

    def packed(ref, d, h):
        return jnp.concatenate([ref[d, h * pack + i : h * pack + i + 1, :] for i in range(pack)], axis=1)

    sources = [packed(src_ref, d, h) for d in range(groups) for h in range(tiles)]
    cols = code_columns(jnp.concatenate(sources, axis=0))
    eye = iota((slots, LANES), 0) == (iota((slots, LANES), 1) & (slots - 1))
    for d in range(groups):
        ones = []
        pats = []
        for h in range(tiles):
            i = d * tiles + h
            ones.append(onehot(jnp.broadcast_to(cols[:, i : i + 1], (LANES, LANES)), boxes))
            pats.append(pattern_matrix(packed(pat_ref, d, h), eye, patterns))
        got = dot(jnp.concatenate(ones, axis=0), m).astype(BF16)
        s = dot(jnp.concatenate(pats, axis=1), got).astype(BF16)
        for p in range(patterns):
            sums[d * slots : (d + 1) * slots, p * width : (p + 1) * width] = s[
                p * slots : (p + 1) * slots
            ]
    operators_here.wait()
    result = dot(sums[...], ops_ref[...])
    hi = result.astype(BF16)
    lo = (result - hi.astype(F32)).astype(BF16)
    for d in range(groups):
        target = tgt_ref[d : d + 1, :].astype(F32)
        out_ref[d, 0:slots, :] = hi[d * slots : (d + 1) * slots]
        out_ref[d, slots : 2 * slots, :] = lo[d * slots : (d + 1) * slots]
        out_ref[d, 2 * slots : rows, :] = jnp.broadcast_to(
            jnp.concatenate([target, target], axis=1), (rows - 2 * slots, 2 * slots)
        ).astype(BF16)


def plan_kernel(*refs):
    cnt_ref, strength_ref, m_ref, nb_ref, pos_ref, src_ref, pat_ref, tgt_ref, ops_hbm = refs[:9]
    plan_ref, rows_ref, coords_ref, left_ref, sent_ref = refs[9:14]
    ranked, sums, ops_ref, sem = refs[14:]
    operators_here = pltpu.make_async_copy(ops_hbm, ops_ref, sem)
    operators_here.start()
    boxes = strength_ref.shape[0]
    column = count_columns(cnt_ref, boxes)
    row = jnp.concatenate([cnt_ref[i : i + 1, :] for i in range(boxes // LANES)], axis=1)
    rows_ref[1] = strength_ref[...]

    down, across = iota((boxes, boxes), 0), iota((boxes, boxes), 1)
    ahead = (column < row) | ((column == row) & (down < across))
    rank_row = jnp.sum(jnp.where(ahead, 1.0, 0.0), axis=0, keepdims=True)
    behind = (row < column) | ((row == column) & (across < down))
    rank_column = jnp.sum(jnp.where(behind, 1.0, 0.0), axis=1, keepdims=True)
    to_rank = jnp.where(rank_row == down.astype(F32), 1.0, 0.0).astype(BF16)
    from_rank = jnp.where(rank_column == across.astype(F32), 1.0, 0.0).astype(BF16)

    lists = jnp.concatenate(
        [
            nb_ref[...].astype(F32),
            row.astype(F32),
            across[0:1].astype(F32),
            jnp.zeros((16 - 2 - nb_ref.shape[0], boxes), F32),
        ],
        axis=0,
    )
    plan = dot(lists.astype(BF16), from_rank)[0:8].astype(jnp.int32)
    within = jnp.where(column <= STEP * across, 1.0, 0.0)
    ends = jnp.sum(within, axis=0, keepdims=True).astype(jnp.int32) >> log2(TEAM)
    plan_ref[...] = jnp.where(iota((8, boxes), 0) == nb_ref.shape[0] + 2, ends, plan)

    norm = jnp.zeros((boxes, LANES), F32)
    parts = []
    for c in range(3):
        u = pos_ref[c] - 1.0
        h = u.astype(BF16).astype(F32)
        m = (u - h).astype(BF16).astype(F32)
        coords_ref[2 * c] = h
        coords_ref[2 * c + 1] = m
        parts += [-2.0 * h, -2.0 * m]
        v = h + m
        norm = norm + v * v
    rows_ref[0] = norm
    n = norm + EPS
    n1 = n.astype(BF16).astype(F32)
    n2 = (n - n1).astype(BF16).astype(F32)
    parts += [n1, n2, n - n1 - n2]
    ranked[...] = dot(to_rank, jnp.concatenate([p.astype(BF16) for p in parts], axis=1))

    def build(g, carry):
        rows = pl.ds(pl.multiple_of(g * 8, 8), 8)
        f = [ranked[rows, i * LANES : (i + 1) * LANES] for i in range(9)]
        stack = []
        for c in range(3):
            stack += [f[2 * c], f[2 * c], f[2 * c + 1], f[2 * c + 1]]
        stack += f[6:9] + [jnp.zeros((8, LANES), F32)]
        left_ref[g] = jnp.concatenate(stack, axis=0).T.astype(BF16)
        return carry

    lax.fori_loop(0, boxes // 8, build, 0, unroll=4)
    slot_stage(m_ref, src_ref, pat_ref, tgt_ref, ops_ref, sent_ref, sums, operators_here)


def near_kernel(plan_ref, rows_ref, coords_ref, left_ref, out_ref, right, *, start, stop):
    boxes = out_ref.shape[0]
    knear = 4
    out_ref[...] = jnp.zeros_like(out_ref)

    def build(g, carry):
        for r in range(8):
            row = pl.ds(g * 8 + r, 1)
            for c in range(3):
                h = jnp.broadcast_to(coords_ref[2 * c, row, :], (8, LANES))
                m = jnp.broadcast_to(coords_ref[2 * c + 1, row, :], (8, LANES))
                right[g * 8 + r, 16 * c : 16 * c + 16, :] = jnp.concatenate(
                    [h, m], axis=0
                ).astype(BF16)
        return carry

    lax.fori_loop(0, boxes // 8, build, 0, unroll=4)

    ones = jnp.where(iota((32, LANES), 0) < 24, 1.0, 0.0).astype(BF16)

    def operand(box):
        x, y, z = [right[box, 16 * c : 16 * c + 16, :] for c in range(3)]
        return jnp.concatenate([x, x, y, y, z, z, ones], axis=0)

    def team(depth, g, carry):
        masks = [
            jnp.where((iota((depth, LANES), 1) & 7) == j, 1.0, 0.0).astype(BF16) for j in range(8)
        ]
        eye = iota((depth, LANES), 0) == iota((depth, LANES), 1)
        for e in range(TEAM // 8):
            turned = left_ref[g * (TEAM // 8) + e, 0:depth, :]
            for r in range(8):
                place = g * TEAM + e * 8 + r
                lhs = turned * masks[r]
                acc = None
                for k in range(0, knear, 2):
                    pair = [plan_ref[k + i, place] for i in range(2)]
                    dist = dot(lhs, jnp.concatenate([operand(b) for b in pair], axis=1))
                    for i in range(2):
                        shift = rows_ref[0, pl.ds(pair[i], 1), :]
                        q = rows_ref[1, pl.ds(pair[i], 1), :]
                        term = lax.rsqrt(dist[:, i * LANES : (i + 1) * LANES] + shift) * q
                        acc = term if acc is None else acc + term
                total = jnp.sum(acc, axis=1, keepdims=True)
                out_ref[pl.ds(plan_ref[knear + 1, place], 1), :] = jnp.sum(
                    jnp.where(eye, total, 0.0), axis=0, keepdims=True
                )
        return carry

    done = start
    for step in range(1, LANES // STEP + 1):
        until = jnp.clip(plan_ref[knear + 2, step], done, stop)
        lax.fori_loop(done, until, functools.partial(team, step * STEP), 0)
        done = until


def far_kernel(*refs, blocks, fanin, pieces):
    code_ref, cnt_ref, ops_ref, eval_ref, mine_ref, other_ref = refs[:6]
    near_refs = refs[6 : 6 + pieces]
    pay_refs = refs[6 + pieces : -2]
    out_ref, sums = refs[-2:]
    width = mine_ref.shape[1]
    boxes = mine_ref.shape[0] // (blocks // 2)
    patterns = ops_ref.shape[0] // width
    per = LANES // fanin
    tiles = code_ref.shape[0]
    span = 2 * boxes
    pages = blocks // 2
    table = jnp.concatenate(
        [
            jnp.concatenate(
                [mine_ref[j * boxes : (j + 1) * boxes], other_ref[j * boxes : (j + 1) * boxes]], axis=0
            )
            for j in range(pages)
        ],
        axis=1,
    )
    codes = code_ref[...]
    cols = code_columns(codes)
    eye = iota((per, LANES), 0) == (iota((per, LANES), 1) >> log2(fanin))
    batch = 4
    for base in range(0, tiles, batch):
        picks = [
            jnp.broadcast_to(cols[:, i : i + 1], (LANES, LANES)) for i in range(base, base + batch)
        ]
        wide = dot(jnp.concatenate([onehot(c & (span - 1), span) for c in picks], axis=0), table)
        for n in range(batch):
            i = base + n
            page = (picks[n] >> log2(span)) & (pages - 1)
            part = wide[n * LANES : (n + 1) * LANES]
            got = part[:, 0:width]
            for j in range(1, pages):
                got = jnp.where(page == j, part[:, j * width : (j + 1) * width], got)
            pat = pattern_matrix(codes[i : i + 1, :] >> log2(blocks * boxes), eye, patterns)
            s = dot(pat, got.astype(BF16)).astype(BF16)
            for p in range(patterns):
                sums[i * per : (i + 1) * per, p * width : (p + 1) * width] = s[
                    p * per : (p + 1) * per
                ]
    hits = []
    values = []
    for pay in pay_refs:
        depth = pay.shape[0] - 16
        target = pay[depth : depth + 16, :].astype(F32)[0:1]
        box = iota((boxes, depth), 0).astype(F32)
        hits.append(jnp.where(box == target, 1.0, 0.0).astype(BF16))
        values.append(pay[0:depth, :])
    remote_local = dot(jnp.concatenate(hits, axis=1), jnp.concatenate(values, axis=0))
    near = near_refs[0][...]
    for ref in near_refs[1:]:
        near = near + ref[...]
    live = iota((boxes, LANES), 1) < count_columns(cnt_ref, boxes)
    local = dot(sums[...], ops_ref[...]) + remote_local
    far = dot(local.astype(BF16), eval_ref[...])
    total = near * (1.0 / (4.0 * math.pi)) + far
    out_ref[...] = jnp.where(live, total, 0.0)


VMEM = pl.BlockSpec(memory_space=pltpu.VMEM)
HBM = pl.BlockSpec(memory_space=pltpu.HBM)
SMEM = pl.BlockSpec(memory_space=pltpu.SMEM)
MIB = 1024 * 1024


def in_hbm(value):
    return pltpu.with_memory_space_constraint(value, pltpu.HBM)


PIECES = 2
TEAM = 32
STEP = 16


def body(
    n_oct,
    n_cube,
    charges,
    panel_counts,
    positions,
    moment_map,
    translations,
    evaluation,
    near_boxes,
    group_sources,
    group_patterns,
    remote_sources,
    remote_patterns,
    remote_targets,
):
    boxes, panels = charges.shape
    width = moment_map.shape[1]
    patterns = translations.shape[0]
    operators = translations.reshape(patterns * width, width)
    counts = panel_counts.reshape(boxes // LANES, LANES)
    handed = (
        near_boxes.T,
        positions,
        remote_sources[0, 0].transpose(0, 2, 1),
        remote_patterns[0, 0].transpose(0, 2, 1),
        remote_targets[0, 0],
        evaluation,
    )
    strength, counts, multipole, *handed, evaluation = pl.pallas_call(
        functools.partial(front_kernel, extra=len(handed)),
        out_shape=(
            jax.ShapeDtypeStruct((boxes, panels), F32),
            jax.ShapeDtypeStruct(counts.shape, jnp.int32),
            jax.ShapeDtypeStruct((boxes, width), BF16),
            *[jax.ShapeDtypeStruct(v.shape, v.dtype) for v in handed],
        ),
        in_specs=[HBM] * (3 + len(handed)),
        out_specs=(VMEM,) * (3 + len(handed)),
        scratch_shapes=[pltpu.VMEM(v.shape, v.dtype) for v in (charges, counts, moment_map)]
        + [pltpu.SemaphoreType.DMA((3 + len(handed),))],
        compiler_params=pltpu.CompilerParams(vmem_limit_bytes=8 * MIB),
        cost_estimate=pl.CostEstimate(
            flops=10_000_000, bytes_accessed=300_000, transcendentals=0
        ),
        name="front",
    )(in_hbm(charges), in_hbm(counts), in_hbm(moment_map), *map(in_hbm, handed))

    me = lax.axis_index("cube")
    octant = lax.axis_index("oct")

    def over_cube(value, k):
        return lax.ppermute(value, "cube", [(i, i ^ k) for i in range(n_cube)])

    def over_oct(value, k):
        return lax.ppermute(value, "oct", [(i, i ^ k) for i in range(n_oct)])

    def after(value, *earlier):
        return lax.optimization_barrier((value, *earlier))[0]

    slots = remote_sources.shape[3]
    plan, *tables, sent = pl.pallas_call(
        plan_kernel,
        out_shape=(
            jax.ShapeDtypeStruct((8, boxes), jnp.int32),
            jax.ShapeDtypeStruct((2, boxes, panels), F32),
            jax.ShapeDtypeStruct((6, boxes, panels), F32),
            jax.ShapeDtypeStruct((boxes // 8, panels, LANES), BF16),
            jax.ShapeDtypeStruct((n_oct, 2 * slots + 16, width), BF16),
        ),
        in_specs=[VMEM] * (3 + len(handed)) + [HBM],
        out_specs=(VMEM,) * 5,
        scratch_shapes=[
            pltpu.VMEM((boxes, 9 * LANES), F32),
            pltpu.VMEM((n_oct * slots, patterns * width), BF16),
            pltpu.VMEM(operators.shape, BF16),
            pltpu.SemaphoreType.DMA,
        ],
        compiler_params=pltpu.CompilerParams(vmem_limit_bytes=16 * MIB),
        cost_estimate=pl.CostEstimate(
            flops=1_000_000_000, bytes_accessed=2_000_000, transcendentals=0
        ),
        name="plan",
    )(counts, strength, multipole, *handed, in_hbm(operators))

    teams = boxes // TEAM
    cut = teams * 3 // 4

    def near_piece(start, stop, tables):
        return pl.pallas_call(
            functools.partial(near_kernel, start=start, stop=stop),
            out_shape=jax.ShapeDtypeStruct((boxes, panels), F32),
            in_specs=[SMEM, VMEM, VMEM, VMEM],
            out_specs=VMEM,
            scratch_shapes=[pltpu.VMEM((boxes, 48, panels), BF16)],
            compiler_params=pltpu.CompilerParams(vmem_limit_bytes=12 * MIB),
            cost_estimate=pl.CostEstimate(
                flops=200_000_000, bytes_accessed=1_000_000, transcendentals=0
            ),
            name="near",
        )(plan, *tables)

    box = {k: lax.dynamic_index_in_dim(sent, octant ^ k, 0, keepdims=False) for k in range(n_oct)}

    def oct_step(bit):
        moving = [k for k in range(n_oct) if k & bit]
        load = jnp.concatenate([box[k] for k in moving], axis=0)
        return load, over_oct(load, bit)

    def unpack(bit, came):
        moving = [k for k in range(n_oct) if k & bit]
        rows = came.shape[0] // len(moving)
        for i, k in enumerate(moving):
            box[k] = came[i * rows : (i + 1) * rows]

    def cube_step(bit, mine):
        return jnp.concatenate([mine, over_cube(mine, bit)], axis=0)

    oct_bits = [1 << i for i in range(log2(n_oct))]
    cube_bits = [1 << i for i in range(1, log2(n_cube))]
    mine = cube_step(cube_bits[0], multipole)
    mine = after(mine, plan, sent)
    anchor = [mine]
    for bit in oct_bits[:-1]:
        load, came = oct_step(bit)
        unpack(bit, came)
        anchor.append(load)
    for bit in cube_bits[1:]:
        mine = cube_step(bit, mine)
    tables = lax.optimization_barrier((*tables, *anchor))[: len(tables)]
    first = near_piece(0, cut, tables)

    mine = after(mine, first)
    other = over_cube(mine, 1)
    for k in range(n_oct):
        box[k] = after(box[k], first) if k > 0 else box[k]
    load, came = oct_step(oct_bits[-1])
    tables = lax.optimization_barrier((*tables, mine, load))[: len(tables)]
    second = near_piece(cut, teams, tables)
    other, second, came = lax.optimization_barrier((other, second, came))
    unpack(oct_bits[-1], came)
    payloads = [box[k] for k in range(n_oct)]
    near = [first, second]

    klist = group_sources.shape[1]
    group = n_cube * boxes
    code = (group_sources ^ (me * boxes)) + group * group_patterns
    return pl.pallas_call(
        functools.partial(far_kernel, blocks=n_cube, fanin=klist, pieces=PIECES),
        out_shape=jax.ShapeDtypeStruct((boxes, panels), F32),
        in_specs=[VMEM] * (6 + PIECES + n_oct),
        out_specs=VMEM,
        scratch_shapes=[pltpu.VMEM((boxes, patterns * width), BF16)],
        compiler_params=pltpu.CompilerParams(vmem_limit_bytes=24 * MIB),
        cost_estimate=pl.CostEstimate(
            flops=3_000_000_000, bytes_accessed=2_000_000, transcendentals=0
        ),
        name="far",
    )(
        code.reshape(-1, LANES),
        counts,
        operators,
        evaluation,
        mine,
        other,
        *near,
        *payloads,
    )


def solution(mesh):
    n_oct = mesh.shape["oct"]
    n_cube = mesh.shape["cube"]

    def run(*arrays):
        return body(n_oct, n_cube, *arrays)

    return jax.shard_map(
        run,
        mesh=mesh,
        in_specs=(
            P(("oct", "cube"), None),
            P(("oct", "cube")),
            P(None, ("oct", "cube"), None),
            P(),
            P(),
            P(),
            P(("oct", "cube"), None),
            P(("oct", "cube"), None),
            P(("oct", "cube"), None),
            P("oct", "cube", None, None, None),
            P("oct", "cube", None, None, None),
            P("oct", "cube", None, None),
        ),
        out_specs=P(("oct", "cube"), None),
        check_vma=False,
    )
```
